32 devices in a mesh: mocks: 2 (over x), blk: 8 (over z, y), offs: 2 (over core).
Axes of the slice: x: 2, y: 2, z: 4, core: 2. Of those that a mesh axis runs over, the one named last changes fastest.
Arguments:
- position: float32 [3, 16384], P(None, ('mocks', 'blk')), parts along dimension 1, may hold values from -200 to 200, as said below
- noise_var: float32 [16384], P(('mocks', 'blk')), parts along dimension 0, may hold values from 2 to 80
- rhs: float32 [8, 16384], P(None, ('mocks', 'blk')), parts along dimension 1, may hold values from -6 to 6
- block_count: int32 [16], P(('mocks', 'blk')), parts along dimension 0, may hold values from 1 to 1024, 5120 in all
Outputs:
- solution: float32 [8, 16384], P(None, ('mocks', 'blk')), parts along dimension 1
- residual: float32 [8, 16384], P(None, ('mocks', 'blk')), parts along dimension 1
The draws below stay inside these ranges and needn't reach their ends.
There are 2 independent parts, one for each index of `mocks`. The reference program is written for one: setup_inputs(seed, part) draws one part's arguments, and reference() takes and returns one part's arrays. A program takes and returns all parts, laid end to end along the dimension named above; each array names one. Nothing has to cross between parts.
Inputs may be any that keep to these rules, and one draw needn't show every extreme that they name: `position`: every galaxy lies between 20 and 200 from the observer. Block b holds its galaxies in its first block_count[b] slots; the counts sum to 5120, and some block is full.
All inputs are finite; a program needn't handle non-finite values.
Results may differ from the reference program's by a relative error of at most 0.0001.
Values sent between devices are 32-bit elements; how exact they have to be, the bound alone decides.
No kernel may reach another device: no remote copies, remote signals or barrier semaphores. Data moves between devices by JAX's collectives and lax.ppermute only.
A program may use at most 64 MiB of HBM per device.

```python
import math
import jax
import jax.numpy as jnp
import numpy as np
from jax import lax

SLOT_DEV = 1024
RHS = 8
ITERS = 1
SLOTS = 8192
GALAXIES = 5120
N_BLK = 8


def draw_position(key, part):
    first_key, second_key = jax.random.split(jax.random.fold_in(key, 11))
    heading = jax.random.normal(first_key, (3, SLOTS), jnp.float32)
    length = jnp.sqrt(jnp.sum(heading * heading, axis=0))
    unit = heading / jnp.maximum(length, 0.001)
    distance = jax.random.uniform(second_key, (SLOTS,), jnp.float32, 20.0, 200.0)
    return (unit * distance[None, :]).astype(jnp.float32)


def shard_levels(rng, extent, shards, smallest, top_value):
    def one(dim, parts):
        steps = jax.random.uniform(jax.random.fold_in(jax.random.fold_in(rng, 6), dim), (parts,), jnp.float32, smallest / len(shards), top_value / len(shards))
        return jnp.repeat(jnp.exp(steps), extent[dim] // parts).reshape((-1,) + (1,) * (len(extent) - dim - 1))

    gain = one(*shards[0])
    for cut in shards[1:]:
        gain = gain * one(*cut)
    return gain


def split_up(count, total, most, lean):
    portions = [(1 << 20) // math.isqrt(grade ** lean) + 1 for grade in range(2, count + 1)]
    surplus, holding = total - most - (count - 1), [1] * (count - 1)
    while surplus > 0:
        free = [i for i in range(count - 1) if holding[i] < most]
        whole, budget = sum([portions[i] for i in free]), surplus
        for i in free:
            more = min(most - holding[i], max(1, budget * portions[i] // whole), surplus)
            holding[i] = holding[i] + more
            surplus = surplus - more
    return np.array([most] + holding)


def ragged_sizes(own_key, amount, total, reach, lean):
    if amount == 2:
        one = jax.random.randint(own_key, (), max(1, total - reach), min(reach, total - 1) + 1)
        return jnp.stack([one, total - one])
    sizes = jnp.asarray(split_up(amount, total, reach, lean), jnp.int32)
    twos = (amount - 1) // 2
    source_of, receiver = sizes[1:1 + 2 * twos:2], sizes[2:2 + 2 * twos:2]
    room = jnp.minimum(source_of - 1, reach - receiver)
    moved = jax.random.randint(jax.random.fold_in(own_key, 1), (twos,), 0, 1 << 20) % (room + 1)
    sizes = sizes.at[1:1 + 2 * twos:2].set(source_of - moved).at[2:2 + 2 * twos:2].set(receiver + moved)
    return sizes[jax.random.permutation(jax.random.fold_in(own_key, 2), amount)]


def bell_draw(rng, dims, scale, reach, shards=(), kind=jnp.bfloat16):
    entries = scale * jax.random.normal(rng, dims, jnp.float32)
    if shards:
        entries = entries * shard_levels(rng, dims, shards, -0.22, 0.18)
    return jnp.clip(entries, -reach, reach).astype(kind)


def setup_inputs(seed: int = 0, part: int = 0) -> dict:
    arg_keys = jax.random.split(jax.random.key(seed), 5)
    part_splits = jax.random.split(jax.random.fold_in(arg_keys[4], part), 5)
    position = draw_position(jax.random.fold_in(jax.random.fold_in(arg_keys[4], part), 71), part)
    noise_var = jnp.clip(jnp.exp(math.log(80.0) - 3.6888795 * jax.random.uniform(part_splits[1], (SLOTS,), jnp.float32) ** shard_levels(part_splits[1], (SLOTS,), ((0, 8),), -0.2, 0.2)), 2.0, 80.0)
    rhs = bell_draw(part_splits[2], (RHS, SLOTS), 1.0, 6.0, ((1, 8),), jnp.float32)
    block_count = ragged_sizes(part_splits[3], N_BLK, GALAXIES, SLOT_DEV, 2).astype(jnp.int32)
    return dict(position=position, noise_var=noise_var, rhs=rhs, block_count=block_count)


near_weight = 0.6
near_length = 40.0
far_weight = 0.4
far_length = 120.0

def covariance(rows_pos, rows_live, cols_pos, cols_live):
    highest = lax.Precision.HIGHEST
    sq_rows = lax.optimization_barrier(jnp.sum(rows_pos * rows_pos, axis=0))
    sq_cols = lax.optimization_barrier(jnp.sum(cols_pos * cols_pos, axis=0))
    cross = jnp.einsum('ka,kb->ab', rows_pos, cols_pos, precision=highest)
    dist2 = jnp.maximum(sq_rows[:, None] + sq_cols[None, :] - 2.0 * cross, 0.0)
    cosine = cross / (jnp.sqrt(sq_rows)[:, None] * jnp.sqrt(sq_cols)[None, :])
    kernel = near_weight / (1.0 + dist2 / (near_length * near_length)) + far_weight / (1.0 + dist2 / (far_length * far_length))
    return kernel * cosine * rows_live[:, None] * cols_live[None, :]

def operate(position, live, noise_var, direction):
    highest = lax.Precision.HIGHEST

    def one_block(index):
        first = index * SLOT_DEV
        rows_pos = lax.dynamic_slice_in_dim(position, first, SLOT_DEV, 1)
        rows_live = lax.dynamic_slice_in_dim(live, first, SLOT_DEV, 0)
        cover = covariance(rows_pos, rows_live, position, live)
        return lax.dot_general(direction, cover, (((1,), (1,)), ((), ())), precision=highest)
    pieces = lax.map(one_block, jnp.arange(N_BLK, dtype=jnp.int32))
    image = jnp.transpose(pieces, (1, 0, 2)).reshape(RHS, SLOTS)
    return image + noise_var * live * direction

def reference(position, noise_var, rhs, block_count):
    highest = lax.Precision.HIGHEST
    slot = jnp.arange(SLOTS, dtype=jnp.int32)
    live = (slot % SLOT_DEV < block_count[slot // SLOT_DEV]).astype(jnp.float32)
    residual = rhs * live
    direction = residual
    solution = jnp.zeros_like(residual)
    norm_now = jnp.dot(residual, residual.T, precision=highest)
    for turn in range(ITERS):
        image = operate(position, live, noise_var, direction)
        curv = jnp.dot(direction, image.T, precision=highest)
        alpha = jax.scipy.linalg.cho_solve((jnp.linalg.cholesky(curv), True), norm_now)
        solution = solution + jnp.dot(alpha.T, direction, precision=highest)
        residual = residual - jnp.dot(alpha.T, image, precision=highest)
        if turn + 1 < ITERS:
            norm_next = jnp.dot(residual, residual.T, precision=highest)
            beta = jax.scipy.linalg.cho_solve((jnp.linalg.cholesky(norm_now), True), norm_next)
            direction = residual + jnp.dot(beta.T, direction, precision=highest)
            norm_now = norm_next
    return (solution, residual)
```

```python
import functools

import jax
import jax.numpy as jnp
from jax import lax
from jax.experimental import pallas as pl
from jax.experimental.pallas import tpu as pltpu
from jax.sharding import PartitionSpec as P

near_weight = 0.6
near_length = 40.0
far_weight = 0.4
far_length = 120.0
near_sq = near_length * near_length
far_sq = far_length * far_length
gap = far_sq - near_sq
scale = near_weight * near_sq + far_weight * far_sq
lift = near_weight * near_sq * gap / scale

LANES = 128
STEP = 512
f32 = jnp.float32
bf16 = jnp.bfloat16
VMEM = pl.BlockSpec(memory_space=pltpu.VMEM)
HBM = pl.BlockSpec(memory_space=pl.ANY)
LIMIT = 24 * 2**20
highest = lax.Precision.HIGHEST


def split3(x):
    top = x.astype(bf16).astype(f32)
    rest = x - top
    mid = rest.astype(bf16).astype(f32)
    return top, mid, rest - mid


def stack(rows, width):
    rows = rows + [jnp.zeros((32 - len(rows), width), f32)]
    return jnp.concatenate(rows, axis=0).astype(bf16)


def row_side(pos):
    width = pos.shape[1]
    rows = []
    for k in range(3):
        top, mid, low = split3(pos[k : k + 1])
        rows += [top, mid, top, low, top, mid]
    one = jnp.ones((1, width), f32)
    square = jnp.sum(pos * pos, axis=0, keepdims=True) + near_sq
    return stack(rows + [one] * 3 + list(split3(square)), width)


def column_side(pos):
    width = pos.shape[1]
    rows = []
    for k in range(3):
        top, mid, low = split3(-2.0 * pos[k : k + 1])
        rows += [top, top, mid, top, low, mid]
    one = jnp.ones((1, width), f32)
    square = jnp.sum(pos * pos, axis=0, keepdims=True)
    return stack(rows + list(split3(square)) + [one] * 3, width)


def unit_of(pos):
    square = jnp.sum(pos * pos, axis=0, keepdims=True)
    return pos * jnp.where(square > 0.0, lax.rsqrt(square), 0.0)


def pack_kernel(pos_hbm, rhs_hbm, count_hbm, out, pos, rhs, count, sems):
    copies = [
        pltpu.make_async_copy(pos_hbm, pos, sems.at[0]),
        pltpu.make_async_copy(rhs_hbm, rhs, sems.at[1]),
        pltpu.make_async_copy(count_hbm, count, sems.at[2]),
    ]
    for copy in copies:
        copy.start()
    for copy in copies:
        copy.wait()
    width, slots = rhs.shape
    tiles = slots // LANES // 2
    side = (lax.axis_index("offs") + lax.axis_index("blk")) % 2
    odd = side == 1
    n = count[0]
    lane = lax.broadcasted_iota(jnp.int32, (1, LANES), 1)
    held = jnp.clip((n + LANES - 1 - side * LANES + LANES) // (2 * LANES), 0, tiles)
    held = jnp.full((1, LANES), held.astype(f32))
    for t in range(tiles):
        even_at = slice(2 * t * LANES, (2 * t + 1) * LANES)
        odd_at = slice((2 * t + 1) * LANES, (2 * t + 2) * LANES)
        first = (2 * t + side) * LANES
        value = jnp.where(odd, rhs[:, odd_at], rhs[:, even_at])
        out[:, t * LANES : (t + 1) * LANES] = jnp.where(first + lane < n, value, 0.0)
        place = jnp.where(odd, pos[:, odd_at], pos[:, even_at])
        at = (tiles + t // 2) * LANES
        row = (t % 2) * 4
        out[row : row + 4, at : at + LANES] = jnp.concatenate([place, held], axis=0)


def pair_kernel(first, last, blocks, tiles, *refs):
    refs = list(refs)
    packet = refs.pop(0)
    if first:
        pos_hbm = refs.pop(0)
    else:
        rows_in, acc_in = refs.pop(0), refs.pop(0)
    if last:
        pos_hbm, noise_hbm, rhs_hbm, count_hbm = (refs.pop(0) for _ in range(4))
        out = refs.pop(0)
    else:
        if first:
            rows_out = refs.pop(0)
        acc_out = refs.pop(0)
    cols, weights = refs.pop(0), refs.pop(0)
    if first or last:
        sems = refs.pop(0)
        pos = refs.pop(0)
        copies = [pltpu.make_async_copy(pos_hbm, pos, sems.at[0])]
    if last:
        noise, rhs, count = (refs.pop(0) for _ in range(3))
        copies += [
            pltpu.make_async_copy(noise_hbm, noise, sems.at[1]),
            pltpu.make_async_copy(rhs_hbm, rhs, sems.at[2]),
            pltpu.make_async_copy(count_hbm, count, sems.at[3]),
        ]
    if first or last:
        for copy in copies:
            copy.start()

    width = packet.shape[0]
    half = tiles * LANES
    stride = half + half // 2
    filled = jnp.int32(0)
    for b in range(blocks):
        base = b * stride
        v = packet[:, base : base + half]
        parts = []
        for t in range(tiles):
            at = base + half + (t // 2) * LANES
            row = (t % 2) * 4
            parts.append(packet[row : row + 3, at : at + LANES])
        place = jnp.concatenate(parts, axis=1)
        unit = unit_of(place)
        product = jnp.concatenate([unit[k : k + 1] * v for k in range(3)], axis=0)
        top = product.astype(bf16)
        low = (product - top.astype(f32)).astype(bf16)
        at = pl.ds(pl.multiple_of(filled, LANES), half)
        cols[:, at] = column_side(place)
        weights[:, at] = jnp.concatenate([top, low], axis=0)
        held = jnp.max(packet[3:4, base + half : base + half + LANES])
        filled = filled + held.astype(jnp.int32) * LANES
    at = pl.ds(pl.multiple_of(filled, LANES), STEP)
    cols[:, at] = jnp.zeros((cols.shape[0], STEP), bf16)
    weights[:, at] = jnp.zeros((weights.shape[0], STEP), bf16)

    if first:
        for copy in copies:
            copy.wait()
        rows = row_side(pos[...])
        rows_out[...] = rows
        slots = rows.shape[1]
        total = jnp.zeros((6 * width, slots), f32)
    else:
        rows = rows_in[...]
        slots = rows.shape[1]
        total = acc_in[...]

    def step(i, total):
        at = pl.ds(pl.multiple_of(i * STEP, STEP), STEP)
        u = lax.dot_general(
            cols[:, at], rows, (((0,), (0,)), ((), ())), preferred_element_type=f32
        )
        u = jnp.maximum(u, near_sq)
        value = (u + lift) * pl.reciprocal(u * (u + gap), approx=True)
        top = value.astype(bf16)
        low = (value - top.astype(f32)).astype(bf16)
        w = weights[:, at]
        total = total + jnp.dot(w, top, preferred_element_type=f32)
        return total + jnp.dot(w, low, preferred_element_type=f32)

    total = lax.fori_loop(0, (filled + STEP - 1) // STEP, step, total)
    if not last:
        acc_out[...] = total
        return
    for copy in copies:
        copy.wait()
    total = total[: 3 * width] + total[3 * width :]
    lane = lax.broadcasted_iota(jnp.int32, (1, slots), 1)
    live = (lane < count[0]).astype(f32)
    unit = unit_of(pos[...]) * (live * scale)
    image = sum(unit[k : k + 1] * total[k * width : (k + 1) * width] for k in range(3))
    direction = rhs[...] * live
    mine = (lax.axis_index("offs") == 0).astype(f32)
    noise_row = noise[...].reshape(1, slots)
    image = image + (mine * noise_row * live) * direction
    out[:, :slots] = image
    dims = (((1,), (1,)), ((), ()))
    both = jnp.concatenate([image, direction * mine], axis=0)
    small = lax.dot_general(
        direction, both, dims, precision=highest, preferred_element_type=f32
    )
    pad = jnp.zeros((width, LANES - 2 * width), f32)
    out[:, slots:] = jnp.concatenate([small, pad], axis=1)


def tail_kernel(small, mine, other, rhs_hbm, count_hbm, sol, res, rhs, count, sems):
    copies = [
        pltpu.make_async_copy(rhs_hbm, rhs, sems.at[0]),
        pltpu.make_async_copy(count_hbm, count, sems.at[1]),
    ]
    for copy in copies:
        copy.start()
    a = small[...]
    width = a.shape[0]
    row = lax.broadcasted_iota(jnp.int32, a.shape, 0)
    for k in range(width):
        pivot = a[k : k + 1] / a[k : k + 1, k : k + 1]
        a = jnp.where(row == k, pivot, a - a[:, k : k + 1] * pivot)
    alpha = a[:, width : 2 * width]
    for copy in copies:
        copy.wait()
    slots = rhs.shape[1]
    lane = lax.broadcasted_iota(jnp.int32, (1, slots), 1)
    direction = rhs[...] * (lane < count[0]).astype(f32)
    image = mine[:, :slots] + other[:, :slots]
    dims = (((0,), (0,)), ((), ()))
    sol[...] = lax.dot_general(
        alpha, direction, dims, precision=highest, preferred_element_type=f32
    )
    res[...] = direction - lax.dot_general(
        alpha, image, dims, precision=highest, preferred_element_type=f32
    )


def call(kernel, out_shape, in_specs, out_specs, scratch, name, flops=0):
    return pl.pallas_call(
        kernel,
        out_shape=out_shape,
        in_specs=in_specs,
        out_specs=out_specs,
        scratch_shapes=scratch,
        compiler_params=pltpu.CompilerParams(vmem_limit_bytes=LIMIT),
        cost_estimate=pl.CostEstimate(
            flops=flops, bytes_accessed=1 << 17, transcendentals=0
        ),
        name=name,
    )


def exchanged(block, axis, distance):
    n = lax.axis_size(axis)
    return lax.ppermute(block, axis, [(i ^ distance, i) for i in range(n)])


def body(position, noise_var, rhs, block_count):
    width, slots = rhs.shape
    blocks = lax.axis_size("blk")
    tiles = slots // LANES // 2
    half = tiles * LANES
    shape = jax.ShapeDtypeStruct
    pos_buf = pltpu.VMEM(position.shape, f32)
    rhs_buf = pltpu.VMEM(rhs.shape, f32)
    noise_buf = pltpu.VMEM(noise_var.shape, f32)
    count_buf = pltpu.SMEM((1,), jnp.int32)

    packet = call(
        pack_kernel,
        shape((width, half + half // 2), f32),
        [HBM, HBM, HBM],
        VMEM,
        [pos_buf, rhs_buf, count_buf, pltpu.SemaphoreType.DMA((3,))],
        "pack",
    )(position, rhs, block_count)

    acc_shape = shape((6 * width, slots), f32)
    rows_shape = shape((32, slots), bf16)

    def pairs(fresh, count, first=False, last=False, rows=None, acc=None):
        scratch = [
            pltpu.VMEM((32, count * half + STEP), bf16),
            pltpu.VMEM((6 * width, count * half + STEP), bf16),
        ]
        if first:
            args, specs = [fresh, position], [VMEM, HBM]
            outs, out_specs = (rows_shape, acc_shape), (VMEM, VMEM)
        else:
            args, specs = [fresh, rows, acc], [VMEM] * 3
            outs, out_specs = acc_shape, VMEM
        if first or last:
            scratch += [pltpu.SemaphoreType.DMA((4,)), pos_buf]
        if last:
            args += [position, noise_var, rhs, block_count]
            specs += [HBM] * 4
            outs = shape((width, slots + LANES), f32)
            scratch += [noise_buf, rhs_buf, count_buf]
        kernel = functools.partial(pair_kernel, first, last, count, tiles)
        flops = 2 * slots * count * half * 64
        name = f"pairs_{count}"
        return call(kernel, outs, specs, out_specs, scratch, name, flops)(*args)

    known, fresh, count = packet, packet, 1
    rows = acc = None
    distance = blocks // 2
    while distance:
        arrived = exchanged(known, "blk", distance)
        if rows is None:
            rows, acc = pairs(fresh, count, first=True)
        else:
            acc = pairs(fresh, count, rows=rows, acc=acc)
            count *= 2
        if distance > 1:
            known = jnp.concatenate([known, arrived], axis=1)
        fresh = arrived
        distance //= 2
    mine = pairs(fresh, count, last=True, rows=rows, acc=acc)
    other = exchanged(mine, "offs", 1)
    small = mine[:, slots:] + other[:, slots:]
    distance = blocks // 2
    while distance:
        small = small + exchanged(small, "blk", distance)
        distance //= 2

    return tuple(
        call(
            tail_kernel,
            (shape(rhs.shape, f32),) * 2,
            [VMEM, VMEM, VMEM, HBM, HBM],
            (VMEM, VMEM),
            [rhs_buf, count_buf, pltpu.SemaphoreType.DMA((2,))],
            "tail",
        )(small, mine, other, rhs, block_count)
    )


def solution(mesh):
    return jax.shard_map(
        body,
        mesh=mesh,
        in_specs=(
            P(None, ("mocks", "blk")),
            P(("mocks", "blk")),
            P(None, ("mocks", "blk")),
            P(("mocks", "blk")),
        ),
        out_specs=(P(None, ("mocks", "blk")), P(None, ("mocks", "blk"))),
        check_vma=False,
    )
```

```python
import functools

import jax
import jax.numpy as jnp
from jax import lax
from jax.experimental import pallas as pl
from jax.experimental.pallas import tpu as pltpu
from jax.sharding import PartitionSpec as P

near_weight = 0.6
near_length = 40.0
far_weight = 0.4
far_length = 120.0
near_sq = near_length * near_length
far_sq = far_length * far_length
gap = far_sq - near_sq
scale = near_weight * near_sq + far_weight * far_sq
lift = near_weight * near_sq * gap / scale

LANES = 128
STEP = 512
f32 = jnp.float32
bf16 = jnp.bfloat16
VMEM = pl.BlockSpec(memory_space=pltpu.VMEM)
HBM = pl.BlockSpec(memory_space=pltpu.HBM)
LIMIT = 24 * 2**20
highest = lax.Precision.HIGHEST


def split3(x):
    top = x.astype(bf16).astype(f32)
    rest = x - top
    mid = rest.astype(bf16).astype(f32)
    return top, mid, rest - mid


def stack(rows, width):
    rows = rows + [jnp.zeros((32 - len(rows), width), f32)]
    return jnp.concatenate(rows, axis=0).astype(bf16)


def row_side(pos):
    width = pos.shape[1]
    rows = []
    for k in range(3):
        top, mid, low = split3(pos[k : k + 1])
        rows += [top, mid, top, low, top, mid]
    one = jnp.ones((1, width), f32)
    square = jnp.sum(pos * pos, axis=0, keepdims=True) + near_sq
    return stack(rows + [one] * 3 + list(split3(square)), width)


def column_side(pos):
    width = pos.shape[1]
    rows = []
    for k in range(3):
        top, mid, low = split3(-2.0 * pos[k : k + 1])
        rows += [top, top, mid, top, low, mid]
    one = jnp.ones((1, width), f32)
    square = jnp.sum(pos * pos, axis=0, keepdims=True)
    return stack(rows + list(split3(square)) + [one] * 3, width)


def unit_of(pos):
    square = jnp.sum(pos * pos, axis=0, keepdims=True)
    return pos * jnp.where(square > 0.0, lax.rsqrt(square), 0.0)


def pack_kernel(pos_hbm, rhs_hbm, count_hbm, out, pos, rhs, count, sems):
    copies = [
        pltpu.make_async_copy(pos_hbm, pos, sems.at[0]),
        pltpu.make_async_copy(rhs_hbm, rhs, sems.at[1]),
        pltpu.make_async_copy(count_hbm, count, sems.at[2]),
    ]
    for copy in copies:
        copy.start()
    for copy in copies:
        copy.wait()
    width, slots = rhs.shape
    tiles = slots // LANES // 2
    side = (lax.axis_index("offs") + lax.axis_index("blk")) % 2
    odd = side == 1
    n = count[0]
    lane = lax.broadcasted_iota(jnp.int32, (1, LANES), 1)
    held = jnp.clip((n + LANES - 1 - side * LANES + LANES) // (2 * LANES), 0, tiles)
    held = jnp.full((1, LANES), held.astype(f32))
    for t in range(tiles):
        even_at = slice(2 * t * LANES, (2 * t + 1) * LANES)
        odd_at = slice((2 * t + 1) * LANES, (2 * t + 2) * LANES)
        first = (2 * t + side) * LANES
        value = jnp.where(odd, rhs[:, odd_at], rhs[:, even_at])
        out[:, t * LANES : (t + 1) * LANES] = jnp.where(first + lane < n, value, 0.0)
        place = jnp.where(odd, pos[:, odd_at], pos[:, even_at])
        at = (tiles + t // 2) * LANES
        row = (t % 2) * 4
        out[row : row + 4, at : at + LANES] = jnp.concatenate([place, held], axis=0)


def pair_kernel(first, last, start, blocks, tiles, *refs):
    refs = list(refs)
    packet = refs.pop(0)
    if first or last:
        pos_hbm = refs.pop(0)
    if not first:
        rows_in, acc_in = refs.pop(0), refs.pop(0)
    if last:
        noise_hbm, rhs_hbm, count_hbm, out = (refs.pop(0) for _ in range(4))
        acc = refs.pop(0)
    else:
        known_out, acc = refs.pop(0), refs.pop(0)
        rows_ref = refs.pop(0) if first else rows_in
    if last:
        rows_ref = rows_in
    cols, weights = refs.pop(0), refs.pop(0)
    copies = []
    if first or last:
        sems, pos = refs.pop(0), refs.pop(0)
        copies.append(pltpu.make_async_copy(pos_hbm, pos, sems.at[0]))
    if last:
        noise, rhs, count = (refs.pop(0) for _ in range(3))
        copies += [
            pltpu.make_async_copy(noise_hbm, noise, sems.at[1]),
            pltpu.make_async_copy(rhs_hbm, rhs, sems.at[2]),
            pltpu.make_async_copy(count_hbm, count, sems.at[3]),
        ]
    for copy in copies:
        copy.start()
    if not last:
        known_out[...] = packet[...]

    width = packet.shape[0]
    half = tiles * LANES
    stride = half + half // 2
    filled = jnp.int32(0)
    for b in range(start, start + blocks):
        base = b * stride
        v = packet[:, base : base + half]
        parts = []
        for t in range(tiles):
            at = base + half + (t // 2) * LANES
            row = (t % 2) * 4
            parts.append(packet[row : row + 3, at : at + LANES])
        place = jnp.concatenate(parts, axis=1)
        unit = unit_of(place)
        product = jnp.concatenate([unit[k : k + 1] * v for k in range(3)], axis=0)
        top = product.astype(bf16)
        low = (product - top.astype(f32)).astype(bf16)
        at = pl.ds(pl.multiple_of(filled, LANES), half)
        cols[:, at] = column_side(place)
        weights[:, at] = jnp.concatenate([top, low], axis=0)
        held = jnp.max(packet[3:4, base + half : base + half + LANES])
        filled = filled + held.astype(jnp.int32) * LANES
    at = pl.ds(pl.multiple_of(filled, LANES), STEP)
    cols[:, at] = jnp.zeros((cols.shape[0], STEP), bf16)
    weights[:, at] = jnp.zeros((weights.shape[0], STEP), bf16)

    slots = acc.shape[1]
    if first:
        copies[0].wait()
        rows_ref[...] = row_side(pos[...])
        acc[...] = jnp.zeros(acc.shape, f32)
    else:
        acc[...] = acc_in[...]

    def step(begin, size):
        at = pl.ds(pl.multiple_of(begin, LANES), size)
        u = lax.dot_general(
            cols[:, at],
            rows_ref[...],
            (((0,), (0,)), ((), ())),
            preferred_element_type=f32,
        )
        u = jnp.maximum(u, near_sq)
        value = (u + lift) * pl.reciprocal(u * (u + gap), approx=True)
        top = value.astype(bf16)
        low = (value - top.astype(f32)).astype(bf16)
        w = weights[:, at]
        acc[...] += jnp.dot(w, top, preferred_element_type=f32) + jnp.dot(
            w, low, preferred_element_type=f32
        )

    steps = (filled + STEP // 2 - 1) // STEP

    @pl.loop(0, steps)
    def _(i):
        step(i * STEP, STEP)

    @pl.when(filled > steps * STEP)
    def _():
        step(steps * STEP, STEP // 2)

    if not last:
        return
    for copy in copies:
        copy.wait()
    total = acc[: 3 * width] + acc[3 * width :]
    lane = lax.broadcasted_iota(jnp.int32, (1, slots), 1)
    live = (lane < count[0]).astype(f32)
    unit = unit_of(pos[...]) * (live * scale)
    image = sum(unit[k : k + 1] * total[k * width : (k + 1) * width] for k in range(3))
    direction = rhs[...] * live
    mine = (lax.axis_index("offs") == 0).astype(f32)
    noise_row = noise[...].reshape(1, slots)
    image = image + (mine * noise_row * live) * direction
    out[:, :slots] = image
    dims = (((1,), (1,)), ((), ()))
    both = jnp.concatenate([image, direction * mine], axis=0)
    small = lax.dot_general(
        direction, both, dims, precision=highest, preferred_element_type=f32
    )
    pad = jnp.zeros((width, LANES - 2 * width), f32)
    out[:, slots:] = jnp.concatenate([small, pad], axis=1)


def tail_kernel(small, mine, other, rhs_hbm, count_hbm, sol, res, rhs, count, sems):
    copies = [
        pltpu.make_async_copy(rhs_hbm, rhs, sems.at[0]),
        pltpu.make_async_copy(count_hbm, count, sems.at[1]),
    ]
    for copy in copies:
        copy.start()
    a = small[...]
    width = a.shape[0]
    row = lax.broadcasted_iota(jnp.int32, a.shape, 0)
    for k in range(width):
        pivot = a[k : k + 1] / a[k : k + 1, k : k + 1]
        a = jnp.where(row == k, pivot, a - a[:, k : k + 1] * pivot)
    alpha = a[:, width : 2 * width]
    for copy in copies:
        copy.wait()
    slots = rhs.shape[1]
    lane = lax.broadcasted_iota(jnp.int32, (1, slots), 1)
    direction = rhs[...] * (lane < count[0]).astype(f32)
    image = mine[:, :slots] + other[:, :slots]
    dims = (((0,), (0,)), ((), ()))
    sol[...] = lax.dot_general(
        alpha, direction, dims, precision=highest, preferred_element_type=f32
    )
    res[...] = direction - lax.dot_general(
        alpha, image, dims, precision=highest, preferred_element_type=f32
    )


def call(kernel, out_shape, in_specs, out_specs, scratch, name, flops=0):
    return pl.pallas_call(
        kernel,
        out_shape=out_shape,
        in_specs=in_specs,
        out_specs=out_specs,
        scratch_shapes=scratch,
        compiler_params=pltpu.CompilerParams(vmem_limit_bytes=LIMIT),
        cost_estimate=pl.CostEstimate(
            flops=flops, bytes_accessed=1 << 17, transcendentals=0
        ),
        name=name,
    )


def exchanged(block, distance):
    blocks, sides = lax.axis_size("blk"), lax.axis_size("offs")
    route = [
        ((b ^ distance) * sides + sides - 1 - c, b * sides + c)
        for b in range(blocks)
        for c in range(sides)
    ]
    return lax.ppermute(block, ("blk", "offs"), route)


def body(position, noise_var, rhs, block_count):
    width, slots = rhs.shape
    blocks = lax.axis_size("blk")
    tiles = slots // LANES // 2
    half = tiles * LANES
    shape = jax.ShapeDtypeStruct
    pos_buf = pltpu.VMEM(position.shape, f32)
    rhs_buf = pltpu.VMEM(rhs.shape, f32)
    noise_buf = pltpu.VMEM(noise_var.shape, f32)
    count_buf = pltpu.SMEM((1,), jnp.int32)

    packet = call(
        pack_kernel,
        shape((width, half + half // 2), f32),
        [HBM, HBM, HBM],
        VMEM,
        [pos_buf, rhs_buf, count_buf, pltpu.SemaphoreType.DMA((3,))],
        "pack",
    )(position, rhs, block_count)

    acc_shape = shape((6 * width, slots), f32)
    rows_shape = shape((32, slots), bf16)

    def pairs(known, start, count, last, rows=None, acc=None):
        first = rows is None
        args, specs = [known], [VMEM]
        if first or last:
            args.append(position)
            specs.append(HBM)
        if not first:
            args += [rows, acc]
            specs += [VMEM] * 2
        scratch = [
            pltpu.VMEM((32, count * half + STEP), bf16),
            pltpu.VMEM((6 * width, count * half + STEP), bf16),
        ]
        if first or last:
            scratch += [pltpu.SemaphoreType.DMA((4,)), pos_buf]
        if last:
            args += [noise_var, rhs, block_count]
            specs += [HBM] * 3
            outs = (shape((width, slots + LANES), f32),)
            scratch = [pltpu.VMEM(acc_shape.shape, f32)] + scratch
            scratch += [noise_buf, rhs_buf, count_buf]
        else:
            outs = (shape(known.shape, f32), acc_shape)
            if first:
                outs += (rows_shape,)
        kernel = functools.partial(pair_kernel, first, last, start, count, tiles)
        flops = 2 * slots * count * half * 64
        specs_out = (VMEM,) * len(outs)
        return call(kernel, outs, specs, specs_out, scratch, f"pairs_{start}", flops)(*args)

    known, start, count = packet, 0, 1
    rows = acc = None
    distance = blocks // 2
    while distance:
        arrived = exchanged(known, distance)
        if rows is None:
            known, acc, rows = pairs(known, start, count, False)
        else:
            known, acc = pairs(known, start, count, False, rows, acc)
        start += count
        count = start
        known = jnp.concatenate([known, arrived], axis=1)
        distance //= 2
    (mine,) = pairs(arrived, 0, count, True, rows, acc)
    other = exchanged(mine, 0)
    small = mine[:, slots:] + other[:, slots:]
    distance = blocks // 2
    while distance:
        small = small + exchanged(small, distance)
        distance //= 2

    return tuple(
        call(
            tail_kernel,
            (shape(rhs.shape, f32),) * 2,
            [VMEM, VMEM, VMEM, HBM, HBM],
            (VMEM, VMEM),
            [rhs_buf, count_buf, pltpu.SemaphoreType.DMA((2,))],
            "tail",
        )(small, mine, other, rhs, block_count)
    )


def solution(mesh):
    return jax.shard_map(
        body,
        mesh=mesh,
        in_specs=(
            P(None, ("mocks", "blk")),
            P(("mocks", "blk")),
            P(None, ("mocks", "blk")),
            P(("mocks", "blk")),
        ),
        out_specs=(P(None, ("mocks", "blk")), P(None, ("mocks", "blk"))),
        check_vma=False,
    )
```

```python
import functools

import jax
import jax.numpy as jnp
from jax import lax
from jax.experimental import pallas as pl
from jax.experimental.pallas import tpu as pltpu
from jax.sharding import PartitionSpec as P

near_weight = 0.6
near_length = 40.0
far_weight = 0.4
far_length = 120.0
near_sq = near_length * near_length
far_sq = far_length * far_length
gap = far_sq - near_sq
scale = near_weight * near_sq + far_weight * far_sq
lift = near_weight * near_sq * gap / scale

LANES = 128
STEP = 512
f32 = jnp.float32
bf16 = jnp.bfloat16
VMEM = pl.BlockSpec(memory_space=pltpu.VMEM)
HBM = pl.BlockSpec(memory_space=pltpu.HBM)
LIMIT = 24 * 2**20
highest = lax.Precision.HIGHEST


def split3(x):
    top = x.astype(bf16).astype(f32)
    rest = x - top
    mid = rest.astype(bf16).astype(f32)
    return top, mid, rest - mid


def row_side(pos):
    width = pos.shape[1]
    one, none = jnp.ones((1, width), f32), jnp.zeros((1, width), f32)
    top, mid, low = split3(pos)
    square = split3(jnp.sum(pos * pos, axis=0, keepdims=True) + near_sq)
    a = jnp.concatenate([top, one, mid, none], axis=0)
    b = jnp.concatenate([top, one, low, none], axis=0)
    c = jnp.concatenate([*square, *[none] * 5], axis=0)
    return jnp.concatenate([a, b, a, c], axis=0).astype(bf16)


def column_sides(group):
    row = lax.broadcasted_iota(jnp.int32, group.shape, 0)
    fourth = row % 4 == 3
    upper = row < 4
    square = group * group
    square = sum(pltpu.roll(square, k, 0) for k in (1, 2, 3))
    scaled = jnp.where(fourth, square, -2.0 * group)
    ahead = split3(scaled)
    swapped = [pltpu.roll(x, 4, 0) for x in ahead]
    tail = jnp.where(upper, 1.0, 0.0)
    sides = []
    for (t, m, w), (tt, mm, _) in ((ahead, swapped), (swapped, ahead)):
        pairs = [(t, tt), (m, tt), (w, mm)]
        rows = [jnp.where(upper, x, y) for x, y in pairs] + [tail]
        sides.append(jnp.concatenate(rows, axis=0).astype(bf16))
    inverse = jnp.where(square > 0.0, lax.rsqrt(square), 0.0)
    return sides, inverse


def unit_of(pos):
    square = jnp.sum(pos * pos, axis=0, keepdims=True)
    return pos * jnp.where(square > 0.0, lax.rsqrt(square), 0.0)


def pack_kernel(pos_hbm, rhs_hbm, count_hbm, out, pos, rhs, count, sems):
    copies = [
        pltpu.make_async_copy(pos_hbm, pos, sems.at[0]),
        pltpu.make_async_copy(rhs_hbm, rhs, sems.at[1]),
        pltpu.make_async_copy(count_hbm, count, sems.at[2]),
    ]
    for copy in copies:
        copy.start()
    for copy in copies:
        copy.wait()
    width, slots = rhs.shape
    tiles = slots // LANES // 2
    side = (lax.axis_index("offs") + lax.axis_index("blk")) % 2
    odd = side == 1
    n = count[0]
    lane = lax.broadcasted_iota(jnp.int32, (1, LANES), 1)
    held = jnp.clip((n + LANES - 1 - side * LANES + LANES) // (2 * LANES), 0, tiles)
    held = jnp.full((1, LANES), held.astype(f32))
    for t in range(tiles):
        even_at = slice(2 * t * LANES, (2 * t + 1) * LANES)
        odd_at = slice((2 * t + 1) * LANES, (2 * t + 2) * LANES)
        first = (2 * t + side) * LANES
        value = jnp.where(odd, rhs[:, odd_at], rhs[:, even_at])
        out[:, t * LANES : (t + 1) * LANES] = jnp.where(first + lane < n, value, 0.0)
        place = jnp.where(odd, pos[:, odd_at], pos[:, even_at])
        at = (tiles + t // 2) * LANES
        row = (t % 2) * 4
        out[row : row + 4, at : at + LANES] = jnp.concatenate([place, held], axis=0)


def pair_kernel(first, last, start, blocks, tiles, *refs):
    refs = list(refs)
    packet = refs.pop(0)
    if first or last:
        pos_hbm = refs.pop(0)
    if not first:
        rows_in, acc_in = refs.pop(0), refs.pop(0)
    if last:
        noise_hbm, rhs_hbm, count_hbm, out = (refs.pop(0) for _ in range(4))
        acc = refs.pop(0)
    else:
        known_out, acc = refs.pop(0), refs.pop(0)
        rows_ref = refs.pop(0) if first else rows_in
    if last:
        rows_ref = rows_in
    cols, weights = refs.pop(0), refs.pop(0)
    copies = []
    if first or last:
        sems, pos = refs.pop(0), refs.pop(0)
        copies.append(pltpu.make_async_copy(pos_hbm, pos, sems.at[0]))
    if last:
        noise, rhs, count = (refs.pop(0) for _ in range(3))
        copies += [
            pltpu.make_async_copy(noise_hbm, noise, sems.at[1]),
            pltpu.make_async_copy(rhs_hbm, rhs, sems.at[2]),
            pltpu.make_async_copy(count_hbm, count, sems.at[3]),
        ]
    for copy in copies:
        copy.start()
    if not last:
        known_out[...] = packet[...]

    width = packet.shape[0]
    half = tiles * LANES
    stride = half + half // 2
    filled = jnp.int32(0)
    for b in range(start, start + blocks):
        base = b * stride
        for t in range(tiles):
            if t % 2 == 0:
                at = base + half + (t // 2) * LANES
                group = packet[:, at : at + LANES]
                sides, inverse = column_sides(group)
            v = packet[:, base + t * LANES : base + (t + 1) * LANES]
            row = (t % 2) * 4
            v = v * inverse[row + 3 : row + 4]
            rows = []
            for k in range(3):
                product = group[row + k : row + k + 1] * v
                top = product.astype(bf16).astype(f32)
                rows += [top, product - top]
            at = pl.ds(pl.multiple_of(filled + t * LANES, LANES), LANES)
            cols[:, at] = sides[t % 2]
            weights[:, at] = jnp.concatenate(rows, axis=0).astype(bf16)
        held = jnp.max(packet[3:4, base + half : base + half + LANES])
        filled = filled + held.astype(jnp.int32) * LANES
    at = pl.ds(pl.multiple_of(filled, LANES), STEP)
    cols[:, at] = jnp.zeros((cols.shape[0], STEP), bf16)
    weights[:, at] = jnp.zeros((weights.shape[0], STEP), bf16)

    slots = acc.shape[1]
    if first:
        copies[0].wait()
        rows_ref[...] = row_side(pos[...])
        acc[...] = jnp.zeros(acc.shape, f32)
    else:
        acc[...] = acc_in[...]

    def step(begin, size):
        at = pl.ds(pl.multiple_of(begin, LANES), size)
        u = lax.dot_general(
            cols[:, at],
            rows_ref[...],
            (((0,), (0,)), ((), ())),
            preferred_element_type=f32,
        )
        u = jnp.maximum(u, near_sq)
        value = (u + lift) * pl.reciprocal(u * (u + gap), approx=True)
        top = value.astype(bf16)
        low = (value - top.astype(f32)).astype(bf16)
        w = weights[:, at]
        acc[...] += jnp.dot(w, top, preferred_element_type=f32) + jnp.dot(
            w, low, preferred_element_type=f32
        )

    steps = (filled + STEP // 2 - 1) // STEP

    @pl.loop(0, steps)
    def _(i):
        step(i * STEP, STEP)

    @pl.when(filled > steps * STEP)
    def _():
        step(steps * STEP, STEP // 2)

    if not last:
        return
    for copy in copies:
        copy.wait()
    lane = lax.broadcasted_iota(jnp.int32, (1, slots), 1)
    live = (lane < count[0]).astype(f32)
    unit = unit_of(pos[...]) * (live * scale)
    image = jnp.zeros((width, slots), f32)
    for k in range(3):
        at = 2 * k * width
        pulled = acc[at : at + width] + acc[at + width : at + 2 * width]
        image += unit[k : k + 1] * pulled
    direction = rhs[...] * live
    mine = (lax.axis_index("offs") == 0).astype(f32)
    noise_row = noise[...].reshape(1, slots)
    image = image + (mine * noise_row * live) * direction
    out[:, :slots] = image
    dims = (((1,), (1,)), ((), ()))
    both = jnp.concatenate([image, direction * mine], axis=0)
    small = lax.dot_general(
        direction, both, dims, precision=highest, preferred_element_type=f32
    )
    pad = jnp.zeros((width, LANES - 2 * width), f32)
    out[:, slots:] = jnp.concatenate([small, pad], axis=1)


def tail_kernel(small, mine, other, rhs_hbm, count_hbm, sol, res, rhs, count, sems):
    copies = [
        pltpu.make_async_copy(rhs_hbm, rhs, sems.at[0]),
        pltpu.make_async_copy(count_hbm, count, sems.at[1]),
    ]
    for copy in copies:
        copy.start()
    a = small[...]
    width = a.shape[0]
    row = lax.broadcasted_iota(jnp.int32, a.shape, 0)
    for k in range(width):
        pivot = a[k : k + 1] / a[k : k + 1, k : k + 1]
        a = jnp.where(row == k, pivot, a - a[:, k : k + 1] * pivot)
    alpha = a[:, width : 2 * width]
    for copy in copies:
        copy.wait()
    slots = rhs.shape[1]
    lane = lax.broadcasted_iota(jnp.int32, (1, slots), 1)
    direction = rhs[...] * (lane < count[0]).astype(f32)
    image = mine[:, :slots] + other[:, :slots]
    dims = (((0,), (0,)), ((), ()))
    sol[...] = lax.dot_general(
        alpha, direction, dims, precision=highest, preferred_element_type=f32
    )
    res[...] = direction - lax.dot_general(
        alpha, image, dims, precision=highest, preferred_element_type=f32
    )


def call(kernel, out_shape, in_specs, out_specs, scratch, name, flops=0):
    return pl.pallas_call(
        kernel,
        out_shape=out_shape,
        in_specs=in_specs,
        out_specs=out_specs,
        scratch_shapes=scratch,
        compiler_params=pltpu.CompilerParams(vmem_limit_bytes=LIMIT),
        cost_estimate=pl.CostEstimate(
            flops=flops, bytes_accessed=1 << 17, transcendentals=0
        ),
        name=name,
    )


def exchanged(block, distance):
    blocks, sides = lax.axis_size("blk"), lax.axis_size("offs")
    route = [
        ((b ^ distance) * sides + sides - 1 - c, b * sides + c)
        for b in range(blocks)
        for c in range(sides)
    ]
    return lax.ppermute(block, ("blk", "offs"), route)


def body(position, noise_var, rhs, block_count):
    width, slots = rhs.shape
    blocks = lax.axis_size("blk")
    tiles = slots // LANES // 2
    half = tiles * LANES
    shape = jax.ShapeDtypeStruct
    pos_buf = pltpu.VMEM(position.shape, f32)
    rhs_buf = pltpu.VMEM(rhs.shape, f32)
    noise_buf = pltpu.VMEM(noise_var.shape, f32)
    count_buf = pltpu.SMEM((1,), jnp.int32)

    packet = call(
        pack_kernel,
        shape((width, half + half // 2), f32),
        [HBM, HBM, HBM],
        VMEM,
        [pos_buf, rhs_buf, count_buf, pltpu.SemaphoreType.DMA((3,))],
        "pack",
    )(*(pltpu.with_memory_space_constraint(x, pltpu.HBM) for x in (position, rhs)), block_count)

    acc_shape = shape((6 * width, slots), f32)
    rows_shape = shape((32, slots), bf16)

    def pairs(known, start, count, last, rows=None, acc=None):
        first = rows is None
        args, specs = [known], [VMEM]
        if first or last:
            args.append(position)
            specs.append(HBM)
        if not first:
            args += [rows, acc]
            specs += [VMEM] * 2
        scratch = [
            pltpu.VMEM((32, count * half + STEP), bf16),
            pltpu.VMEM((6 * width, count * half + STEP), bf16),
        ]
        if first or last:
            scratch += [pltpu.SemaphoreType.DMA((4,)), pos_buf]
        if last:
            args += [noise_var, rhs, block_count]
            specs += [HBM] * 3
            outs = (shape((width, slots + LANES), f32),)
            scratch = [pltpu.VMEM(acc_shape.shape, f32)] + scratch
            scratch += [noise_buf, rhs_buf, count_buf]
        else:
            outs = (shape(known.shape, f32), acc_shape)
            if first:
                outs += (rows_shape,)
        kernel = functools.partial(pair_kernel, first, last, start, count, tiles)
        flops = 2 * slots * count * half * 64
        specs_out = (VMEM,) * len(outs)
        return call(kernel, outs, specs, specs_out, scratch, f"pairs_{start}", flops)(*args)

    known, start, count = packet, 0, 1
    rows = acc = None
    distance = blocks // 2
    while distance:
        arrived = exchanged(known, distance)
        if rows is None:
            known, acc, rows = pairs(known, start, count, False)
        else:
            known, acc = pairs(known, start, count, False, rows, acc)
        start += count
        count = start
        known = jnp.concatenate([known, arrived], axis=1)
        distance //= 2
    (mine,) = pairs(arrived, 0, count, True, rows, acc)
    other = exchanged(mine, 0)
    small = mine[:, slots:] + other[:, slots:]
    distance = blocks // 2
    while distance:
        small = small + exchanged(small, distance)
        distance //= 2

    return tuple(
        call(
            tail_kernel,
            (shape(rhs.shape, f32),) * 2,
            [VMEM, VMEM, VMEM, HBM, HBM],
            (VMEM, VMEM),
            [rhs_buf, count_buf, pltpu.SemaphoreType.DMA((2,))],
            "tail",
        )(small, mine, other, rhs, block_count)
    )


def solution(mesh):
    return jax.shard_map(
        body,
        mesh=mesh,
        in_specs=(
            P(None, ("mocks", "blk")),
            P(("mocks", "blk")),
            P(None, ("mocks", "blk")),
            P(("mocks", "blk")),
        ),
        out_specs=(P(None, ("mocks", "blk")), P(None, ("mocks", "blk"))),
        check_vma=False,
    )
```

```python
import functools

import jax
import jax.numpy as jnp
from jax import lax
from jax.experimental import pallas as pl
from jax.experimental.pallas import tpu as pltpu
from jax.sharding import PartitionSpec as P

near_weight = 0.6
near_length = 40.0
far_weight = 0.4
far_length = 120.0
near_sq = near_length * near_length
far_sq = far_length * far_length
gap = far_sq - near_sq
scale = near_weight * near_sq + far_weight * far_sq
lift = near_weight * near_sq * gap / scale

LANES = 128
UNIT = 256
STEP = 1024
f32 = jnp.float32
bf16 = jnp.bfloat16
VMEM = pl.BlockSpec(memory_space=pltpu.VMEM)
HBM = pl.BlockSpec(memory_space=pltpu.HBM)
LIMIT = 24 * 2**20
highest = lax.Precision.HIGHEST


def split3(x):
    top = x.astype(bf16).astype(f32)
    rest = x - top
    mid = rest.astype(bf16).astype(f32)
    return top, mid, rest - mid


def row_side(pos):
    width = pos.shape[1]
    one, none = jnp.ones((1, width), f32), jnp.zeros((1, width), f32)
    top, mid, low = split3(pos)
    square = split3(jnp.sum(pos * pos, axis=0, keepdims=True) + near_sq)
    a = jnp.concatenate([top, one, mid, none], axis=0)
    b = jnp.concatenate([top, one, low, none], axis=0)
    c = jnp.concatenate([*square, *[none] * 5], axis=0)
    return jnp.concatenate([a, b, a, c], axis=0).astype(bf16)


def column_sides(group):
    row = lax.broadcasted_iota(jnp.int32, group.shape, 0)
    fourth = row % 4 == 3
    upper = row < 4
    square = group * group
    square = sum(pltpu.roll(square, k, 0) for k in (1, 2, 3))
    scaled = jnp.where(fourth, square, -2.0 * group)
    ahead = split3(scaled)
    swapped = [pltpu.roll(x, 4, 0) for x in ahead]
    tail = jnp.where(upper, 1.0, 0.0)
    sides = []
    for (t, m, w), (tt, mm, _) in ((ahead, swapped), (swapped, ahead)):
        pairs = [(t, tt), (m, tt), (w, mm)]
        rows = [jnp.where(upper, x, y) for x, y in pairs] + [tail]
        sides.append(jnp.concatenate(rows, axis=0).astype(bf16))
    inverse = jnp.where(square > 0.0, lax.rsqrt(square), 0.0)
    return sides, inverse


def unit_of(pos):
    square = jnp.sum(pos * pos, axis=0, keepdims=True)
    return pos * jnp.where(square > 0.0, lax.rsqrt(square), 0.0)


def gram(left, right, first):
    width, slots = left.shape
    lane = lax.broadcasted_iota(jnp.int32, (width, LANES), 1)
    out = jnp.zeros((width, LANES), f32)
    for s in range(width):
        product = left * right[s : s + 1]
        folded = sum(product[:, t : t + LANES] for t in range(0, slots, LANES))
        out = jnp.where(lane == first + s, jnp.sum(folded, axis=1, keepdims=True), out)
    return out


def pack_kernel(pos_hbm, rhs_hbm, count_hbm, out, pos, rhs, count, sems):
    copies = [
        pltpu.make_async_copy(pos_hbm, pos, sems.at[0]),
        pltpu.make_async_copy(rhs_hbm, rhs, sems.at[1]),
        pltpu.make_async_copy(count_hbm, count, sems.at[2]),
    ]
    for copy in copies:
        copy.start()
    for copy in copies:
        copy.wait()
    width, slots = rhs.shape
    tiles = slots // LANES // 2
    side = (lax.axis_index("offs") + lax.axis_index("blk")) % 2
    odd = side == 1
    n = count[0]
    lane = lax.broadcasted_iota(jnp.int32, (1, LANES), 1)
    held = jnp.clip((n + LANES - 1 - side * LANES + LANES) // (2 * LANES), 0, tiles)
    held = jnp.full((1, LANES), held.astype(f32))
    for t in range(tiles):
        even_at = slice(2 * t * LANES, (2 * t + 1) * LANES)
        odd_at = slice((2 * t + 1) * LANES, (2 * t + 2) * LANES)
        first = (2 * t + side) * LANES
        value = jnp.where(odd, rhs[:, odd_at], rhs[:, even_at])
        out[:, t * LANES : (t + 1) * LANES] = jnp.where(first + lane < n, value, 0.0)
        place = jnp.where(odd, pos[:, odd_at], pos[:, even_at])
        at = (tiles + t // 2) * LANES
        row = (t % 2) * 4
        out[row : row + 4, at : at + LANES] = jnp.concatenate([place, held], axis=0)


def pair_kernel(first, last, start, blocks, tiles, *refs):
    refs = list(refs)
    packet = refs.pop(0)
    if first or last:
        pos_hbm = refs.pop(0)
    if not first:
        rows_in, acc_in = refs.pop(0), refs.pop(0)
    if last:
        norm = refs.pop(0)
        noise_hbm, rhs_hbm, count_hbm, out = (refs.pop(0) for _ in range(4))
        acc = refs.pop(0)
    else:
        known_out, acc = refs.pop(0), refs.pop(0)
        rows_ref = refs.pop(0) if first else rows_in
        if first:
            norm = refs.pop(0)
    if last:
        rows_ref = rows_in
    cols, weights = refs.pop(0), refs.pop(0)
    copies = []
    if first or last:
        sems, pos = refs.pop(0), refs.pop(0)
        copies.append(pltpu.make_async_copy(pos_hbm, pos, sems.at[0]))
    if last:
        noise, rhs, count = (refs.pop(0) for _ in range(3))
        copies += [
            pltpu.make_async_copy(noise_hbm, noise, sems.at[1]),
            pltpu.make_async_copy(rhs_hbm, rhs, sems.at[2]),
            pltpu.make_async_copy(count_hbm, count, sems.at[3]),
        ]
    for copy in copies:
        copy.start()
    if not last:
        known_out[...] = packet[...]

    width = packet.shape[0]
    half = tiles * LANES
    stride = half + half // 2
    filled = jnp.int32(0)
    for b in range(start, start + blocks):
        base = b * stride
        for t in range(tiles):
            if t % 2 == 0:
                at = base + half + (t // 2) * LANES
                group = packet[:, at : at + LANES]
                sides, inverse = column_sides(group)
            v = packet[:, base + t * LANES : base + (t + 1) * LANES]
            row = (t % 2) * 4
            v = v * inverse[row + 3 : row + 4]
            rows = []
            for k in range(3):
                product = group[row + k : row + k + 1] * v
                top = product.astype(bf16).astype(f32)
                rows += [top, product - top]
            at = pl.ds(pl.multiple_of(filled + t * LANES, LANES), LANES)
            cols[:, at] = sides[t % 2]
            weights[:, at] = jnp.concatenate(rows, axis=0).astype(bf16)
        held = jnp.max(packet[3:4, base + half : base + half + LANES])
        filled = filled + held.astype(jnp.int32) * LANES
    at = pl.ds(pl.multiple_of(filled, LANES), UNIT)
    cols[:, at] = jnp.zeros((cols.shape[0], UNIT), bf16)
    weights[:, at] = jnp.zeros((weights.shape[0], UNIT), bf16)

    slots = acc.shape[1]
    if first:
        copies[0].wait()
        rows_ref[...] = row_side(pos[...])
        norm[...] = gram(packet[:, :half], packet[:, :half], width)
        acc[...] = jnp.zeros(acc.shape, f32)
    else:
        acc[...] = acc_in[...]

    def step(begin, size):
        at = pl.ds(pl.multiple_of(begin, LANES), size)
        side, w = cols[:, at], weights[:, at]
        for r in range(0, slots, UNIT):
            near = slice(r, r + UNIT)
            u = lax.dot_general(
                side,
                rows_ref[:, near],
                (((0,), (0,)), ((), ())),
                preferred_element_type=f32,
            )
            u = jnp.maximum(u, near_sq)
            value = (u + lift) * pl.reciprocal(u * (u + gap), approx=True)
            top = value.astype(bf16)
            low = (value - top.astype(f32)).astype(bf16)
            part = acc[:, near] + jnp.dot(w, top, preferred_element_type=f32)
            acc[:, near] = part + jnp.dot(w, low, preferred_element_type=f32)

    full = min(STEP, blocks * half)
    steps = (filled + UNIT - LANES) // full
    rest = filled - steps * full

    @pl.loop(0, steps)
    def _(i):
        step(i * full, full)

    for size in range(UNIT, full, UNIT):

        @pl.when((rest > size - UNIT) & (rest <= size))
        def _(size=size):
            step(steps * full, size)

    if not last:
        return
    for copy in copies:
        copy.wait()
    lane = lax.broadcasted_iota(jnp.int32, (1, slots), 1)
    live = (lane < count[0]).astype(f32)
    unit = unit_of(pos[...]) * (live * scale)
    image = jnp.zeros((width, slots), f32)
    for k in range(3):
        at = 2 * k * width
        pulled = acc[at : at + width] + acc[at + width : at + 2 * width]
        image += unit[k : k + 1] * pulled
    direction = rhs[...] * live
    mine = (lax.axis_index("offs") == 0).astype(f32)
    noise_row = noise[...].reshape(1, slots)
    image = image + (mine * noise_row * live) * direction
    out[:, :slots] = image
    out[:, slots:] = norm[...] + gram(direction, image, 0)


def tail_kernel(small, mine, other, rhs_hbm, count_hbm, sol, res, rhs, count, sems):
    copies = [
        pltpu.make_async_copy(rhs_hbm, rhs, sems.at[0]),
        pltpu.make_async_copy(count_hbm, count, sems.at[1]),
    ]
    for copy in copies:
        copy.start()
    a = small[...]
    width = a.shape[0]
    row = lax.broadcasted_iota(jnp.int32, a.shape, 0)
    for k in range(width):
        pivot = a[k : k + 1] / a[k : k + 1, k : k + 1]
        a = jnp.where(row == k, pivot, a - a[:, k : k + 1] * pivot)
    alpha = a[:, width : 2 * width]
    for copy in copies:
        copy.wait()
    slots = rhs.shape[1]
    lane = lax.broadcasted_iota(jnp.int32, (1, slots), 1)
    direction = rhs[...] * (lane < count[0]).astype(f32)
    image = mine[:, :slots] + other[:, :slots]
    dims = (((0,), (0,)), ((), ()))
    sol[...] = lax.dot_general(
        alpha, direction, dims, precision=highest, preferred_element_type=f32
    )
    res[...] = direction - lax.dot_general(
        alpha, image, dims, precision=highest, preferred_element_type=f32
    )


def call(kernel, out_shape, in_specs, out_specs, scratch, name, flops=0):
    return pl.pallas_call(
        kernel,
        out_shape=out_shape,
        in_specs=in_specs,
        out_specs=out_specs,
        scratch_shapes=scratch,
        compiler_params=pltpu.CompilerParams(vmem_limit_bytes=LIMIT),
        cost_estimate=pl.CostEstimate(
            flops=flops, bytes_accessed=1 << 17, transcendentals=0
        ),
        name=name,
    )


def exchanged(block, distance):
    blocks, sides = lax.axis_size("blk"), lax.axis_size("offs")
    route = [
        ((b ^ distance) * sides + sides - 1 - c, b * sides + c)
        for b in range(blocks)
        for c in range(sides)
    ]
    return lax.ppermute(block, ("blk", "offs"), route)


def body(position, noise_var, rhs, block_count):
    width, slots = rhs.shape
    blocks = lax.axis_size("blk")
    tiles = slots // LANES // 2
    half = tiles * LANES
    shape = jax.ShapeDtypeStruct
    pos_buf = pltpu.VMEM(position.shape, f32)
    rhs_buf = pltpu.VMEM(rhs.shape, f32)
    noise_buf = pltpu.VMEM(noise_var.shape, f32)
    count_buf = pltpu.SMEM((1,), jnp.int32)

    packet = call(
        pack_kernel,
        shape((width, half + half // 2), f32),
        [HBM, HBM, HBM],
        VMEM,
        [pos_buf, rhs_buf, count_buf, pltpu.SemaphoreType.DMA((3,))],
        "pack",
    )(*(pltpu.with_memory_space_constraint(x, pltpu.HBM) for x in (position, rhs)), block_count)

    acc_shape = shape((6 * width, slots), f32)
    rows_shape = shape((32, slots), bf16)

    def pairs(known, start, count, last, rows=None, acc=None, norm=None):
        first = rows is None
        args, specs = [known], [VMEM]
        if first or last:
            args.append(position)
            specs.append(HBM)
        if not first:
            args += [rows, acc]
            specs += [VMEM] * 2
        scratch = [
            pltpu.VMEM((32, count * half + UNIT), bf16),
            pltpu.VMEM((6 * width, count * half + UNIT), bf16),
        ]
        if first or last:
            scratch += [pltpu.SemaphoreType.DMA((4,)), pos_buf]
        if last:
            args += [norm, noise_var, rhs, block_count]
            specs += [VMEM] + [HBM] * 3
            outs = (shape((width, slots + LANES), f32),)
            scratch = [pltpu.VMEM(acc_shape.shape, f32)] + scratch
            scratch += [noise_buf, rhs_buf, count_buf]
        else:
            outs = (shape(known.shape, f32), acc_shape)
            if first:
                outs += (rows_shape, shape((width, LANES), f32))
        kernel = functools.partial(pair_kernel, first, last, start, count, tiles)
        flops = 2 * slots * count * half * 64
        specs_out = (VMEM,) * len(outs)
        return call(kernel, outs, specs, specs_out, scratch, f"pairs_{start}", flops)(*args)

    known, start, count = packet, 0, 1
    rows = acc = None
    distance = blocks // 2
    while distance:
        arrived = exchanged(known, distance)
        if rows is None:
            known, acc, rows, norm = pairs(known, start, count, False)
        else:
            known, acc = pairs(known, start, count, False, rows, acc)
        start += count
        count = start
        known = jnp.concatenate([known, arrived], axis=1)
        distance //= 2
    (mine,) = pairs(arrived, 0, count, True, rows, acc, norm)
    other = exchanged(mine, 0)
    small = mine[:, slots:] + other[:, slots:]
    distance = blocks // 2
    while distance:
        small = small + exchanged(small, distance)
        distance //= 2

    return tuple(
        call(
            tail_kernel,
            (shape(rhs.shape, f32),) * 2,
            [VMEM, VMEM, VMEM, HBM, HBM],
            (VMEM, VMEM),
            [rhs_buf, count_buf, pltpu.SemaphoreType.DMA((2,))],
            "tail",
        )(small, mine, other, rhs, block_count)
    )


def solution(mesh):
    return jax.shard_map(
        body,
        mesh=mesh,
        in_specs=(
            P(None, ("mocks", "blk")),
            P(("mocks", "blk")),
            P(None, ("mocks", "blk")),
            P(("mocks", "blk")),
        ),
        out_specs=(P(None, ("mocks", "blk")), P(None, ("mocks", "blk"))),
        check_vma=False,
    )
```

```python
import functools

import jax
import jax.numpy as jnp
from jax import lax
from jax.experimental import pallas as pl
from jax.experimental.pallas import tpu as pltpu
from jax.sharding import PartitionSpec as P

near_weight = 0.6
near_length = 40.0
far_weight = 0.4
far_length = 120.0
near_sq = near_length * near_length
far_sq = far_length * far_length
gap = far_sq - near_sq
scale = near_weight * near_sq + far_weight * far_sq
lift = near_weight * near_sq * gap / scale

LANES = 128
UNIT = 256
STEP = 1024
f32 = jnp.float32
bf16 = jnp.bfloat16
VMEM = pl.BlockSpec(memory_space=pltpu.VMEM)
HBM = pl.BlockSpec(memory_space=pltpu.HBM)
LIMIT = 24 * 2**20
highest = lax.Precision.HIGHEST


def split3(x):
    top = x.astype(bf16).astype(f32)
    rest = x - top
    mid = rest.astype(bf16).astype(f32)
    return top, mid, rest - mid


def row_side(pos):
    width = pos.shape[1]
    one, none = jnp.ones((1, width), f32), jnp.zeros((1, width), f32)
    top, mid, low = split3(pos)
    square = split3(jnp.sum(pos * pos, axis=0, keepdims=True) + near_sq)
    a = jnp.concatenate([top, one, mid, none], axis=0)
    b = jnp.concatenate([top, one, low, none], axis=0)
    c = jnp.concatenate([*square, *[none] * 5], axis=0)
    return jnp.concatenate([a, b, a, c], axis=0).astype(bf16)


def column_sides(group):
    row = lax.broadcasted_iota(jnp.int32, group.shape, 0)
    fourth = row % 4 == 3
    upper = row < 4
    square = group * group
    square = sum(pltpu.roll(square, k, 0) for k in (1, 2, 3))
    scaled = jnp.where(fourth, square, -2.0 * group)
    ahead = split3(scaled)
    swapped = [pltpu.roll(x, 4, 0) for x in ahead]
    tail = jnp.where(upper, 1.0, 0.0)
    sides = []
    for (t, m, w), (tt, mm, _) in ((ahead, swapped), (swapped, ahead)):
        pairs = [(t, tt), (m, tt), (w, mm)]
        rows = [jnp.where(upper, x, y) for x, y in pairs] + [tail]
        sides.append(jnp.concatenate(rows, axis=0).astype(bf16))
    inverse = jnp.where(square > 0.0, lax.rsqrt(square), 0.0)
    return sides, inverse


def unit_of(pos):
    square = jnp.sum(pos * pos, axis=0, keepdims=True)
    return pos * jnp.where(square > 0.0, lax.rsqrt(square), 0.0)


def gram(left, right, first):
    width, slots = left.shape
    lane = lax.broadcasted_iota(jnp.int32, (width, LANES), 1)
    out = jnp.zeros((width, LANES), f32)
    for s in range(width):
        product = left * right[s : s + 1]
        folded = sum(product[:, t : t + LANES] for t in range(0, slots, LANES))
        out = jnp.where(lane == first + s, jnp.sum(folded, axis=1, keepdims=True), out)
    return out


def pack_kernel(pos_hbm, rhs_hbm, count_hbm, out, pos, rhs, count, sems):
    copies = [
        pltpu.make_async_copy(pos_hbm, pos, sems.at[0]),
        pltpu.make_async_copy(rhs_hbm, rhs, sems.at[1]),
        pltpu.make_async_copy(count_hbm, count, sems.at[2]),
    ]
    for copy in copies:
        copy.start()
    for copy in copies:
        copy.wait()
    width, slots = rhs.shape
    tiles = slots // LANES // 2
    side = (lax.axis_index("offs") + lax.axis_index("blk")) % 2
    odd = side == 1
    n = count[0]
    lane = lax.broadcasted_iota(jnp.int32, (1, LANES), 1)
    held = jnp.clip((n + LANES - 1 - side * LANES + LANES) // (2 * LANES), 0, tiles)
    held = jnp.full((1, LANES), held.astype(f32))
    for t in range(tiles):
        even_at = slice(2 * t * LANES, (2 * t + 1) * LANES)
        odd_at = slice((2 * t + 1) * LANES, (2 * t + 2) * LANES)
        first = (2 * t + side) * LANES
        value = jnp.where(odd, rhs[:, odd_at], rhs[:, even_at])
        out[:, t * LANES : (t + 1) * LANES] = jnp.where(first + lane < n, value, 0.0)
        place = jnp.where(odd, pos[:, odd_at], pos[:, even_at])
        at = (tiles + t // 2) * LANES
        row = (t % 2) * 4
        out[row : row + 4, at : at + LANES] = jnp.concatenate([place, held], axis=0)


def pair_kernel(first, last, keep, taken, tiles, *refs):
    refs = list(refs)
    packets = [refs.pop(0) for _ in taken]
    packet = packets[0]
    if first or last:
        pos_hbm = refs.pop(0)
    if not first:
        rows_in, acc_in = refs.pop(0), refs.pop(0)
    if last:
        norm = refs.pop(0)
        noise_hbm, rhs_hbm, count_hbm, out = (refs.pop(0) for _ in range(4))
        acc = refs.pop(0)
    else:
        known_out = refs.pop(0) if keep else None
        acc = refs.pop(0)
        rows_ref = refs.pop(0) if first else rows_in
        if first:
            norm = refs.pop(0)
    if last:
        rows_ref = rows_in
    cols, weights = refs.pop(0), refs.pop(0)
    copies = []
    if first or last:
        sems, pos = refs.pop(0), refs.pop(0)
        copies.append(pltpu.make_async_copy(pos_hbm, pos, sems.at[0]))
    if last:
        noise, rhs, count = (refs.pop(0) for _ in range(3))
        copies += [
            pltpu.make_async_copy(noise_hbm, noise, sems.at[1]),
            pltpu.make_async_copy(rhs_hbm, rhs, sems.at[2]),
            pltpu.make_async_copy(count_hbm, count, sems.at[3]),
        ]
    for copy in copies:
        copy.start()
    if keep:
        known_out[...] = packet[...]

    width = packet.shape[0]
    half = tiles * LANES
    stride = half + half // 2
    filled = jnp.int32(0)
    listed = [(ref, b) for ref, (i, j) in zip(packets, taken) for b in range(i, j)]
    for packet, b in listed:
        base = b * stride
        for t in range(tiles):
            if t % 2 == 0:
                at = base + half + (t // 2) * LANES
                group = packet[:, at : at + LANES]
                sides, inverse = column_sides(group)
            v = packet[:, base + t * LANES : base + (t + 1) * LANES]
            row = (t % 2) * 4
            v = v * inverse[row + 3 : row + 4]
            rows = []
            for k in range(3):
                product = group[row + k : row + k + 1] * v
                top = product.astype(bf16).astype(f32)
                rows += [top, product - top]
            at = pl.ds(pl.multiple_of(filled + t * LANES, LANES), LANES)
            cols[:, at] = sides[t % 2]
            weights[:, at] = jnp.concatenate(rows, axis=0).astype(bf16)
        held = jnp.max(packet[3:4, base + half : base + half + LANES])
        filled = filled + held.astype(jnp.int32) * LANES
    at = pl.ds(pl.multiple_of(filled, LANES), UNIT)
    cols[:, at] = jnp.zeros((cols.shape[0], UNIT), bf16)
    weights[:, at] = jnp.zeros((weights.shape[0], UNIT), bf16)

    slots = acc.shape[1]
    if first:
        copies[0].wait()
        rows_ref[...] = row_side(pos[...])
        norm[...] = gram(packets[0][:, :half], packets[0][:, :half], width)
        acc[...] = jnp.zeros(acc.shape, f32)
    else:
        acc[...] = acc_in[...]

    def step(begin, size):
        at = pl.ds(pl.multiple_of(begin, LANES), size)
        side, w = cols[:, at], weights[:, at]
        for r in range(0, slots, UNIT):
            near = slice(r, r + UNIT)
            u = lax.dot_general(
                side,
                rows_ref[:, near],
                (((0,), (0,)), ((), ())),
                preferred_element_type=f32,
            )
            u = jnp.maximum(u, near_sq)
            value = (u + lift) * pl.reciprocal(u * (u + gap), approx=True)
            top = value.astype(bf16)
            low = (value - top.astype(f32)).astype(bf16)
            part = acc[:, near] + jnp.dot(w, top, preferred_element_type=f32)
            acc[:, near] = part + jnp.dot(w, low, preferred_element_type=f32)

    full = min(STEP, len(listed) * half)
    steps = (filled + UNIT - LANES) // full
    rest = filled - steps * full

    @pl.loop(0, steps)
    def _(i):
        step(i * full, full)

    for size in range(UNIT, full, UNIT):

        @pl.when((rest > size - UNIT) & (rest <= size))
        def _(size=size):
            step(steps * full, size)

    if not last:
        return
    for copy in copies:
        copy.wait()
    lane = lax.broadcasted_iota(jnp.int32, (1, slots), 1)
    live = (lane < count[0]).astype(f32)
    unit = unit_of(pos[...]) * (live * scale)
    image = jnp.zeros((width, slots), f32)
    for k in range(3):
        at = 2 * k * width
        pulled = acc[at : at + width] + acc[at + width : at + 2 * width]
        image += unit[k : k + 1] * pulled
    direction = rhs[...] * live
    mine = (lax.axis_index("offs") == 0).astype(f32)
    noise_row = noise[...].reshape(1, slots)
    image = image + (mine * noise_row * live) * direction
    out[:, :slots] = image
    out[:, slots:] = norm[...] + gram(direction, image, 0)


def tail_kernel(small, mine, other, rhs_hbm, count_hbm, sol, res, rhs, count, sems):
    copies = [
        pltpu.make_async_copy(rhs_hbm, rhs, sems.at[0]),
        pltpu.make_async_copy(count_hbm, count, sems.at[1]),
    ]
    for copy in copies:
        copy.start()
    a = small[...]
    width = a.shape[0]
    row = lax.broadcasted_iota(jnp.int32, a.shape, 0)
    for k in range(width):
        pivot = a[k : k + 1] / a[k : k + 1, k : k + 1]
        a = jnp.where(row == k, pivot, a - a[:, k : k + 1] * pivot)
    alpha = a[:, width : 2 * width]
    for copy in copies:
        copy.wait()
    slots = rhs.shape[1]
    lane = lax.broadcasted_iota(jnp.int32, (1, slots), 1)
    direction = rhs[...] * (lane < count[0]).astype(f32)
    image = mine[:, :slots] + other[:, :slots]
    dims = (((0,), (0,)), ((), ()))
    sol[...] = lax.dot_general(
        alpha, direction, dims, precision=highest, preferred_element_type=f32
    )
    res[...] = direction - lax.dot_general(
        alpha, image, dims, precision=highest, preferred_element_type=f32
    )


def call(kernel, out_shape, in_specs, out_specs, scratch, name, flops=0):
    return pl.pallas_call(
        kernel,
        out_shape=out_shape,
        in_specs=in_specs,
        out_specs=out_specs,
        scratch_shapes=scratch,
        compiler_params=pltpu.CompilerParams(vmem_limit_bytes=LIMIT),
        cost_estimate=pl.CostEstimate(
            flops=flops, bytes_accessed=1 << 17, transcendentals=0
        ),
        name=name,
    )


def exchanged(block, distance):
    blocks, sides = lax.axis_size("blk"), lax.axis_size("offs")
    route = [
        ((b ^ distance) * sides + sides - 1 - c, b * sides + c)
        for b in range(blocks)
        for c in range(sides)
    ]
    return lax.ppermute(block, ("blk", "offs"), route)


def body(position, noise_var, rhs, block_count):
    width, slots = rhs.shape
    blocks = lax.axis_size("blk")
    tiles = slots // LANES // 2
    half = tiles * LANES
    shape = jax.ShapeDtypeStruct
    pos_buf = pltpu.VMEM(position.shape, f32)
    rhs_buf = pltpu.VMEM(rhs.shape, f32)
    noise_buf = pltpu.VMEM(noise_var.shape, f32)
    count_buf = pltpu.SMEM((1,), jnp.int32)

    packet = call(
        pack_kernel,
        shape((width, half + half // 2), f32),
        [HBM, HBM, HBM],
        VMEM,
        [pos_buf, rhs_buf, count_buf, pltpu.SemaphoreType.DMA((3,))],
        "pack",
    )(*(pltpu.with_memory_space_constraint(x, pltpu.HBM) for x in (position, rhs)), block_count)

    acc_shape = shape((6 * width, slots), f32)
    rows_shape = shape((32, slots), bf16)

    def pairs(parts, taken, rows=None, acc=None, norm=None, keep=False):
        first, last = rows is None, norm is not None
        args, specs = list(parts), [VMEM] * len(parts)
        if first or last:
            args.append(position)
            specs.append(HBM)
        if not first:
            args += [rows, acc]
            specs += [VMEM] * 2
        count = sum(stop - start for start, stop in taken)
        scratch = [
            pltpu.VMEM((32, count * half + UNIT), bf16),
            pltpu.VMEM((6 * width, count * half + UNIT), bf16),
        ]
        if first or last:
            scratch += [pltpu.SemaphoreType.DMA((4,)), pos_buf]
        if last:
            args += [norm, noise_var, rhs, block_count]
            specs += [VMEM] + [HBM] * 3
            outs = (shape((width, slots + LANES), f32),)
            scratch = [pltpu.VMEM(acc_shape.shape, f32)] + scratch
            scratch += [noise_buf, rhs_buf, count_buf]
        else:
            outs = (shape(parts[0].shape, f32),) if keep else ()
            outs += (acc_shape,)
            if first:
                outs += (rows_shape, shape((width, LANES), f32))
        kernel = functools.partial(pair_kernel, first, last, keep, taken, tiles)
        flops = 2 * slots * count * half * 64
        name = f"pairs_{count}"
        return call(kernel, outs, specs, (VMEM,) * len(outs), scratch, name, flops)(*args)

    distances = [blocks >> k for k in range(1, blocks.bit_length())]
    known, size = packet, 1
    rows = None
    for distance in distances[:-2]:
        arrived = exchanged(known, distance)
        fresh = (size // 2, size)
        if rows is None:
            known, acc, rows, norm = pairs([known], [fresh], keep=True)
        else:
            known, acc = pairs([known], [fresh], rows, acc, keep=True)
        known = jnp.concatenate([known, arrived], axis=1)
        size *= 2
    near = exchanged(known, distances[-2])
    far = exchanged(known, distances[-1])
    (acc,) = pairs([known], [(size // 2, size)], rows, acc)
    near, acc = lax.optimization_barrier((near, acc))
    rest = exchanged(near, distances[-1])
    (acc,) = pairs([near, far], [(0, size)] * 2, rows, acc)
    (mine,) = pairs([rest], [(0, size)], rows, acc, norm)
    other = exchanged(mine, 0)
    small = mine[:, slots:] + other[:, slots:]
    distance = blocks // 2
    while distance:
        small = small + exchanged(small, distance)
        distance //= 2

    return tuple(
        call(
            tail_kernel,
            (shape(rhs.shape, f32),) * 2,
            [VMEM, VMEM, VMEM, HBM, HBM],
            (VMEM, VMEM),
            [rhs_buf, count_buf, pltpu.SemaphoreType.DMA((2,))],
            "tail",
        )(small, mine, other, rhs, block_count)
    )


def solution(mesh):
    return jax.shard_map(
        body,
        mesh=mesh,
        in_specs=(
            P(None, ("mocks", "blk")),
            P(("mocks", "blk")),
            P(None, ("mocks", "blk")),
            P(("mocks", "blk")),
        ),
        out_specs=(P(None, ("mocks", "blk")), P(None, ("mocks", "blk"))),
        check_vma=False,
    )
```

```python
import functools

import jax
import jax.numpy as jnp
from jax import lax
from jax.experimental import pallas as pl
from jax.experimental.pallas import tpu as pltpu
from jax.sharding import PartitionSpec as P

near_weight = 0.6
near_length = 40.0
far_weight = 0.4
far_length = 120.0
near_sq = near_length * near_length
far_sq = far_length * far_length
gap = far_sq - near_sq
scale = near_weight * near_sq + far_weight * far_sq
lift = near_weight * near_sq * gap / scale

LANES = 128
UNIT = 256
STEP = 1024
f32 = jnp.float32
bf16 = jnp.bfloat16
VMEM = pl.BlockSpec(memory_space=pltpu.VMEM)
HBM = pl.BlockSpec(memory_space=pltpu.HBM)
LIMIT = 24 * 2**20


def split3(x):
    top = x.astype(bf16).astype(f32)
    rest = x - top
    mid = rest.astype(bf16).astype(f32)
    return top, mid, rest - mid


def row_side(pos):
    width = pos.shape[1]
    one, none = jnp.ones((1, width), f32), jnp.zeros((1, width), f32)
    top, mid, low = split3(pos)
    square = split3(jnp.sum(pos * pos, axis=0, keepdims=True) + near_sq)
    a = jnp.concatenate([top, one, mid, none], axis=0)
    b = jnp.concatenate([top, one, low, none], axis=0)
    c = jnp.concatenate([*square, *[none] * 5], axis=0)
    return jnp.concatenate([a, b, a, c], axis=0).astype(bf16)


def column_sides(group):
    row = lax.broadcasted_iota(jnp.int32, group.shape, 0)
    fourth = row % 4 == 3
    upper = row < 4
    square = group * group
    square = sum(pltpu.roll(square, k, 0) for k in (1, 2, 3))
    scaled = jnp.where(fourth, square, -2.0 * group)
    ahead = split3(scaled)
    swapped = [pltpu.roll(x, 4, 0) for x in ahead]
    tail = jnp.where(upper, 1.0, 0.0)
    sides = []
    for (t, m, w), (tt, mm, _) in ((ahead, swapped), (swapped, ahead)):
        pairs = [(t, tt), (m, tt), (w, mm)]
        rows = [jnp.where(upper, x, y) for x, y in pairs] + [tail]
        sides.append(jnp.concatenate(rows, axis=0).astype(bf16))
    inverse = jnp.where(square > 0.0, lax.rsqrt(square), 0.0)
    return sides, inverse


def unit_of(pos):
    square = jnp.sum(pos * pos, axis=0, keepdims=True)
    return pos * jnp.where(square > 0.0, lax.rsqrt(square), 0.0)


def gram(left, right, first):
    width, slots = left.shape
    lane = lax.broadcasted_iota(jnp.int32, (width, LANES), 1)
    out = jnp.zeros((width, LANES), f32)
    for s in range(width):
        product = left * right[s : s + 1]
        folded = sum(product[:, t : t + LANES] for t in range(0, slots, LANES))
        out = jnp.where(lane == first + s, jnp.sum(folded, axis=1, keepdims=True), out)
    return out


def pack_kernel(pos_hbm, rhs_hbm, count_hbm, out, pos, rhs, count, sems):
    copies = [
        pltpu.make_async_copy(pos_hbm, pos, sems.at[0]),
        pltpu.make_async_copy(rhs_hbm, rhs, sems.at[1]),
        pltpu.make_async_copy(count_hbm, count, sems.at[2]),
    ]
    for copy in copies:
        copy.start()
    for copy in copies:
        copy.wait()
    width, slots = rhs.shape
    tiles = slots // LANES // 2
    side = (lax.axis_index("offs") + lax.axis_index("blk")) % 2
    odd = side == 1
    n = count[0]
    lane = lax.broadcasted_iota(jnp.int32, (1, LANES), 1)
    held = jnp.clip((n + LANES - 1 - side * LANES + LANES) // (2 * LANES), 0, tiles)
    held = jnp.full((1, LANES), held.astype(f32))
    for t in range(tiles):
        even_at = slice(2 * t * LANES, (2 * t + 1) * LANES)
        odd_at = slice((2 * t + 1) * LANES, (2 * t + 2) * LANES)
        first = (2 * t + side) * LANES
        value = jnp.where(odd, rhs[:, odd_at], rhs[:, even_at])
        out[:, t * LANES : (t + 1) * LANES] = jnp.where(first + lane < n, value, 0.0)
        place = jnp.where(odd, pos[:, odd_at], pos[:, even_at])
        at = (tiles + t // 2) * LANES
        row = (t % 2) * 4
        out[row : row + 4, at : at + LANES] = jnp.concatenate([place, held], axis=0)


def pair_kernel(first, last, keep, taken, tiles, *refs):
    refs = list(refs)
    packets = [refs.pop(0) for _ in taken]
    packet = packets[0]
    if first or last:
        pos_hbm = refs.pop(0)
    if not first:
        rows_in, acc_in = refs.pop(0), refs.pop(0)
    if last:
        norm = refs.pop(0)
        noise_hbm, rhs_hbm, count_hbm = (refs.pop(0) for _ in range(3))
        out, direction_out = refs.pop(0), refs.pop(0)
        acc = refs.pop(0)
    else:
        known_out = refs.pop(0) if keep else None
        acc = refs.pop(0)
        rows_ref = refs.pop(0) if first else rows_in
        if first:
            norm = refs.pop(0)
    if last:
        rows_ref = rows_in
    cols, weights = refs.pop(0), refs.pop(0)
    copies = []
    if first or last:
        sems, pos = refs.pop(0), refs.pop(0)
        copies.append(pltpu.make_async_copy(pos_hbm, pos, sems.at[0]))
    if last:
        noise, rhs, count = (refs.pop(0) for _ in range(3))
        copies += [
            pltpu.make_async_copy(noise_hbm, noise, sems.at[1]),
            pltpu.make_async_copy(rhs_hbm, rhs, sems.at[2]),
            pltpu.make_async_copy(count_hbm, count, sems.at[3]),
        ]
    for copy in copies:
        copy.start()
    if keep:
        known_out[...] = packet[...]

    width = packet.shape[0]
    half = tiles * LANES
    stride = half + half // 2
    filled = jnp.int32(0)
    listed = [(ref, b) for ref, (i, j) in zip(packets, taken) for b in range(i, j)]
    for packet, b in listed:
        base = b * stride
        for t in range(tiles):
            if t % 2 == 0:
                at = base + half + (t // 2) * LANES
                group = packet[:, at : at + LANES]
                sides, inverse = column_sides(group)
            v = packet[:, base + t * LANES : base + (t + 1) * LANES]
            row = (t % 2) * 4
            v = v * inverse[row + 3 : row + 4]
            rows = []
            for k in range(3):
                product = group[row + k : row + k + 1] * v
                top = product.astype(bf16).astype(f32)
                rows += [top, product - top]
            at = pl.ds(pl.multiple_of(filled + t * LANES, LANES), LANES)
            cols[:, at] = sides[t % 2]
            weights[:, at] = jnp.concatenate(rows, axis=0).astype(bf16)
        held = jnp.max(packet[3:4, base + half : base + half + LANES])
        filled = filled + held.astype(jnp.int32) * LANES
    at = pl.ds(pl.multiple_of(filled, LANES), UNIT)
    cols[:, at] = jnp.zeros((cols.shape[0], UNIT), bf16)
    weights[:, at] = jnp.zeros((weights.shape[0], UNIT), bf16)

    slots = acc.shape[1]
    if first:
        copies[0].wait()
        rows_ref[...] = row_side(pos[...])
        norm[...] = gram(packets[0][:, :half], packets[0][:, :half], width)
        acc[...] = jnp.zeros(acc.shape, f32)
    else:
        acc[...] = acc_in[...]

    def step(begin, size):
        at = pl.ds(pl.multiple_of(begin, LANES), size)
        side, w = cols[:, at], weights[:, at]
        for r in range(0, slots, UNIT):
            near = slice(r, r + UNIT)
            u = lax.dot_general(
                side,
                rows_ref[:, near],
                (((0,), (0,)), ((), ())),
                preferred_element_type=f32,
            )
            u = jnp.maximum(u, near_sq)
            value = (u + lift) * pl.reciprocal(u * (u + gap), approx=True)
            top = value.astype(bf16)
            low = (value - top.astype(f32)).astype(bf16)
            part = acc[:, near] + jnp.dot(w, top, preferred_element_type=f32)
            acc[:, near] = part + jnp.dot(w, low, preferred_element_type=f32)

    full = min(STEP, len(listed) * half)
    steps = (filled + UNIT - LANES) // full
    rest = filled - steps * full

    @pl.loop(0, steps)
    def _(i):
        step(i * full, full)

    for size in range(UNIT, full, UNIT):

        @pl.when((rest > size - UNIT) & (rest <= size))
        def _(size=size):
            step(steps * full, size)

    if not last:
        return
    for copy in copies:
        copy.wait()
    lane = lax.broadcasted_iota(jnp.int32, (1, slots), 1)
    live = (lane < count[0]).astype(f32)
    unit = unit_of(pos[...]) * (live * scale)
    image = jnp.zeros((width, slots), f32)
    for k in range(3):
        at = 2 * k * width
        pulled = acc[at : at + width] + acc[at + width : at + 2 * width]
        image += unit[k : k + 1] * pulled
    direction = rhs[...] * live
    direction_out[...] = direction
    mine = (lax.axis_index("offs") == 0).astype(f32)
    noise_row = noise[...].reshape(1, slots)
    image = image + (mine * noise_row * live) * direction
    out[:, :slots] = image
    out[:, slots:] = norm[...] + gram(direction, image, 0)


def solved(small):
    width = small.shape[0]
    shape = small.shape
    c = [jnp.broadcast_to(small[:, j : j + 1], shape) for j in range(width)]
    r = [
        jnp.broadcast_to(small[:, j : j + 1], shape) for j in range(width, 2 * width)
    ]
    for k in range(width):
        inverse = pl.reciprocal(c[k], approx=True)[k : k + 1]
        ck, rk = c[k], r[k]
        for j in range(width):
            if j != k:
                factor = c[j][k : k + 1] * inverse
                c[j] = c[j] - ck * factor
                r[j] = r[j] - rk * factor
        c[k], r[k] = ck * inverse, rk * inverse
    return r


def combined(columns, x):
    parts = []
    for t in range(0, x.shape[1], LANES):
        tile = x[:, t : t + LANES]
        parts.append(sum(col * tile[m : m + 1] for m, col in enumerate(columns)))
    return jnp.concatenate(parts, axis=1)


def tail_kernel(small, mine, other, direction_ref, sol, res):
    columns = solved(small[...])
    direction = direction_ref[...]
    slots = direction.shape[1]
    image = mine[:, :slots] + other[:, :slots]
    sol[...] = combined(columns, direction)
    res[...] = direction - combined(columns, image)


def call(kernel, out_shape, in_specs, out_specs, scratch, name, flops=0):
    return pl.pallas_call(
        kernel,
        out_shape=out_shape,
        in_specs=in_specs,
        out_specs=out_specs,
        scratch_shapes=scratch,
        compiler_params=pltpu.CompilerParams(vmem_limit_bytes=LIMIT),
        cost_estimate=pl.CostEstimate(
            flops=flops, bytes_accessed=1 << 17, transcendentals=0
        ),
        name=name,
    )


def exchanged(block, distance):
    blocks, sides = lax.axis_size("blk"), lax.axis_size("offs")
    route = [
        ((b ^ distance) * sides + sides - 1 - c, b * sides + c)
        for b in range(blocks)
        for c in range(sides)
    ]
    return lax.ppermute(block, ("blk", "offs"), route)


def body(position, noise_var, rhs, block_count):
    width, slots = rhs.shape
    blocks = lax.axis_size("blk")
    tiles = slots // LANES // 2
    half = tiles * LANES
    shape = jax.ShapeDtypeStruct
    pos_buf = pltpu.VMEM(position.shape, f32)
    rhs_buf = pltpu.VMEM(rhs.shape, f32)
    noise_buf = pltpu.VMEM(noise_var.shape, f32)
    count_buf = pltpu.SMEM((1,), jnp.int32)

    packet = call(
        pack_kernel,
        shape((width, half + half // 2), f32),
        [HBM, HBM, HBM],
        VMEM,
        [pos_buf, rhs_buf, count_buf, pltpu.SemaphoreType.DMA((3,))],
        "pack",
    )(*(pltpu.with_memory_space_constraint(x, pltpu.HBM) for x in (position, rhs)), block_count)

    acc_shape = shape((6 * width, slots), f32)
    rows_shape = shape((32, slots), bf16)

    def pairs(parts, taken, rows=None, acc=None, norm=None, keep=False):
        first, last = rows is None, norm is not None
        args, specs = list(parts), [VMEM] * len(parts)
        if first or last:
            args.append(position)
            specs.append(HBM)
        if not first:
            args += [rows, acc]
            specs += [VMEM] * 2
        count = sum(stop - start for start, stop in taken)
        scratch = [
            pltpu.VMEM((32, count * half + UNIT), bf16),
            pltpu.VMEM((6 * width, count * half + UNIT), bf16),
        ]
        if first or last:
            scratch += [pltpu.SemaphoreType.DMA((4,)), pos_buf]
        if last:
            args += [norm, noise_var, rhs, block_count]
            specs += [VMEM] + [HBM] * 3
            outs = (shape((width, slots + LANES), f32), shape((width, slots), f32))
            scratch = [pltpu.VMEM(acc_shape.shape, f32)] + scratch
            scratch += [noise_buf, rhs_buf, count_buf]
        else:
            outs = (shape(parts[0].shape, f32),) if keep else ()
            outs += (acc_shape,)
            if first:
                outs += (rows_shape, shape((width, LANES), f32))
        kernel = functools.partial(pair_kernel, first, last, keep, taken, tiles)
        flops = 2 * slots * count * half * 64
        name = f"pairs_{count}"
        return call(kernel, outs, specs, (VMEM,) * len(outs), scratch, name, flops)(*args)

    distances = [blocks >> k for k in range(1, blocks.bit_length())]
    known, size = packet, 1
    rows = None
    for distance in distances[:-2]:
        arrived = exchanged(known, distance)
        fresh = (size // 2, size)
        if rows is None:
            known, acc, rows, norm = pairs([known], [fresh], keep=True)
        else:
            known, acc = pairs([known], [fresh], rows, acc, keep=True)
        known = jnp.concatenate([known, arrived], axis=1)
        size *= 2
    near = exchanged(known, distances[-2])
    far = exchanged(known, distances[-1])
    (acc,) = pairs([known], [(size // 2, size)], rows, acc)
    near, acc = lax.optimization_barrier((near, acc))
    rest = exchanged(near, distances[-1])
    (acc,) = pairs([near, far], [(0, size)] * 2, rows, acc)
    mine, direction = pairs([rest], [(0, size)], rows, acc, norm)
    other = exchanged(mine, 0)
    small = mine[:, slots:] + other[:, slots:]
    distance = blocks // 2
    while distance:
        small = small + exchanged(small, distance)
        distance //= 2

    return tuple(
        call(
            tail_kernel,
            (shape(rhs.shape, f32),) * 2,
            [VMEM] * 4,
            (VMEM, VMEM),
            [],
            "tail",
        )(small, mine, other, direction)
    )


def solution(mesh):
    return jax.shard_map(
        body,
        mesh=mesh,
        in_specs=(
            P(None, ("mocks", "blk")),
            P(("mocks", "blk")),
            P(None, ("mocks", "blk")),
            P(("mocks", "blk")),
        ),
        out_specs=(P(None, ("mocks", "blk")), P(None, ("mocks", "blk"))),
        check_vma=False,
    )
```

```python
import functools

import jax
import jax.numpy as jnp
from jax import lax
from jax.experimental import pallas as pl
from jax.experimental.pallas import tpu as pltpu
from jax.sharding import PartitionSpec as P

near_weight = 0.6
near_length = 40.0
far_weight = 0.4
far_length = 120.0
near_sq = near_length * near_length
far_sq = far_length * far_length
gap = far_sq - near_sq
scale = near_weight * near_sq + far_weight * far_sq
lift = near_weight * near_sq * gap / scale

LANES = 128
UNIT = 256
STEP = 1024
f32 = jnp.float32
bf16 = jnp.bfloat16
VMEM = pl.BlockSpec(memory_space=pltpu.VMEM)
HBM = pl.BlockSpec(memory_space=pltpu.HBM)
LIMIT = 24 * 2**20


def split3(x):
    top = x.astype(bf16).astype(f32)
    rest = x - top
    mid = rest.astype(bf16).astype(f32)
    return top, mid, rest - mid


def row_side(pos):
    width = pos.shape[1]
    one, none = jnp.ones((1, width), f32), jnp.zeros((1, width), f32)
    top, mid, low = split3(pos)
    square = split3(jnp.sum(pos * pos, axis=0, keepdims=True) + near_sq)
    a = jnp.concatenate([top, one, mid, none], axis=0)
    b = jnp.concatenate([top, one, low, none], axis=0)
    c = jnp.concatenate([*square, *[none] * 5], axis=0)
    return jnp.concatenate([a, b, a, c], axis=0).astype(bf16)


def column_sides(group):
    row = lax.broadcasted_iota(jnp.int32, group.shape, 0)
    fourth = row % 4 == 3
    upper = row < 4
    square = group * group
    square = sum(pltpu.roll(square, k, 0) for k in (1, 2, 3))
    scaled = jnp.where(fourth, square, -2.0 * group)
    ahead = split3(scaled)
    swapped = [pltpu.roll(x, 4, 0) for x in ahead]
    tail = jnp.where(upper, 1.0, 0.0)
    sides = []
    for (t, m, w), (tt, mm, _) in ((ahead, swapped), (swapped, ahead)):
        pairs = [(t, tt), (m, tt), (w, mm)]
        rows = [jnp.where(upper, x, y) for x, y in pairs] + [tail]
        sides.append(jnp.concatenate(rows, axis=0).astype(bf16))
    inverse = jnp.where(square > 0.0, lax.rsqrt(square), 0.0)
    return sides, inverse


def unit_of(pos):
    square = jnp.sum(pos * pos, axis=0, keepdims=True)
    return pos * jnp.where(square > 0.0, lax.rsqrt(square), 0.0)


def gram(left, right, first):
    width, slots = left.shape
    lane = lax.broadcasted_iota(jnp.int32, (width, LANES), 1)
    out = jnp.zeros((width, LANES), f32)
    for s in range(width):
        product = left * right[s : s + 1]
        folded = sum(product[:, t : t + LANES] for t in range(0, slots, LANES))
        out = jnp.where(lane == first + s, jnp.sum(folded, axis=1, keepdims=True), out)
    return out


def pack_kernel(pos_hbm, rhs_hbm, count_hbm, out, pos, rhs, count, sems):
    copies = [
        pltpu.make_async_copy(pos_hbm, pos, sems.at[0]),
        pltpu.make_async_copy(rhs_hbm, rhs, sems.at[1]),
        pltpu.make_async_copy(count_hbm, count, sems.at[2]),
    ]
    for copy in copies:
        copy.start()
    for copy in copies:
        copy.wait()
    width, slots = rhs.shape
    tiles = slots // LANES // 2
    side = (lax.axis_index("offs") + lax.axis_index("blk")) % 2
    odd = side == 1
    n = count[0]
    lane = lax.broadcasted_iota(jnp.int32, (1, LANES), 1)
    held = jnp.clip((n + LANES - 1 - side * LANES + LANES) // (2 * LANES), 0, tiles)
    held = jnp.full((1, LANES), held.astype(f32))
    for t in range(tiles):
        even_at = slice(2 * t * LANES, (2 * t + 1) * LANES)
        odd_at = slice((2 * t + 1) * LANES, (2 * t + 2) * LANES)
        first = (2 * t + side) * LANES
        value = jnp.where(odd, rhs[:, odd_at], rhs[:, even_at])
        out[:, t * LANES : (t + 1) * LANES] = jnp.where(first + lane < n, value, 0.0)
        place = jnp.where(odd, pos[:, odd_at], pos[:, even_at])
        at = (tiles + t // 2) * LANES
        row = (t % 2) * 4
        out[row : row + 4, at : at + LANES] = jnp.concatenate([place, held], axis=0)


def pair_kernel(first, last, keep, taken, tiles, *refs):
    refs = list(refs)
    packets = [refs.pop(0) for _ in taken]
    packet = packets[0]
    if first or last:
        pos_hbm = refs.pop(0)
    if not first:
        rows_in, acc_in = refs.pop(0), refs.pop(0)
    if last:
        norm = refs.pop(0)
        noise_hbm, rhs_hbm, count_hbm = (refs.pop(0) for _ in range(3))
        out, direction_out = refs.pop(0), refs.pop(0)
        acc = refs.pop(0)
    else:
        known_out = refs.pop(0) if keep else None
        acc = refs.pop(0)
        rows_ref = refs.pop(0) if first else rows_in
        if first:
            norm = refs.pop(0)
    if last:
        rows_ref = rows_in
    cols, weights = refs.pop(0), refs.pop(0)
    copies = []
    if first or last:
        sems, pos = refs.pop(0), refs.pop(0)
        copies.append(pltpu.make_async_copy(pos_hbm, pos, sems.at[0]))
    if last:
        noise, rhs, count = (refs.pop(0) for _ in range(3))
        copies += [
            pltpu.make_async_copy(noise_hbm, noise, sems.at[1]),
            pltpu.make_async_copy(rhs_hbm, rhs, sems.at[2]),
            pltpu.make_async_copy(count_hbm, count, sems.at[3]),
        ]
    for copy in copies:
        copy.start()
    if keep:
        known_out[...] = packet[...]

    width = packet.shape[0]
    half = tiles * LANES
    stride = half + half // 2
    filled = jnp.int32(0)
    listed = [(ref, b) for ref, (i, j) in zip(packets, taken) for b in range(i, j)]
    for packet, b in listed:
        base = b * stride
        for t in range(tiles):
            if t % 2 == 0:
                at = base + half + (t // 2) * LANES
                group = packet[:, at : at + LANES]
                sides, inverse = column_sides(group)
            v = packet[:, base + t * LANES : base + (t + 1) * LANES]
            row = (t % 2) * 4
            v = v * inverse[row + 3 : row + 4]
            rows = []
            for k in range(3):
                product = group[row + k : row + k + 1] * v
                top = product.astype(bf16).astype(f32)
                rows += [top, product - top]
            at = pl.ds(pl.multiple_of(filled + t * LANES, LANES), LANES)
            cols[:, at] = sides[t % 2]
            weights[:, at] = jnp.concatenate(rows, axis=0).astype(bf16)
        held = jnp.max(packet[3:4, base + half : base + half + LANES])
        filled = filled + held.astype(jnp.int32) * LANES

    slots = acc.shape[1]
    if first:
        copies[0].wait()
        rows_ref[...] = row_side(pos[...])
        norm[...] = gram(packets[0][:, :half], packets[0][:, :half], width)
        acc[...] = jnp.zeros(acc.shape, f32)
    else:
        acc[...] = acc_in[...]

    def step(begin, size):
        at = pl.ds(pl.multiple_of(begin, LANES), size)
        side, w = cols[:, at], weights[:, at]
        for r in range(0, slots, UNIT):
            near = slice(r, r + UNIT)
            u = lax.dot_general(
                side,
                rows_ref[:, near],
                (((0,), (0,)), ((), ())),
                preferred_element_type=f32,
            )
            u = jnp.maximum(u, near_sq)
            value = (u + lift) * pl.reciprocal(u * (u + gap), approx=True)
            top = value.astype(bf16)
            low = (value - top.astype(f32)).astype(bf16)
            part = acc[:, near] + jnp.dot(w, top, preferred_element_type=f32)
            acc[:, near] = part + jnp.dot(w, low, preferred_element_type=f32)

    full = min(STEP, len(listed) * half)
    steps = filled // full
    rest = filled - steps * full

    @pl.loop(0, steps)
    def _(i):
        step(i * full, full)

    for size in range(LANES, full, LANES):

        @pl.when(rest == size)
        def _(size=size):
            step(steps * full, size)

    if not last:
        return
    for copy in copies:
        copy.wait()
    lane = lax.broadcasted_iota(jnp.int32, (1, slots), 1)
    live = (lane < count[0]).astype(f32)
    unit = unit_of(pos[...]) * (live * scale)
    image = jnp.zeros((width, slots), f32)
    for k in range(3):
        at = 2 * k * width
        pulled = acc[at : at + width] + acc[at + width : at + 2 * width]
        image += unit[k : k + 1] * pulled
    direction = rhs[...] * live
    direction_out[...] = direction
    mine = (lax.axis_index("offs") == 0).astype(f32)
    noise_row = noise[...].reshape(1, slots)
    image = image + (mine * noise_row * live) * direction
    out[:, :slots] = image
    out[:, slots:] = norm[...] + gram(direction, image, 0)


def solved(small):
    width = small.shape[0]
    shape = small.shape
    c = [jnp.broadcast_to(small[:, j : j + 1], shape) for j in range(width)]
    r = [
        jnp.broadcast_to(small[:, j : j + 1], shape) for j in range(width, 2 * width)
    ]
    for k in range(width):
        inverse = pl.reciprocal(c[k], approx=True)[k : k + 1]
        ck, rk = c[k], r[k]
        for j in range(width):
            if j != k:
                factor = c[j][k : k + 1] * inverse
                c[j] = c[j] - ck * factor
                r[j] = r[j] - rk * factor
        c[k], r[k] = ck * inverse, rk * inverse
    return r


def combined(columns, x):
    parts = []
    for t in range(0, x.shape[1], LANES):
        tile = x[:, t : t + LANES]
        parts.append(sum(col * tile[m : m + 1] for m, col in enumerate(columns)))
    return jnp.concatenate(parts, axis=1)


def tail_kernel(small, mine, other, direction_ref, sol, res):
    columns = solved(small[...])
    direction = direction_ref[...]
    slots = direction.shape[1]
    image = mine[:, :slots] + other[:, :slots]
    sol[...] = combined(columns, direction)
    res[...] = direction - combined(columns, image)


def call(kernel, out_shape, in_specs, out_specs, scratch, name, flops=0):
    return pl.pallas_call(
        kernel,
        out_shape=out_shape,
        in_specs=in_specs,
        out_specs=out_specs,
        scratch_shapes=scratch,
        compiler_params=pltpu.CompilerParams(vmem_limit_bytes=LIMIT),
        cost_estimate=pl.CostEstimate(
            flops=flops, bytes_accessed=1 << 17, transcendentals=0
        ),
        name=name,
    )


def exchanged(block, distance):
    blocks, sides = lax.axis_size("blk"), lax.axis_size("offs")
    route = [
        ((b ^ distance) * sides + sides - 1 - c, b * sides + c)
        for b in range(blocks)
        for c in range(sides)
    ]
    return lax.ppermute(block, ("blk", "offs"), route)


def body(position, noise_var, rhs, block_count):
    width, slots = rhs.shape
    blocks = lax.axis_size("blk")
    tiles = slots // LANES // 2
    half = tiles * LANES
    shape = jax.ShapeDtypeStruct
    pos_buf = pltpu.VMEM(position.shape, f32)
    rhs_buf = pltpu.VMEM(rhs.shape, f32)
    noise_buf = pltpu.VMEM(noise_var.shape, f32)
    count_buf = pltpu.SMEM((1,), jnp.int32)

    packet = call(
        pack_kernel,
        shape((width, half + half // 2), f32),
        [HBM, HBM, HBM],
        VMEM,
        [pos_buf, rhs_buf, count_buf, pltpu.SemaphoreType.DMA((3,))],
        "pack",
    )(*(pltpu.with_memory_space_constraint(x, pltpu.HBM) for x in (position, rhs)), block_count)

    acc_shape = shape((6 * width, slots), f32)
    rows_shape = shape((32, slots), bf16)

    def pairs(parts, taken, rows=None, acc=None, norm=None, keep=False):
        first, last = rows is None, norm is not None
        args, specs = list(parts), [VMEM] * len(parts)
        if first or last:
            args.append(position)
            specs.append(HBM)
        if not first:
            args += [rows, acc]
            specs += [VMEM] * 2
        count = sum(stop - start for start, stop in taken)
        scratch = [
            pltpu.VMEM((32, count * half), bf16),
            pltpu.VMEM((6 * width, count * half), bf16),
        ]
        if first or last:
            scratch += [pltpu.SemaphoreType.DMA((4,)), pos_buf]
        if last:
            args += [norm, noise_var, rhs, block_count]
            specs += [VMEM] + [HBM] * 3
            outs = (shape((width, slots + LANES), f32), shape((width, slots), f32))
            scratch = [pltpu.VMEM(acc_shape.shape, f32)] + scratch
            scratch += [noise_buf, rhs_buf, count_buf]
        else:
            outs = (shape(parts[0].shape, f32),) if keep else ()
            outs += (acc_shape,)
            if first:
                outs += (rows_shape, shape((width, LANES), f32))
        kernel = functools.partial(pair_kernel, first, last, keep, taken, tiles)
        flops = 2 * slots * count * half * 64
        name = f"pairs_{count}"
        return call(kernel, outs, specs, (VMEM,) * len(outs), scratch, name, flops)(*args)

    distances = [blocks >> k for k in range(1, blocks.bit_length())]
    known, size = packet, 1
    rows = None
    for distance in distances[:-2]:
        arrived = exchanged(known, distance)
        fresh = (size // 2, size)
        if rows is None:
            known, acc, rows, norm = pairs([known], [fresh], keep=True)
        else:
            known, acc = pairs([known], [fresh], rows, acc, keep=True)
        known = jnp.concatenate([known, arrived], axis=1)
        size *= 2
    near = exchanged(known, distances[-2])
    far = exchanged(known, distances[-1])
    (acc,) = pairs([known], [(size // 2, size)], rows, acc)
    near, acc = lax.optimization_barrier((near, acc))
    rest = exchanged(near, distances[-1])
    (acc,) = pairs([near, far], [(0, size)] * 2, rows, acc)
    mine, direction = pairs([rest], [(0, size)], rows, acc, norm)
    other = exchanged(mine, 0)
    small = mine[:, slots:] + other[:, slots:]
    distance = blocks // 2
    while distance:
        small = small + exchanged(small, distance)
        distance //= 2

    return tuple(
        call(
            tail_kernel,
            (shape(rhs.shape, f32),) * 2,
            [VMEM] * 4,
            (VMEM, VMEM),
            [],
            "tail",
        )(small, mine, other, direction)
    )


def solution(mesh):
    return jax.shard_map(
        body,
        mesh=mesh,
        in_specs=(
            P(None, ("mocks", "blk")),
            P(("mocks", "blk")),
            P(None, ("mocks", "blk")),
            P(("mocks", "blk")),
        ),
        out_specs=(P(None, ("mocks", "blk")), P(None, ("mocks", "blk"))),
        check_vma=False,
    )
```

```python
import functools

import jax
import jax.numpy as jnp
from jax import lax
from jax.experimental import pallas as pl
from jax.experimental.pallas import tpu as pltpu
from jax.sharding import PartitionSpec as P

near_weight = 0.6
near_length = 40.0
far_weight = 0.4
far_length = 120.0
near_sq = near_length * near_length
far_sq = far_length * far_length
gap = far_sq - near_sq
scale = near_weight * near_sq + far_weight * far_sq
lift = near_weight * near_sq * gap / scale

LANES = 128
UNIT = 256
STEP = 2048
f32 = jnp.float32
bf16 = jnp.bfloat16
VMEM = pl.BlockSpec(memory_space=pltpu.VMEM)
HBM = pl.BlockSpec(memory_space=pltpu.HBM)
LIMIT = 24 * 2**20


def split3(x):
    top = x.astype(bf16).astype(f32)
    rest = x - top
    mid = rest.astype(bf16).astype(f32)
    return top, mid, rest - mid


def row_side(pos):
    width = pos.shape[1]
    one, none = jnp.ones((1, width), f32), jnp.zeros((1, width), f32)
    top, mid, low = split3(pos)
    square = split3(jnp.sum(pos * pos, axis=0, keepdims=True) + near_sq)
    a = jnp.concatenate([top, one, mid, none], axis=0)
    b = jnp.concatenate([top, one, low, none], axis=0)
    c = jnp.concatenate([*square, *[none] * 5], axis=0)
    return jnp.concatenate([a, b, a, c], axis=0).astype(bf16)


def column_sides(group):
    row = lax.broadcasted_iota(jnp.int32, group.shape, 0)
    fourth = row % 4 == 3
    upper = row < 4
    square = group * group
    square = sum(pltpu.roll(square, k, 0) for k in (1, 2, 3))
    scaled = jnp.where(fourth, square, -2.0 * group)
    ahead = split3(scaled)
    swapped = [pltpu.roll(x, 4, 0) for x in ahead]
    tail = jnp.where(upper, 1.0, 0.0)
    sides = []
    for (t, m, w), (tt, mm, _) in ((ahead, swapped), (swapped, ahead)):
        pairs = [(t, tt), (m, tt), (w, mm)]
        rows = [jnp.where(upper, x, y) for x, y in pairs] + [tail]
        sides.append(jnp.concatenate(rows, axis=0).astype(bf16))
    inverse = jnp.where(square > 0.0, lax.rsqrt(square), 0.0)
    return sides, inverse


def unit_of(pos):
    square = jnp.sum(pos * pos, axis=0, keepdims=True)
    return pos * jnp.where(square > 0.0, lax.rsqrt(square), 0.0)


def gram(left, right, first):
    width, slots = left.shape
    lane = lax.broadcasted_iota(jnp.int32, (width, LANES), 1)
    out = jnp.zeros((width, LANES), f32)
    for s in range(width):
        product = left * right[s : s + 1]
        folded = sum(product[:, t : t + LANES] for t in range(0, slots, LANES))
        out = jnp.where(lane == first + s, jnp.sum(folded, axis=1, keepdims=True), out)
    return out


def pack_kernel(pos_hbm, rhs_hbm, count_hbm, out, pos, rhs, count, sems):
    copies = [
        pltpu.make_async_copy(pos_hbm, pos, sems.at[0]),
        pltpu.make_async_copy(rhs_hbm, rhs, sems.at[1]),
        pltpu.make_async_copy(count_hbm, count, sems.at[2]),
    ]
    for copy in copies:
        copy.start()
    for copy in copies:
        copy.wait()
    width, slots = rhs.shape
    tiles = slots // LANES // 2
    side = (lax.axis_index("offs") + lax.axis_index("blk")) % 2
    odd = side == 1
    n = count[0]
    lane = lax.broadcasted_iota(jnp.int32, (1, LANES), 1)
    held = jnp.clip((n + LANES - 1 - side * LANES + LANES) // (2 * LANES), 0, tiles)
    held = jnp.full((1, LANES), held.astype(f32))
    for t in range(tiles):
        even_at = slice(2 * t * LANES, (2 * t + 1) * LANES)
        odd_at = slice((2 * t + 1) * LANES, (2 * t + 2) * LANES)
        first = (2 * t + side) * LANES
        value = jnp.where(odd, rhs[:, odd_at], rhs[:, even_at])
        out[:, t * LANES : (t + 1) * LANES] = jnp.where(first + lane < n, value, 0.0)
        place = jnp.where(odd, pos[:, odd_at], pos[:, even_at])
        at = (tiles + t // 2) * LANES
        row = (t % 2) * 4
        out[row : row + 4, at : at + LANES] = jnp.concatenate([place, held], axis=0)


def pair_kernel(first, last, keep, taken, tiles, *refs):
    refs = list(refs)
    packets = [refs.pop(0) for _ in taken]
    packet = packets[0]
    if first or last:
        pos_hbm = refs.pop(0)
    if not first:
        rows_in, acc_in = refs.pop(0), refs.pop(0)
    if last:
        norm = refs.pop(0)
        noise_hbm, rhs_hbm, count_hbm = (refs.pop(0) for _ in range(3))
        out, direction_out = refs.pop(0), refs.pop(0)
        acc = refs.pop(0)
    else:
        known_out = refs.pop(0) if keep else None
        acc = refs.pop(0)
        rows_ref = refs.pop(0) if first else rows_in
        if first:
            norm = refs.pop(0)
    if last:
        rows_ref = rows_in
    cols, weights = refs.pop(0), refs.pop(0)
    copies = []
    if first or last:
        sems, pos = refs.pop(0), refs.pop(0)
        copies.append(pltpu.make_async_copy(pos_hbm, pos, sems.at[0]))
    if last:
        noise, rhs, count = (refs.pop(0) for _ in range(3))
        copies += [
            pltpu.make_async_copy(noise_hbm, noise, sems.at[1]),
            pltpu.make_async_copy(rhs_hbm, rhs, sems.at[2]),
            pltpu.make_async_copy(count_hbm, count, sems.at[3]),
        ]
    for copy in copies:
        copy.start()
    if keep:
        known_out[...] = packet[...]

    width = packet.shape[0]
    half = tiles * LANES
    stride = half + half // 2
    filled = jnp.int32(0)
    listed = [(ref, b) for ref, (i, j) in zip(packets, taken) for b in range(i, j)]
    for packet, b in listed:
        base = b * stride
        for t in range(tiles):
            if t % 2 == 0:
                at = base + half + (t // 2) * LANES
                group = packet[:, at : at + LANES]
                sides, inverse = column_sides(group)
            v = packet[:, base + t * LANES : base + (t + 1) * LANES]
            row = (t % 2) * 4
            v = v * inverse[row + 3 : row + 4]
            rows = []
            for k in range(3):
                product = group[row + k : row + k + 1] * v
                top = product.astype(bf16).astype(f32)
                rows += [top, product - top]
            at = pl.ds(pl.multiple_of(filled + t * LANES, LANES), LANES)
            cols[:, at] = sides[t % 2]
            weights[:, at] = jnp.concatenate(rows, axis=0).astype(bf16)
        held = jnp.max(packet[3:4, base + half : base + half + LANES])
        filled = filled + held.astype(jnp.int32) * LANES

    slots = acc.shape[1]
    if first:
        copies[0].wait()
        rows_ref[...] = row_side(pos[...])
        norm[...] = gram(packets[0][:, :half], packets[0][:, :half], width)
        acc[...] = jnp.zeros(acc.shape, f32)
    else:
        acc[...] = acc_in[...]

    def step(begin, size):
        at = pl.ds(pl.multiple_of(begin, LANES), size)
        side, w = cols[:, at], weights[:, at]
        for r in range(0, slots, UNIT):
            near = slice(r, r + UNIT)
            u = lax.dot_general(
                side,
                rows_ref[:, near],
                (((0,), (0,)), ((), ())),
                preferred_element_type=f32,
            )
            u = jnp.maximum(u, near_sq)
            value = (u + lift) * pl.reciprocal(u * (u + gap), approx=True)
            top = value.astype(bf16)
            low = (value - top.astype(f32)).astype(bf16)
            part = acc[:, near] + jnp.dot(w, top, preferred_element_type=f32)
            acc[:, near] = part + jnp.dot(w, low, preferred_element_type=f32)

    full = min(STEP, len(listed) * half)
    steps = filled // full
    rest = filled - steps * full

    @pl.loop(0, steps)
    def _(i):
        step(i * full, full)

    for size in range(LANES, full, LANES):

        @pl.when(rest == size)
        def _(size=size):
            step(steps * full, size)

    if not last:
        return
    for copy in copies:
        copy.wait()
    lane = lax.broadcasted_iota(jnp.int32, (1, slots), 1)
    live = (lane < count[0]).astype(f32)
    unit = unit_of(pos[...]) * (live * scale)
    image = jnp.zeros((width, slots), f32)
    for k in range(3):
        at = 2 * k * width
        pulled = acc[at : at + width] + acc[at + width : at + 2 * width]
        image += unit[k : k + 1] * pulled
    direction = rhs[...] * live
    direction_out[...] = direction
    mine = (lax.axis_index("offs") == 0).astype(f32)
    noise_row = noise[...].reshape(1, slots)
    image = image + (mine * noise_row * live) * direction
    out[:, :slots] = image
    out[:, slots:] = norm[...] + gram(direction, image, 0)


def solved(small):
    width = small.shape[0]
    shape = small.shape
    c = [jnp.broadcast_to(small[:, j : j + 1], shape) for j in range(width)]
    r = [
        jnp.broadcast_to(small[:, j : j + 1], shape) for j in range(width, 2 * width)
    ]
    for k in range(width):
        inverse = pl.reciprocal(c[k], approx=True)[k : k + 1]
        ck, rk = c[k], r[k]
        for j in range(width):
            if j != k:
                factor = c[j][k : k + 1] * inverse
                c[j] = c[j] - ck * factor
                r[j] = r[j] - rk * factor
        c[k], r[k] = ck * inverse, rk * inverse
    return r


def combined(columns, x):
    parts = []
    for t in range(0, x.shape[1], LANES):
        tile = x[:, t : t + LANES]
        parts.append(sum(col * tile[m : m + 1] for m, col in enumerate(columns)))
    return jnp.concatenate(parts, axis=1)


def tail_kernel(small, mine, other, direction_ref, sol, res):
    columns = solved(small[...])
    direction = direction_ref[...]
    slots = direction.shape[1]
    image = mine[:, :slots] + other[:, :slots]
    sol[...] = combined(columns, direction)
    res[...] = direction - combined(columns, image)


def call(kernel, out_shape, in_specs, out_specs, scratch, name, flops=0):
    return pl.pallas_call(
        kernel,
        out_shape=out_shape,
        in_specs=in_specs,
        out_specs=out_specs,
        scratch_shapes=scratch,
        compiler_params=pltpu.CompilerParams(vmem_limit_bytes=LIMIT),
        cost_estimate=pl.CostEstimate(
            flops=flops, bytes_accessed=1 << 17, transcendentals=0
        ),
        name=name,
    )


def exchanged(block, distance):
    blocks, sides = lax.axis_size("blk"), lax.axis_size("offs")
    route = [
        ((b ^ distance) * sides + sides - 1 - c, b * sides + c)
        for b in range(blocks)
        for c in range(sides)
    ]
    return lax.ppermute(block, ("blk", "offs"), route)


def body(position, noise_var, rhs, block_count):
    width, slots = rhs.shape
    blocks = lax.axis_size("blk")
    tiles = slots // LANES // 2
    half = tiles * LANES
    shape = jax.ShapeDtypeStruct
    pos_buf = pltpu.VMEM(position.shape, f32)
    rhs_buf = pltpu.VMEM(rhs.shape, f32)
    noise_buf = pltpu.VMEM(noise_var.shape, f32)
    count_buf = pltpu.SMEM((1,), jnp.int32)

    packet = call(
        pack_kernel,
        shape((width, half + half // 2), f32),
        [HBM, HBM, HBM],
        VMEM,
        [pos_buf, rhs_buf, count_buf, pltpu.SemaphoreType.DMA((3,))],
        "pack",
    )(*(pltpu.with_memory_space_constraint(x, pltpu.HBM) for x in (position, rhs)), block_count)

    acc_shape = shape((6 * width, slots), f32)
    rows_shape = shape((32, slots), bf16)

    def pairs(parts, taken, rows=None, acc=None, norm=None, keep=False):
        first, last = rows is None, norm is not None
        args, specs = list(parts), [VMEM] * len(parts)
        if first or last:
            args.append(position)
            specs.append(HBM)
        if not first:
            args += [rows, acc]
            specs += [VMEM] * 2
        count = sum(stop - start for start, stop in taken)
        scratch = [
            pltpu.VMEM((32, count * half), bf16),
            pltpu.VMEM((6 * width, count * half), bf16),
        ]
        if first or last:
            scratch += [pltpu.SemaphoreType.DMA((4,)), pos_buf]
        if last:
            args += [norm, noise_var, rhs, block_count]
            specs += [VMEM] + [HBM] * 3
            outs = (shape((width, slots + LANES), f32), shape((width, slots), f32))
            scratch = [pltpu.VMEM(acc_shape.shape, f32)] + scratch
            scratch += [noise_buf, rhs_buf, count_buf]
        else:
            outs = (shape(parts[0].shape, f32),) if keep else ()
            outs += (acc_shape,)
            if first:
                outs += (rows_shape, shape((width, LANES), f32))
        kernel = functools.partial(pair_kernel, first, last, keep, taken, tiles)
        flops = 2 * slots * count * half * 64
        name = f"pairs_{count}"
        return call(kernel, outs, specs, (VMEM,) * len(outs), scratch, name, flops)(*args)

    distances = [blocks >> k for k in range(1, blocks.bit_length())]
    known, size = packet, 1
    rows = None
    for distance in distances[:-2]:
        arrived = exchanged(known, distance)
        fresh = (size // 2, size)
        if rows is None:
            known, acc, rows, norm = pairs([known], [fresh], keep=True)
        else:
            known, acc = pairs([known], [fresh], rows, acc, keep=True)
        known = jnp.concatenate([known, arrived], axis=1)
        size *= 2
    near = exchanged(known, distances[-2])
    far = exchanged(known, distances[-1])
    (acc,) = pairs([known], [(size // 2, size)], rows, acc)
    near, acc = lax.optimization_barrier((near, acc))
    rest = exchanged(near, distances[-1])
    (acc,) = pairs([near, far], [(0, size)] * 2, rows, acc)
    mine, direction = pairs([rest], [(0, size)], rows, acc, norm)
    other = exchanged(mine, 0)
    small = mine[:, slots:] + other[:, slots:]
    distance = blocks // 2
    while distance:
        small = small + exchanged(small, distance)
        distance //= 2

    return tuple(
        call(
            tail_kernel,
            (shape(rhs.shape, f32),) * 2,
            [VMEM] * 4,
            (VMEM, VMEM),
            [],
            "tail",
        )(small, mine, other, direction)
    )


def solution(mesh):
    return jax.shard_map(
        body,
        mesh=mesh,
        in_specs=(
            P(None, ("mocks", "blk")),
            P(("mocks", "blk")),
            P(None, ("mocks", "blk")),
            P(("mocks", "blk")),
        ),
        out_specs=(P(None, ("mocks", "blk")), P(None, ("mocks", "blk"))),
        check_vma=False,
    )
```

```python
import functools

import jax
import jax.numpy as jnp
from jax import lax
from jax.experimental import pallas as pl
from jax.experimental.pallas import tpu as pltpu
from jax.sharding import PartitionSpec as P

near_weight = 0.6
near_length = 40.0
far_weight = 0.4
far_length = 120.0
near_sq = near_length * near_length
far_sq = far_length * far_length
gap = far_sq - near_sq
scale = near_weight * near_sq + far_weight * far_sq
lift = near_weight * near_sq * gap / scale

LANES = 128
UNIT = 256
STEP = 1024
f32 = jnp.float32
bf16 = jnp.bfloat16
VMEM = pl.BlockSpec(memory_space=pltpu.VMEM)
HBM = pl.BlockSpec(memory_space=pltpu.HBM)
LIMIT = 24 * 2**20


def split3(x):
    top = x.astype(bf16).astype(f32)
    rest = x - top
    mid = rest.astype(bf16).astype(f32)
    return top, mid, rest - mid


def row_side(pos):
    width = pos.shape[1]
    one, none = jnp.ones((1, width), f32), jnp.zeros((1, width), f32)
    top, mid, low = split3(pos)
    square = split3(jnp.sum(pos * pos, axis=0, keepdims=True) + near_sq)
    a = jnp.concatenate([top, one, mid, none], axis=0)
    b = jnp.concatenate([top, one, low, none], axis=0)
    c = jnp.concatenate([*square, *[none] * 5], axis=0)
    return jnp.concatenate([a, b, a, c], axis=0).astype(bf16)


def column_sides(group):
    row = lax.broadcasted_iota(jnp.int32, group.shape, 0)
    fourth = row % 4 == 3
    upper = row < 4
    square = group * group
    square = sum(pltpu.roll(square, k, 0) for k in (1, 2, 3))
    scaled = jnp.where(fourth, square, -2.0 * group)
    ahead = split3(scaled)
    swapped = [pltpu.roll(x, 4, 0) for x in ahead]
    tail = jnp.where(upper, 1.0, 0.0)
    sides = []
    for (t, m, w), (tt, mm, _) in ((ahead, swapped), (swapped, ahead)):
        pairs = [(t, tt), (m, tt), (w, mm)]
        rows = [jnp.where(upper, x, y) for x, y in pairs] + [tail]
        sides.append(jnp.concatenate(rows, axis=0).astype(bf16))
    inverse = jnp.where(square > 0.0, lax.rsqrt(square), 0.0)
    return sides, inverse


def unit_of(pos):
    square = jnp.sum(pos * pos, axis=0, keepdims=True)
    return pos * jnp.where(square > 0.0, lax.rsqrt(square), 0.0)


def gram(left, right, first):
    width, slots = left.shape
    lane = lax.broadcasted_iota(jnp.int32, (width, LANES), 1)
    out = jnp.zeros((width, LANES), f32)
    for s in range(width):
        product = left * right[s : s + 1]
        folded = sum(product[:, t : t + LANES] for t in range(0, slots, LANES))
        out = jnp.where(lane == first + s, jnp.sum(folded, axis=1, keepdims=True), out)
    return out


def first_kernel(out):
    out[...] = jnp.zeros(out.shape, jnp.int32)


def count_kernel(count, first, out):
    out[...] = jnp.full(out.shape, count[0], jnp.int32) + first[...]


def pack_kernel(pos, rhs, count, out):
    width, slots = rhs.shape
    tiles = slots // LANES // 2
    side = (lax.axis_index("offs") + lax.axis_index("blk")) % 2
    odd = side == 1
    n = count[...]
    lane = lax.broadcasted_iota(jnp.int32, (1, LANES), 1)
    held = jnp.clip((n + LANES - 1 - side * LANES + LANES) // (2 * LANES), 0, tiles)
    held = held.astype(f32)
    for t in range(tiles):
        even_at = slice(2 * t * LANES, (2 * t + 1) * LANES)
        odd_at = slice((2 * t + 1) * LANES, (2 * t + 2) * LANES)
        first = (2 * t + side) * LANES
        value = jnp.where(odd, rhs[:, odd_at], rhs[:, even_at])
        out[:, t * LANES : (t + 1) * LANES] = jnp.where(first + lane < n, value, 0.0)
        place = jnp.where(odd, pos[:, odd_at], pos[:, even_at])
        at = (tiles + t // 2) * LANES
        row = (t % 2) * 4
        out[row : row + 4, at : at + LANES] = jnp.concatenate([place, held], axis=0)


def pair_kernel(first, last, keep, taken, tiles, *refs):
    refs = list(refs)
    packets = [refs.pop(0) for _ in taken]
    packet = packets[0]
    if first or last:
        pos_hbm = refs.pop(0)
    if not first:
        rows_in, acc_in = refs.pop(0), refs.pop(0)
    if last:
        norm = refs.pop(0)
        noise_hbm, rhs_hbm, count_hbm = (refs.pop(0) for _ in range(3))
        out, direction_out = refs.pop(0), refs.pop(0)
        acc = refs.pop(0)
    else:
        known_out = refs.pop(0) if keep else None
        acc = refs.pop(0)
        rows_ref = refs.pop(0) if first else rows_in
        if first:
            norm = refs.pop(0)
    if last:
        rows_ref = rows_in
    cols, weights = refs.pop(0), refs.pop(0)
    copies = []
    if first or last:
        sems, pos = refs.pop(0), refs.pop(0)
        copies.append(pltpu.make_async_copy(pos_hbm, pos, sems.at[0]))
    if last:
        noise, rhs, count = (refs.pop(0) for _ in range(3))
        copies += [
            pltpu.make_async_copy(noise_hbm, noise, sems.at[1]),
            pltpu.make_async_copy(rhs_hbm, rhs, sems.at[2]),
            pltpu.make_async_copy(count_hbm, count, sems.at[3]),
        ]
    for copy in copies:
        copy.start()
    if keep:
        known_out[...] = packet[...]

    width = packet.shape[0]
    half = tiles * LANES
    stride = half + half // 2
    filled = jnp.int32(0)
    listed = [(ref, b) for ref, (i, j) in zip(packets, taken) for b in range(i, j)]
    for packet, b in listed:
        base = b * stride
        for t in range(tiles):
            if t % 2 == 0:
                at = base + half + (t // 2) * LANES
                group = packet[:, at : at + LANES]
                sides, inverse = column_sides(group)
            v = packet[:, base + t * LANES : base + (t + 1) * LANES]
            row = (t % 2) * 4
            v = v * inverse[row + 3 : row + 4]
            rows = []
            for k in range(3):
                product = group[row + k : row + k + 1] * v
                top = product.astype(bf16).astype(f32)
                rows += [top, product - top]
            at = pl.ds(pl.multiple_of(filled + t * LANES, LANES), LANES)
            cols[:, at] = sides[t % 2]
            weights[:, at] = jnp.concatenate(rows, axis=0).astype(bf16)
        held = jnp.max(packet[3:4, base + half : base + half + LANES])
        filled = filled + held.astype(jnp.int32) * LANES

    slots = acc.shape[1]
    if first:
        copies[0].wait()
        rows_ref[...] = row_side(pos[...])
        norm[...] = gram(packets[0][:, :half], packets[0][:, :half], width)
        acc[...] = jnp.zeros(acc.shape, f32)
    else:
        acc[...] = acc_in[...]

    def step(begin, size):
        at = pl.ds(pl.multiple_of(begin, LANES), size)
        side, w = cols[:, at], weights[:, at]
        for r in range(0, slots, UNIT):
            near = slice(r, r + UNIT)
            u = lax.dot_general(
                side,
                rows_ref[:, near],
                (((0,), (0,)), ((), ())),
                preferred_element_type=f32,
            )
            u = jnp.maximum(u, near_sq)
            value = (u + lift) * pl.reciprocal(u * (u + gap), approx=True)
            top = value.astype(bf16)
            low = (value - top.astype(f32)).astype(bf16)
            part = acc[:, near] + jnp.dot(w, top, preferred_element_type=f32)
            acc[:, near] = part + jnp.dot(w, low, preferred_element_type=f32)

    full = min(STEP, len(listed) * half)
    steps = filled // full
    rest = filled - steps * full

    @pl.loop(0, steps)
    def _(i):
        step(i * full, full)

    for size in range(LANES, full, LANES):

        @pl.when(rest == size)
        def _(size=size):
            step(steps * full, size)

    if not last:
        return
    for copy in copies:
        copy.wait()
    lane = lax.broadcasted_iota(jnp.int32, (1, slots), 1)
    live = (lane < count[0]).astype(f32)
    unit = unit_of(pos[...]) * (live * scale)
    image = jnp.zeros((width, slots), f32)
    for k in range(3):
        at = 2 * k * width
        pulled = acc[at : at + width] + acc[at + width : at + 2 * width]
        image += unit[k : k + 1] * pulled
    direction = rhs[...] * live
    direction_out[...] = direction
    mine = (lax.axis_index("offs") == 0).astype(f32)
    noise_row = noise[...].reshape(1, slots)
    image = image + (mine * noise_row * live) * direction
    out[:, :slots] = image
    out[:, slots:] = norm[...] + gram(direction, image, 0)


def solved(small):
    width = small.shape[0]
    shape = small.shape
    c = [jnp.broadcast_to(small[:, j : j + 1], shape) for j in range(width)]
    r = [
        jnp.broadcast_to(small[:, j : j + 1], shape) for j in range(width, 2 * width)
    ]
    for k in range(width):
        inverse = pl.reciprocal(c[k], approx=True)[k : k + 1]
        ck, rk = c[k], r[k]
        for j in range(width):
            if j != k:
                factor = c[j][k : k + 1] * inverse
                c[j] = c[j] - ck * factor
                r[j] = r[j] - rk * factor
        c[k], r[k] = ck * inverse, rk * inverse
    return r


def combined(columns, x):
    parts = []
    for t in range(0, x.shape[1], LANES):
        tile = x[:, t : t + LANES]
        parts.append(sum(col * tile[m : m + 1] for m, col in enumerate(columns)))
    return jnp.concatenate(parts, axis=1)


def tail_kernel(small, mine, other, direction_ref, sol, res):
    columns = solved(small[...])
    direction = direction_ref[...]
    slots = direction.shape[1]
    image = mine[:, :slots] + other[:, :slots]
    sol[...] = combined(columns, direction)
    res[...] = direction - combined(columns, image)


def call(kernel, out_shape, in_specs, out_specs, scratch, name, flops=0):
    return pl.pallas_call(
        kernel,
        out_shape=out_shape,
        in_specs=in_specs,
        out_specs=out_specs,
        scratch_shapes=scratch,
        compiler_params=pltpu.CompilerParams(vmem_limit_bytes=LIMIT),
        cost_estimate=pl.CostEstimate(
            flops=flops, bytes_accessed=1 << 17, transcendentals=0
        ),
        name=name,
    )


def exchanged(block, distance):
    blocks, sides = lax.axis_size("blk"), lax.axis_size("offs")
    route = [
        ((b ^ distance) * sides + sides - 1 - c, b * sides + c)
        for b in range(blocks)
        for c in range(sides)
    ]
    return lax.ppermute(block, ("blk", "offs"), route)


def body(position, noise_var, rhs, block_count):
    width, slots = rhs.shape
    blocks = lax.axis_size("blk")
    tiles = slots // LANES // 2
    half = tiles * LANES
    shape = jax.ShapeDtypeStruct
    pos_buf = pltpu.VMEM(position.shape, f32)
    rhs_buf = pltpu.VMEM(rhs.shape, f32)
    noise_buf = pltpu.VMEM(noise_var.shape, f32)
    count_buf = pltpu.SMEM((1,), jnp.int32)

    first = call(
        first_kernel, shape((1, LANES), jnp.int32), [], VMEM, [], "first", 1 << 30
    )()
    block_count, first = lax.optimization_barrier((block_count, first))
    counted = call(
        count_kernel,
        shape((1, LANES), jnp.int32),
        [pl.BlockSpec(memory_space=pltpu.SMEM), VMEM],
        VMEM,
        [],
        "count",
        0,
    )(block_count, first)
    packet = call(
        pack_kernel,
        shape((width, half + half // 2), f32),
        [VMEM] * 3,
        VMEM,
        [],
        "pack",
    )(position, rhs, counted)

    acc_shape = shape((6 * width, slots), f32)
    rows_shape = shape((32, slots), bf16)

    def pairs(parts, taken, rows=None, acc=None, norm=None, keep=False):
        first, last = rows is None, norm is not None
        args, specs = list(parts), [VMEM] * len(parts)
        if first or last:
            args.append(position)
            specs.append(HBM)
        if not first:
            args += [rows, acc]
            specs += [VMEM] * 2
        count = sum(stop - start for start, stop in taken)
        scratch = [
            pltpu.VMEM((32, count * half), bf16),
            pltpu.VMEM((6 * width, count * half), bf16),
        ]
        if first or last:
            scratch += [pltpu.SemaphoreType.DMA((4,)), pos_buf]
        if last:
            args += [norm, noise_var, rhs, block_count]
            specs += [VMEM] + [HBM] * 3
            outs = (shape((width, slots + LANES), f32), shape((width, slots), f32))
            scratch = [pltpu.VMEM(acc_shape.shape, f32)] + scratch
            scratch += [noise_buf, rhs_buf, count_buf]
        else:
            outs = (shape(parts[0].shape, f32),) if keep else ()
            outs += (acc_shape,)
            if first:
                outs += (rows_shape, shape((width, LANES), f32))
        kernel = functools.partial(pair_kernel, first, last, keep, taken, tiles)
        flops = 2 * slots * count * half * 64
        name = f"pairs_{count}"
        return call(kernel, outs, specs, (VMEM,) * len(outs), scratch, name, flops)(*args)

    distances = [blocks >> k for k in range(1, blocks.bit_length())]
    known, size = packet, 1
    rows = None
    for distance in distances[:-2]:
        arrived = exchanged(known, distance)
        fresh = (size // 2, size)
        if rows is None:
            known, acc, rows, norm = pairs([known], [fresh], keep=True)
        else:
            known, acc = pairs([known], [fresh], rows, acc, keep=True)
        known = jnp.concatenate([known, arrived], axis=1)
        size *= 2
    near = exchanged(known, distances[-2])
    far = exchanged(known, distances[-1])
    (acc,) = pairs([known], [(size // 2, size)], rows, acc)
    near, acc = lax.optimization_barrier((near, acc))
    rest = exchanged(near, distances[-1])
    (acc,) = pairs([near, far], [(0, size)] * 2, rows, acc)
    mine, direction = pairs([rest], [(0, size)], rows, acc, norm)
    other = exchanged(mine, 0)
    small = mine[:, slots:] + other[:, slots:]
    distance = blocks // 2
    while distance:
        small = small + exchanged(small, distance)
        distance //= 2

    return tuple(
        call(
            tail_kernel,
            (shape(rhs.shape, f32),) * 2,
            [VMEM] * 4,
            (VMEM, VMEM),
            [],
            "tail",
        )(small, mine, other, direction)
    )


def solution(mesh):
    return jax.shard_map(
        body,
        mesh=mesh,
        in_specs=(
            P(None, ("mocks", "blk")),
            P(("mocks", "blk")),
            P(None, ("mocks", "blk")),
            P(("mocks", "blk")),
        ),
        out_specs=(P(None, ("mocks", "blk")), P(None, ("mocks", "blk"))),
        check_vma=False,
    )
```

```python
import functools

import jax
import jax.numpy as jnp
from jax import lax
from jax.experimental import pallas as pl
from jax.experimental.pallas import tpu as pltpu
from jax.sharding import PartitionSpec as P

near_weight = 0.6
near_length = 40.0
far_weight = 0.4
far_length = 120.0
near_sq = near_length * near_length
far_sq = far_length * far_length
gap = far_sq - near_sq
scale = near_weight * near_sq + far_weight * far_sq
lift = near_weight * near_sq * gap / scale

LANES = 128
UNIT = 256
STEP = 1024
f32 = jnp.float32
bf16 = jnp.bfloat16
VMEM = pl.BlockSpec(memory_space=pltpu.VMEM)
HBM = pl.BlockSpec(memory_space=pltpu.HBM)
LIMIT = 24 * 2**20


def split3(x):
    top = x.astype(bf16).astype(f32)
    rest = x - top
    mid = rest.astype(bf16).astype(f32)
    return top, mid, rest - mid


def row_side(pos):
    width = pos.shape[1]
    one, none = jnp.ones((1, width), f32), jnp.zeros((1, width), f32)
    top, mid, low = split3(pos)
    square = split3(jnp.sum(pos * pos, axis=0, keepdims=True) + near_sq)
    a = jnp.concatenate([top, one, mid, none], axis=0)
    b = jnp.concatenate([top, one, low, none], axis=0)
    c = jnp.concatenate([*square, *[none] * 5], axis=0)
    return jnp.concatenate([a, b, a, c], axis=0).astype(bf16)


def column_sides(group):
    row = lax.broadcasted_iota(jnp.int32, group.shape, 0)
    fourth = row % 4 == 3
    upper = row < 4
    square = group * group
    square = sum(pltpu.roll(square, k, 0) for k in (1, 2, 3))
    scaled = jnp.where(fourth, square, -2.0 * group)
    ahead = split3(scaled)
    swapped = [pltpu.roll(x, 4, 0) for x in ahead]
    tail = jnp.where(upper, 1.0, 0.0)
    sides = []
    for (t, m, w), (tt, mm, _) in ((ahead, swapped), (swapped, ahead)):
        pairs = [(t, tt), (m, tt), (w, mm)]
        rows = [jnp.where(upper, x, y) for x, y in pairs] + [tail]
        sides.append(jnp.concatenate(rows, axis=0).astype(bf16))
    inverse = jnp.where(square > 0.0, lax.rsqrt(square), 0.0)
    return sides, inverse


def unit_of(pos):
    square = jnp.sum(pos * pos, axis=0, keepdims=True)
    return pos * jnp.where(square > 0.0, lax.rsqrt(square), 0.0)


def gram(left, right, first):
    width, slots = left.shape
    lane = lax.broadcasted_iota(jnp.int32, (width, LANES), 1)
    out = jnp.zeros((width, LANES), f32)
    for s in range(width):
        product = left * right[s : s + 1]
        folded = sum(product[:, t : t + LANES] for t in range(0, slots, LANES))
        out = jnp.where(lane == first + s, jnp.sum(folded, axis=1, keepdims=True), out)
    return out


def first_kernel(out):
    out[...] = jnp.zeros(out.shape, jnp.int32)


def count_kernel(count, first, out):
    out[...] = jnp.full(out.shape, count[0], jnp.int32) + first[...]


def pack_kernel(pos, rhs, count, out):
    width, slots = rhs.shape
    tiles = slots // LANES // 2
    side = (lax.axis_index("offs") + lax.axis_index("blk")) % 2
    odd = side == 1
    n = count[...]
    lane = lax.broadcasted_iota(jnp.int32, (1, LANES), 1)
    held = jnp.clip((n + LANES - 1 - side * LANES + LANES) // (2 * LANES), 0, tiles)
    held = held.astype(f32)
    for t in range(tiles):
        even_at = slice(2 * t * LANES, (2 * t + 1) * LANES)
        odd_at = slice((2 * t + 1) * LANES, (2 * t + 2) * LANES)
        first = (2 * t + side) * LANES
        value = jnp.where(odd, rhs[:, odd_at], rhs[:, even_at])
        out[:, t * LANES : (t + 1) * LANES] = jnp.where(first + lane < n, value, 0.0)
        place = jnp.where(odd, pos[:, odd_at], pos[:, even_at])
        at = (tiles + t // 2) * LANES
        row = (t % 2) * 4
        out[row : row + 4, at : at + LANES] = jnp.concatenate([place, held], axis=0)


def pair_kernel(first, last, keep, taken, tiles, *refs):
    refs = list(refs)
    packets = [refs.pop(0) for _ in taken]
    packet = packets[0]
    if first or last:
        pos_hbm = refs.pop(0)
    if not first:
        rows_in, acc_in = refs.pop(0), refs.pop(0)
    if last:
        norm = refs.pop(0)
        noise_hbm, rhs_hbm, count_hbm = (refs.pop(0) for _ in range(3))
        out, direction_out = refs.pop(0), refs.pop(0)
        acc = refs.pop(0)
    else:
        known_out = refs.pop(0) if keep else None
        acc = refs.pop(0)
        rows_ref = refs.pop(0) if first else rows_in
        if first:
            norm = refs.pop(0)
    if last:
        rows_ref = rows_in
    cols, weights = refs.pop(0), refs.pop(0)
    copies = []
    if first or last:
        sems, pos = refs.pop(0), refs.pop(0)
        copies.append(pltpu.make_async_copy(pos_hbm, pos, sems.at[0]))
    if last:
        noise, rhs, count = (refs.pop(0) for _ in range(3))
        copies += [
            pltpu.make_async_copy(noise_hbm, noise, sems.at[1]),
            pltpu.make_async_copy(rhs_hbm, rhs, sems.at[2]),
            pltpu.make_async_copy(count_hbm, count, sems.at[3]),
        ]
    for copy in copies:
        copy.start()
    if keep:
        known_out[...] = packet[...]

    width = packet.shape[0]
    half = tiles * LANES
    stride = half + half // 2
    filled = jnp.int32(0)
    listed = [(ref, b) for ref, (i, j) in zip(packets, taken) for b in range(i, j)]
    for packet, b in listed:
        base = b * stride
        for t in range(tiles):
            if t % 2 == 0:
                at = base + half + (t // 2) * LANES
                group = packet[:, at : at + LANES]
                sides, inverse = column_sides(group)
            v = packet[:, base + t * LANES : base + (t + 1) * LANES]
            row = (t % 2) * 4
            v = v * inverse[row + 3 : row + 4]
            rows = []
            for k in range(3):
                product = group[row + k : row + k + 1] * v
                top = product.astype(bf16).astype(f32)
                rows += [top, product - top]
            at = pl.ds(pl.multiple_of(filled + t * LANES, LANES), LANES)
            cols[:, at] = sides[t % 2]
            weights[:, at] = jnp.concatenate(rows, axis=0).astype(bf16)
        held = jnp.max(packet[3:4, base + half : base + half + LANES])
        filled = filled + held.astype(jnp.int32) * LANES

    slots = acc.shape[1]
    if first:
        copies[0].wait()
        rows_ref[...] = row_side(pos[...])
        norm[...] = gram(packets[0][:, :half], packets[0][:, :half], width)
        acc[...] = jnp.zeros(acc.shape, f32)
    else:
        acc[...] = acc_in[...]

    def step(begin, size):
        at = pl.ds(pl.multiple_of(begin, LANES), size)
        side, w = cols[:, at], weights[:, at]
        for r in range(0, slots, UNIT):
            near = slice(r, r + UNIT)
            u = lax.dot_general(
                side,
                rows_ref[:, near],
                (((0,), (0,)), ((), ())),
                preferred_element_type=f32,
            )
            u = jnp.maximum(u, near_sq)
            value = (u + lift) * pl.reciprocal(u * (u + gap), approx=True)
            top = value.astype(bf16)
            low = (value - top.astype(f32)).astype(bf16)
            part = acc[:, near] + jnp.dot(w, top, preferred_element_type=f32)
            acc[:, near] = part + jnp.dot(w, low, preferred_element_type=f32)

    full = min(STEP, len(listed) * half)
    steps = filled // full
    rest = filled - steps * full

    @pl.loop(0, steps)
    def _(i):
        step(i * full, full)

    begin, longest = steps * full, full
    if len(listed) * half > full:
        longest = full // 2
        more = rest >= longest

        @pl.when(more)
        def _(begin=begin):
            step(begin, longest)

        begin = jnp.where(more, begin + longest, begin)
        rest = jnp.where(more, rest - longest, rest)

    for size in range(LANES, longest, LANES):

        @pl.when(rest == size)
        def _(size=size, begin=begin):
            step(begin, size)

    if not last:
        return
    for copy in copies:
        copy.wait()
    lane = lax.broadcasted_iota(jnp.int32, (1, slots), 1)
    live = (lane < count[0]).astype(f32)
    unit = unit_of(pos[...]) * (live * scale)
    image = jnp.zeros((width, slots), f32)
    for k in range(3):
        at = 2 * k * width
        pulled = acc[at : at + width] + acc[at + width : at + 2 * width]
        image += unit[k : k + 1] * pulled
    direction = rhs[...] * live
    direction_out[...] = direction
    mine = (lax.axis_index("offs") == 0).astype(f32)
    noise_row = noise[...].reshape(1, slots)
    image = image + (mine * noise_row * live) * direction
    out[:, :slots] = image
    out[:, slots:] = norm[...] + gram(direction, image, 0)


def solved(small):
    width = small.shape[0]
    shape = small.shape
    c = [jnp.broadcast_to(small[:, j : j + 1], shape) for j in range(width)]
    r = [
        jnp.broadcast_to(small[:, j : j + 1], shape) for j in range(width, 2 * width)
    ]
    for k in range(width):
        inverse = pl.reciprocal(c[k], approx=True)[k : k + 1]
        ck, rk = c[k], r[k]
        for j in range(width):
            if j != k:
                factor = c[j][k : k + 1] * inverse
                c[j] = c[j] - ck * factor
                r[j] = r[j] - rk * factor
        c[k], r[k] = ck * inverse, rk * inverse
    return r


def combined(columns, x):
    parts = []
    for t in range(0, x.shape[1], LANES):
        tile = x[:, t : t + LANES]
        parts.append(sum(col * tile[m : m + 1] for m, col in enumerate(columns)))
    return jnp.concatenate(parts, axis=1)


def tail_kernel(small, mine, other, direction_ref, sol, res):
    columns = solved(small[...])
    direction = direction_ref[...]
    slots = direction.shape[1]
    image = mine[:, :slots] + other[:, :slots]
    sol[...] = combined(columns, direction)
    res[...] = direction - combined(columns, image)


def call(kernel, out_shape, in_specs, out_specs, scratch, name, flops=0):
    return pl.pallas_call(
        kernel,
        out_shape=out_shape,
        in_specs=in_specs,
        out_specs=out_specs,
        scratch_shapes=scratch,
        compiler_params=pltpu.CompilerParams(vmem_limit_bytes=LIMIT),
        cost_estimate=pl.CostEstimate(
            flops=flops, bytes_accessed=1 << 17, transcendentals=0
        ),
        name=name,
    )


def exchanged(block, distance):
    blocks, sides = lax.axis_size("blk"), lax.axis_size("offs")
    route = [
        ((b ^ distance) * sides + sides - 1 - c, b * sides + c)
        for b in range(blocks)
        for c in range(sides)
    ]
    return lax.ppermute(block, ("blk", "offs"), route)


def body(position, noise_var, rhs, block_count):
    width, slots = rhs.shape
    blocks = lax.axis_size("blk")
    tiles = slots // LANES // 2
    half = tiles * LANES
    shape = jax.ShapeDtypeStruct
    pos_buf = pltpu.VMEM(position.shape, f32)
    rhs_buf = pltpu.VMEM(rhs.shape, f32)
    noise_buf = pltpu.VMEM(noise_var.shape, f32)
    count_buf = pltpu.SMEM((1,), jnp.int32)

    first = call(
        first_kernel, shape((1, LANES), jnp.int32), [], VMEM, [], "first", 1 << 30
    )()
    block_count, first = lax.optimization_barrier((block_count, first))
    counted = call(
        count_kernel,
        shape((1, LANES), jnp.int32),
        [pl.BlockSpec(memory_space=pltpu.SMEM), VMEM],
        VMEM,
        [],
        "count",
        0,
    )(block_count, first)
    packet = call(
        pack_kernel,
        shape((width, half + half // 2), f32),
        [VMEM] * 3,
        VMEM,
        [],
        "pack",
    )(position, rhs, counted)

    acc_shape = shape((6 * width, slots), f32)
    rows_shape = shape((32, slots), bf16)

    def pairs(parts, taken, rows=None, acc=None, norm=None, keep=False):
        first, last = rows is None, norm is not None
        args, specs = list(parts), [VMEM] * len(parts)
        if first or last:
            args.append(position)
            specs.append(HBM)
        if not first:
            args += [rows, acc]
            specs += [VMEM] * 2
        count = sum(stop - start for start, stop in taken)
        scratch = [
            pltpu.VMEM((32, count * half), bf16),
            pltpu.VMEM((6 * width, count * half), bf16),
        ]
        if first or last:
            scratch += [pltpu.SemaphoreType.DMA((4,)), pos_buf]
        if last:
            args += [norm, noise_var, rhs, block_count]
            specs += [VMEM] + [HBM] * 3
            outs = (shape((width, slots + LANES), f32), shape((width, slots), f32))
            scratch = [pltpu.VMEM(acc_shape.shape, f32)] + scratch
            scratch += [noise_buf, rhs_buf, count_buf]
        else:
            outs = (shape(parts[0].shape, f32),) if keep else ()
            outs += (acc_shape,)
            if first:
                outs += (rows_shape, shape((width, LANES), f32))
        kernel = functools.partial(pair_kernel, first, last, keep, taken, tiles)
        flops = 2 * slots * count * half * 64
        name = f"pairs_{count}"
        return call(kernel, outs, specs, (VMEM,) * len(outs), scratch, name, flops)(*args)

    distances = [blocks >> k for k in range(1, blocks.bit_length())]
    known, size = packet, 1
    rows = None
    for distance in distances[:-2]:
        arrived = exchanged(known, distance)
        fresh = (size // 2, size)
        if rows is None:
            known, acc, rows, norm = pairs([known], [fresh], keep=True)
        else:
            known, acc = pairs([known], [fresh], rows, acc, keep=True)
        known = jnp.concatenate([known, arrived], axis=1)
        size *= 2
    near = exchanged(known, distances[-2])
    far = exchanged(known, distances[-1])
    (acc,) = pairs([known], [(size // 2, size)], rows, acc)
    near, acc = lax.optimization_barrier((near, acc))
    rest = exchanged(near, distances[-1])
    (acc,) = pairs([near, far], [(0, size)] * 2, rows, acc)
    mine, direction = pairs([rest], [(0, size)], rows, acc, norm)
    other = exchanged(mine, 0)
    small = mine[:, slots:] + other[:, slots:]
    distance = blocks // 2
    while distance:
        small = small + exchanged(small, distance)
        distance //= 2

    return tuple(
        call(
            tail_kernel,
            (shape(rhs.shape, f32),) * 2,
            [VMEM] * 4,
            (VMEM, VMEM),
            [],
            "tail",
        )(small, mine, other, direction)
    )


def solution(mesh):
    return jax.shard_map(
        body,
        mesh=mesh,
        in_specs=(
            P(None, ("mocks", "blk")),
            P(("mocks", "blk")),
            P(None, ("mocks", "blk")),
            P(("mocks", "blk")),
        ),
        out_specs=(P(None, ("mocks", "blk")), P(None, ("mocks", "blk"))),
        check_vma=False,
    )
```

```python
import functools

import jax
import jax.numpy as jnp
from jax import lax
from jax.experimental import pallas as pl
from jax.experimental.pallas import tpu as pltpu
from jax.sharding import PartitionSpec as P

near_weight = 0.6
near_length = 40.0
far_weight = 0.4
far_length = 120.0
near_sq = near_length * near_length
far_sq = far_length * far_length
gap = far_sq - near_sq
scale = near_weight * near_sq + far_weight * far_sq
lift = near_weight * near_sq * gap / scale

LANES = 128
UNIT = 256
STEP = 1024
f32 = jnp.float32
bf16 = jnp.bfloat16
VMEM = pl.BlockSpec(memory_space=pltpu.VMEM)
HBM = pl.BlockSpec(memory_space=pltpu.HBM)
LIMIT = 24 * 2**20


def split3(x):
    top = x.astype(bf16).astype(f32)
    rest = x - top
    mid = rest.astype(bf16).astype(f32)
    return top, mid, rest - mid


def row_side(pos):
    width = pos.shape[1]
    one, none = jnp.ones((1, width), f32), jnp.zeros((1, width), f32)
    top, mid, low = split3(pos)
    square = split3(jnp.sum(pos * pos, axis=0, keepdims=True) + near_sq)
    a = jnp.concatenate([top, one, mid, none], axis=0)
    b = jnp.concatenate([top, one, low, none], axis=0)
    c = jnp.concatenate([*square, *[none] * 5], axis=0)
    return jnp.concatenate([a, b, a, c], axis=0).astype(bf16)


def column_sides(group):
    row = lax.broadcasted_iota(jnp.int32, group.shape, 0)
    fourth = row % 4 == 3
    upper = row < 4
    square = group * group
    square = sum(pltpu.roll(square, k, 0) for k in (1, 2, 3))
    scaled = jnp.where(fourth, square, -2.0 * group)
    ahead = split3(scaled)
    swapped = [pltpu.roll(x, 4, 0) for x in ahead]
    tail = jnp.where(upper, 1.0, 0.0)
    sides = []
    for (t, m, w), (tt, mm, _) in ((ahead, swapped), (swapped, ahead)):
        pairs = [(t, tt), (m, tt), (w, mm)]
        rows = [jnp.where(upper, x, y) for x, y in pairs] + [tail]
        sides.append(jnp.concatenate(rows, axis=0).astype(bf16))
    inverse = jnp.where(square > 0.0, lax.rsqrt(square), 0.0)
    return sides, inverse


def unit_of(pos):
    square = jnp.sum(pos * pos, axis=0, keepdims=True)
    return pos * jnp.where(square > 0.0, lax.rsqrt(square), 0.0)


def gram(left, right, first):
    width, slots = left.shape
    lane = lax.broadcasted_iota(jnp.int32, (width, LANES), 1)
    out = jnp.zeros((width, LANES), f32)
    for s in range(width):
        product = left * right[s : s + 1]
        folded = sum(product[:, t : t + LANES] for t in range(0, slots, LANES))
        out = jnp.where(lane == first + s, jnp.sum(folded, axis=1, keepdims=True), out)
    return out


def first_kernel(out):
    out[...] = jnp.zeros(out.shape, jnp.int32)


def count_kernel(count, first, out):
    out[...] = jnp.full(out.shape, count[0], jnp.int32) + first[...]


def pack_kernel(pos, rhs, count, out):
    width, slots = rhs.shape
    tiles = slots // LANES // 2
    side = (lax.axis_index("offs") + lax.axis_index("blk")) % 2
    odd = side == 1
    n = count[...]
    lane = lax.broadcasted_iota(jnp.int32, (1, LANES), 1)
    held = jnp.clip((n + LANES - 1 - side * LANES + LANES) // (2 * LANES), 0, tiles)
    held = held.astype(f32)
    for t in range(tiles):
        even_at = slice(2 * t * LANES, (2 * t + 1) * LANES)
        odd_at = slice((2 * t + 1) * LANES, (2 * t + 2) * LANES)
        first = (2 * t + side) * LANES
        value = jnp.where(odd, rhs[:, odd_at], rhs[:, even_at])
        out[:, t * LANES : (t + 1) * LANES] = jnp.where(first + lane < n, value, 0.0)
        place = jnp.where(odd, pos[:, odd_at], pos[:, even_at])
        at = (tiles + t // 2) * LANES
        row = (t % 2) * 4
        out[row : row + 4, at : at + LANES] = jnp.concatenate([place, held], axis=0)


def pair_kernel(first, last, keep, taken, tiles, *refs):
    refs = list(refs)
    packets = [refs.pop(0) for _ in taken]
    packet = packets[0]
    if first:
        hbm = [refs.pop(0) for _ in range(4)]
    else:
        rows_ref, acc_in = refs.pop(0), refs.pop(0)
    if last:
        norm, lead, direction_ref, own = (refs.pop(0) for _ in range(4))
        out, acc = refs.pop(0), refs.pop(0)
    else:
        known_out = refs.pop(0) if keep else None
        acc = refs.pop(0)
    if first:
        rows_ref, norm, lead, direction_ref, own = (refs.pop(0) for _ in range(5))
    cols, weights = refs.pop(0), refs.pop(0)
    copies = []
    if first:
        sems, *held_here = refs
        pos, noise, rhs, count = held_here
        copies = [
            pltpu.make_async_copy(source, target, sems.at[i])
            for i, (source, target) in enumerate(zip(hbm, held_here))
        ]
    for copy in copies:
        copy.start()
    if keep:
        known_out[...] = packet[...]

    width = packet.shape[0]
    half = tiles * LANES
    stride = half + half // 2
    filled = jnp.int32(0)
    listed = [(ref, b) for ref, (i, j) in zip(packets, taken) for b in range(i, j)]
    for packet, b in listed:
        base = b * stride
        for t in range(tiles):
            if t % 2 == 0:
                at = base + half + (t // 2) * LANES
                group = packet[:, at : at + LANES]
                sides, inverse = column_sides(group)
            v = packet[:, base + t * LANES : base + (t + 1) * LANES]
            row = (t % 2) * 4
            v = v * inverse[row + 3 : row + 4]
            rows = []
            for k in range(3):
                product = group[row + k : row + k + 1] * v
                top = product.astype(bf16).astype(f32)
                rows += [top, product - top]
            at = pl.ds(pl.multiple_of(filled + t * LANES, LANES), LANES)
            cols[:, at] = sides[t % 2]
            weights[:, at] = jnp.concatenate(rows, axis=0).astype(bf16)
        held = jnp.max(packet[3:4, base + half : base + half + LANES])
        filled = filled + held.astype(jnp.int32) * LANES

    slots = acc.shape[1]
    if first:
        copies[0].wait()
        rows_ref[...] = row_side(pos[...])
        norm[...] = gram(packets[0][:, :half], packets[0][:, :half], width)
        acc[...] = jnp.zeros(acc.shape, f32)
    else:
        acc[...] = acc_in[...]

    def step(begin, size):
        at = pl.ds(pl.multiple_of(begin, LANES), size)
        side, w = cols[:, at], weights[:, at]
        for r in range(0, slots, UNIT):
            near = slice(r, r + UNIT)
            u = lax.dot_general(
                side,
                rows_ref[:, near],
                (((0,), (0,)), ((), ())),
                preferred_element_type=f32,
            )
            u = jnp.maximum(u, near_sq)
            value = (u + lift) * pl.reciprocal(u * (u + gap), approx=True)
            top = value.astype(bf16)
            low = (value - top.astype(f32)).astype(bf16)
            part = acc[:, near] + jnp.dot(w, top, preferred_element_type=f32)
            acc[:, near] = part + jnp.dot(w, low, preferred_element_type=f32)

    full = min(STEP, len(listed) * half)
    steps = filled // full
    rest = filled - steps * full

    @pl.loop(0, steps)
    def _(i):
        step(i * full, full)

    begin, longest = steps * full, full
    if len(listed) * half > full:
        longest = full // 2
        more = rest >= longest

        @pl.when(more)
        def _(begin=begin):
            step(begin, longest)

        begin = jnp.where(more, begin + longest, begin)
        rest = jnp.where(more, rest - longest, rest)

    for size in range(LANES, longest, LANES):

        @pl.when(rest == size)
        def _(size=size, begin=begin):
            step(begin, size)

    if first:
        for copy in copies[1:]:
            copy.wait()
        lane = lax.broadcasted_iota(jnp.int32, (1, slots), 1)
        live = (lane < count[0]).astype(f32)
        lead[...] = unit_of(pos[...]) * (live * scale)
        direction = rhs[...] * live
        direction_ref[...] = direction
        mine = (lax.axis_index("offs") == 0).astype(f32)
        own[...] = (mine * noise[...].reshape(1, slots) * live) * direction
    if last:
        image = own[...]
        for k in range(3):
            at = 2 * k * width
            pulled = acc[at : at + width] + acc[at + width : at + 2 * width]
            image += lead[k : k + 1] * pulled
        out[:, :slots] = image
        out[:, slots:] = norm[...] + gram(direction_ref[...], image, 0)


def solved(small):
    width = small.shape[0]
    shape = small.shape
    c = [jnp.broadcast_to(small[:, j : j + 1], shape) for j in range(width)]
    r = [
        jnp.broadcast_to(small[:, j : j + 1], shape) for j in range(width, 2 * width)
    ]
    for k in range(width):
        inverse = pl.reciprocal(c[k], approx=True)[k : k + 1]
        ck, rk = c[k], r[k]
        for j in range(width):
            if j != k:
                factor = c[j][k : k + 1] * inverse
                c[j] = c[j] - ck * factor
                r[j] = r[j] - rk * factor
        c[k], r[k] = ck * inverse, rk * inverse
    return r


def combined(columns, x):
    parts = []
    for t in range(0, x.shape[1], LANES):
        tile = x[:, t : t + LANES]
        parts.append(sum(col * tile[m : m + 1] for m, col in enumerate(columns)))
    return jnp.concatenate(parts, axis=1)


def tail_kernel(small, mine, other, direction_ref, sol, res):
    columns = solved(small[...])
    direction = direction_ref[...]
    slots = direction.shape[1]
    image = mine[:, :slots] + other[:, :slots]
    sol[...] = combined(columns, direction)
    res[...] = direction - combined(columns, image)


def call(kernel, out_shape, in_specs, out_specs, scratch, name, flops=0):
    return pl.pallas_call(
        kernel,
        out_shape=out_shape,
        in_specs=in_specs,
        out_specs=out_specs,
        scratch_shapes=scratch,
        compiler_params=pltpu.CompilerParams(vmem_limit_bytes=LIMIT),
        cost_estimate=pl.CostEstimate(
            flops=flops, bytes_accessed=1 << 17, transcendentals=0
        ),
        name=name,
    )


def exchanged(block, distance):
    blocks, sides = lax.axis_size("blk"), lax.axis_size("offs")
    route = [
        ((b ^ distance) * sides + sides - 1 - c, b * sides + c)
        for b in range(blocks)
        for c in range(sides)
    ]
    return lax.ppermute(block, ("blk", "offs"), route)


def body(position, noise_var, rhs, block_count):
    width, slots = rhs.shape
    blocks = lax.axis_size("blk")
    tiles = slots // LANES // 2
    half = tiles * LANES
    shape = jax.ShapeDtypeStruct
    pos_buf = pltpu.VMEM(position.shape, f32)
    rhs_buf = pltpu.VMEM(rhs.shape, f32)
    noise_buf = pltpu.VMEM(noise_var.shape, f32)
    count_buf = pltpu.SMEM((1,), jnp.int32)

    first = call(
        first_kernel, shape((1, LANES), jnp.int32), [], VMEM, [], "first", 1 << 30
    )()
    block_count, first = lax.optimization_barrier((block_count, first))
    counted = call(
        count_kernel,
        shape((1, LANES), jnp.int32),
        [pl.BlockSpec(memory_space=pltpu.SMEM), VMEM],
        VMEM,
        [],
        "count",
        0,
    )(block_count, first)
    packet = call(
        pack_kernel,
        shape((width, half + half // 2), f32),
        [VMEM] * 3,
        VMEM,
        [],
        "pack",
    )(position, rhs, counted)

    acc_shape = shape((6 * width, slots), f32)
    rows_shape = shape((32, slots), bf16)

    def pairs(parts, taken, rows=None, acc=None, ready=(), keep=False):
        first, last = rows is None, bool(ready)
        args, specs = list(parts), [VMEM] * len(parts)
        if first:
            args += [position, noise_var, rhs, block_count]
            specs += [HBM] * 4
        else:
            args += [rows, acc, *ready]
            specs += [VMEM] * (2 + len(ready))
        count = sum(stop - start for start, stop in taken)
        scratch = [
            pltpu.VMEM((32, count * half), bf16),
            pltpu.VMEM((6 * width, count * half), bf16),
        ]
        if last:
            outs = (shape((width, slots + LANES), f32),)
            scratch = [pltpu.VMEM(acc_shape.shape, f32)] + scratch
        else:
            outs = (shape(parts[0].shape, f32),) if keep else ()
            outs += (acc_shape,)
        if first:
            outs += (rows_shape, shape((width, LANES), f32))
            outs += (shape(position.shape, f32),) + (shape(rhs.shape, f32),) * 2
            scratch += [pltpu.SemaphoreType.DMA((4,))]
            scratch += [pos_buf, noise_buf, rhs_buf, count_buf]
        kernel = functools.partial(pair_kernel, first, last, keep, taken, tiles)
        flops = 2 * slots * count * half * 64
        name = f"pairs_{count}"
        return call(kernel, outs, specs, (VMEM,) * len(outs), scratch, name, flops)(*args)

    distances = [blocks >> k for k in range(1, blocks.bit_length())]
    known, size = packet, 1
    rows = None
    for distance in distances[:-2]:
        arrived = exchanged(known, distance)
        fresh = (size // 2, size)
        if rows is None:
            known, acc, rows, *ready = pairs([known], [fresh], keep=True)
        else:
            known, acc = pairs([known], [fresh], rows, acc, keep=True)
        known = jnp.concatenate([known, arrived], axis=1)
        size *= 2
    near = exchanged(known, distances[-2])
    far = exchanged(known, distances[-1])
    (acc,) = pairs([known], [(size // 2, size)], rows, acc)
    near, acc = lax.optimization_barrier((near, acc))
    rest = exchanged(near, distances[-1])
    (acc,) = pairs([near, far], [(0, size)] * 2, rows, acc)
    (mine,) = pairs([rest], [(0, size)], rows, acc, ready)
    direction = ready[2]
    other = exchanged(mine, 0)
    small = mine[:, slots:] + other[:, slots:]
    distance = blocks // 2
    while distance:
        small = small + exchanged(small, distance)
        distance //= 2

    return tuple(
        call(
            tail_kernel,
            (shape(rhs.shape, f32),) * 2,
            [VMEM] * 4,
            (VMEM, VMEM),
            [],
            "tail",
        )(small, mine, other, direction)
    )


def solution(mesh):
    return jax.shard_map(
        body,
        mesh=mesh,
        in_specs=(
            P(None, ("mocks", "blk")),
            P(("mocks", "blk")),
            P(None, ("mocks", "blk")),
            P(("mocks", "blk")),
        ),
        out_specs=(P(None, ("mocks", "blk")), P(None, ("mocks", "blk"))),
        check_vma=False,
    )
```

```python
import functools

import jax
import jax.numpy as jnp
from jax import lax
from jax.experimental import pallas as pl
from jax.experimental.pallas import tpu as pltpu
from jax.sharding import PartitionSpec as P

near_weight = 0.6
near_length = 40.0
far_weight = 0.4
far_length = 120.0
near_sq = near_length * near_length
far_sq = far_length * far_length
gap = far_sq - near_sq
scale = near_weight * near_sq + far_weight * far_sq
lift = near_weight * near_sq * gap / scale

LANES = 128
UNIT = 256
STEP = 1024
f32 = jnp.float32
bf16 = jnp.bfloat16
VMEM = pl.BlockSpec(memory_space=pltpu.VMEM)
HBM = pl.BlockSpec(memory_space=pltpu.HBM)
LIMIT = 24 * 2**20


def split3(x):
    top = x.astype(bf16).astype(f32)
    rest = x - top
    mid = rest.astype(bf16).astype(f32)
    return top, mid, rest - mid


def row_side(pos):
    width = pos.shape[1]
    one, none = jnp.ones((1, width), f32), jnp.zeros((1, width), f32)
    top, mid, low = split3(pos)
    square = split3(jnp.sum(pos * pos, axis=0, keepdims=True) + near_sq)
    a = jnp.concatenate([top, one, mid, none], axis=0)
    b = jnp.concatenate([top, one, low, none], axis=0)
    c = jnp.concatenate([*square, *[none] * 5], axis=0)
    return jnp.concatenate([a, b, a, c], axis=0).astype(bf16)


def column_sides(group):
    row = lax.broadcasted_iota(jnp.int32, group.shape, 0)
    fourth = row % 4 == 3
    upper = row < 4
    square = group * group
    square = sum(pltpu.roll(square, k, 0) for k in (1, 2, 3))
    scaled = jnp.where(fourth, square, -2.0 * group)
    ahead = split3(scaled)
    swapped = [pltpu.roll(x, 4, 0) for x in ahead]
    tail = jnp.where(upper, 1.0, 0.0)
    sides = []
    for (t, m, w), (tt, mm, _) in ((ahead, swapped), (swapped, ahead)):
        pairs = [(t, tt), (m, tt), (w, mm)]
        rows = [jnp.where(upper, x, y) for x, y in pairs] + [tail]
        sides.append(jnp.concatenate(rows, axis=0).astype(bf16))
    inverse = jnp.where(square > 0.0, lax.rsqrt(square), 0.0)
    return sides, inverse


def unit_of(pos):
    square = jnp.sum(pos * pos, axis=0, keepdims=True)
    return pos * jnp.where(square > 0.0, lax.rsqrt(square), 0.0)


def gram(left, right, first):
    width, slots = left.shape
    lane = lax.broadcasted_iota(jnp.int32, (width, LANES), 1)
    out = jnp.zeros((width, LANES), f32)
    for s in range(width):
        product = left * right[s : s + 1]
        folded = sum(product[:, t : t + LANES] for t in range(0, slots, LANES))
        out = jnp.where(lane == first + s, jnp.sum(folded, axis=1, keepdims=True), out)
    return out


def first_kernel(out):
    out[...] = jnp.zeros(out.shape, jnp.int32)


def count_kernel(count, first, out):
    out[...] = jnp.full(out.shape, count[0], jnp.int32) + first[...]


def pack_kernel(pos, rhs, count, out):
    width, slots = rhs.shape
    tiles = slots // LANES // 2
    side = (lax.axis_index("offs") + lax.axis_index("blk")) % 2
    odd = side == 1
    n = count[...]
    lane = lax.broadcasted_iota(jnp.int32, (1, LANES), 1)
    held = jnp.clip((n + LANES - 1 - side * LANES + LANES) // (2 * LANES), 0, tiles)
    held = held.astype(f32)
    for t in range(tiles):
        even_at = slice(2 * t * LANES, (2 * t + 1) * LANES)
        odd_at = slice((2 * t + 1) * LANES, (2 * t + 2) * LANES)
        first = (2 * t + side) * LANES
        value = jnp.where(odd, rhs[:, odd_at], rhs[:, even_at])
        out[:, t * LANES : (t + 1) * LANES] = jnp.where(first + lane < n, value, 0.0)
        place = jnp.where(odd, pos[:, odd_at], pos[:, even_at])
        at = (tiles + t // 2) * LANES
        row = (t % 2) * 4
        out[row : row + 4, at : at + LANES] = jnp.concatenate([place, held], axis=0)


def pair_kernel(first, last, keep, taken, tiles, *refs):
    refs = list(refs)
    packets = [refs.pop(0) for _ in taken]
    packet = packets[0]
    if first:
        hbm = [refs.pop(0) for _ in range(4)]
    else:
        rows_ref, acc_in = refs.pop(0), refs.pop(0)
    if last:
        norm, lead, direction_ref, own = (refs.pop(0) for _ in range(4))
        out, acc = refs.pop(0), refs.pop(0)
    else:
        known_out = refs.pop(0) if keep else None
        acc = refs.pop(0)
    if first:
        rows_ref, norm, lead, direction_ref, own = (refs.pop(0) for _ in range(5))
    cols, weights = refs.pop(0), refs.pop(0)
    copies = []
    if first:
        sems, *held_here = refs
        pos, noise, rhs, count = held_here
        copies = [
            pltpu.make_async_copy(source, target, sems.at[i])
            for i, (source, target) in enumerate(zip(hbm, held_here))
        ]
    for copy in copies:
        copy.start()
    if keep:
        known_out[...] = packet[...]

    width = packet.shape[0]
    half = tiles * LANES
    stride = half + half // 2
    filled = jnp.int32(0)
    listed = [(ref, b) for ref, (i, j) in zip(packets, taken) for b in range(i, j)]
    for packet, b in listed:
        base = b * stride
        for t in range(tiles):
            if t % 2 == 0:
                at = base + half + (t // 2) * LANES
                group = packet[:, at : at + LANES]
                sides, inverse = column_sides(group)
            v = packet[:, base + t * LANES : base + (t + 1) * LANES]
            row = (t % 2) * 4
            v = v * inverse[row + 3 : row + 4]
            rows = []
            for k in range(3):
                product = group[row + k : row + k + 1] * v
                top = product.astype(bf16).astype(f32)
                rows += [top, product - top]
            at = pl.ds(pl.multiple_of(filled + t * LANES, LANES), LANES)
            cols[:, at] = sides[t % 2]
            weights[:, at] = jnp.concatenate(rows, axis=0).astype(bf16)
        held = jnp.max(packet[3:4, base + half : base + half + LANES])
        filled = filled + held.astype(jnp.int32) * LANES

    slots = acc.shape[1]
    if first:
        copies[0].wait()
        rows_ref[...] = row_side(pos[...])
        norm[...] = gram(packets[0][:, :half], packets[0][:, :half], width)
        acc[...] = jnp.zeros(acc.shape, f32)
    else:
        acc[...] = acc_in[...]

    def step(begin, size):
        at = pl.ds(pl.multiple_of(begin, LANES), size)
        side, w = cols[:, at], weights[:, at]
        for r in range(0, slots, UNIT):
            near = slice(r, r + UNIT)
            u = lax.dot_general(
                side,
                rows_ref[:, near],
                (((0,), (0,)), ((), ())),
                preferred_element_type=f32,
            )
            u = jnp.maximum(u, near_sq)
            value = (u + lift) * pl.reciprocal(u * (u + gap), approx=True)
            top = value.astype(bf16)
            low = (value - top.astype(f32)).astype(bf16)
            part = acc[:, near] + jnp.dot(w, top, preferred_element_type=f32)
            acc[:, near] = part + jnp.dot(w, low, preferred_element_type=f32)

    most = len(listed) * half
    full = STEP * 3 // 4 if most == STEP else min(STEP, most)
    steps = filled // full
    rest = filled - steps * full

    @pl.loop(0, steps)
    def _(i):
        step(i * full, full)

    begin, longest = steps * full, full
    if most > STEP:
        longest = full // 2
        more = rest >= longest

        @pl.when(more)
        def _(begin=begin):
            step(begin, longest)

        begin = jnp.where(more, begin + longest, begin)
        rest = jnp.where(more, rest - longest, rest)

    for size in range(LANES, longest, LANES):

        @pl.when(rest == size)
        def _(size=size, begin=begin):
            step(begin, size)

    if first:
        for copy in copies[1:]:
            copy.wait()
        lane = lax.broadcasted_iota(jnp.int32, (1, slots), 1)
        live = (lane < count[0]).astype(f32)
        lead[...] = unit_of(pos[...]) * (live * scale)
        direction = rhs[...] * live
        direction_ref[...] = direction
        mine = (lax.axis_index("offs") == 0).astype(f32)
        own[...] = (mine * noise[...].reshape(1, slots) * live) * direction
    if last:
        image = own[...]
        for k in range(3):
            at = 2 * k * width
            pulled = acc[at : at + width] + acc[at + width : at + 2 * width]
            image += lead[k : k + 1] * pulled
        out[:, :slots] = image
        out[:, slots:] = norm[...] + gram(direction_ref[...], image, 0)


def solved(small):
    width = small.shape[0]
    shape = small.shape
    c = [jnp.broadcast_to(small[:, j : j + 1], shape) for j in range(width)]
    r = [
        jnp.broadcast_to(small[:, j : j + 1], shape) for j in range(width, 2 * width)
    ]
    for k in range(width):
        inverse = pl.reciprocal(c[k], approx=True)[k : k + 1]
        ck, rk = c[k], r[k]
        for j in range(width):
            if j != k:
                factor = c[j][k : k + 1] * inverse
                c[j] = c[j] - ck * factor
                r[j] = r[j] - rk * factor
        c[k], r[k] = ck * inverse, rk * inverse
    return r


def combined(columns, x):
    parts = []
    for t in range(0, x.shape[1], LANES):
        tile = x[:, t : t + LANES]
        parts.append(sum(col * tile[m : m + 1] for m, col in enumerate(columns)))
    return jnp.concatenate(parts, axis=1)


def tail_kernel(small, mine, other, direction_ref, sol, res):
    columns = solved(small[...])
    direction = direction_ref[...]
    slots = direction.shape[1]
    image = mine[:, :slots] + other[:, :slots]
    sol[...] = combined(columns, direction)
    res[...] = direction - combined(columns, image)


def call(kernel, out_shape, in_specs, out_specs, scratch, name, flops=0):
    return pl.pallas_call(
        kernel,
        out_shape=out_shape,
        in_specs=in_specs,
        out_specs=out_specs,
        scratch_shapes=scratch,
        compiler_params=pltpu.CompilerParams(vmem_limit_bytes=LIMIT),
        cost_estimate=pl.CostEstimate(
            flops=flops, bytes_accessed=1 << 17, transcendentals=0
        ),
        name=name,
    )


def exchanged(block, distance):
    blocks, sides = lax.axis_size("blk"), lax.axis_size("offs")
    route = [
        ((b ^ distance) * sides + sides - 1 - c, b * sides + c)
        for b in range(blocks)
        for c in range(sides)
    ]
    return lax.ppermute(block, ("blk", "offs"), route)


def body(position, noise_var, rhs, block_count):
    width, slots = rhs.shape
    blocks = lax.axis_size("blk")
    tiles = slots // LANES // 2
    half = tiles * LANES
    shape = jax.ShapeDtypeStruct
    pos_buf = pltpu.VMEM(position.shape, f32)
    rhs_buf = pltpu.VMEM(rhs.shape, f32)
    noise_buf = pltpu.VMEM(noise_var.shape, f32)
    count_buf = pltpu.SMEM((1,), jnp.int32)

    first = call(
        first_kernel, shape((1, LANES), jnp.int32), [], VMEM, [], "first", 1 << 30
    )()
    block_count, first = lax.optimization_barrier((block_count, first))
    counted = call(
        count_kernel,
        shape((1, LANES), jnp.int32),
        [pl.BlockSpec(memory_space=pltpu.SMEM), VMEM],
        VMEM,
        [],
        "count",
        0,
    )(block_count, first)
    packet = call(
        pack_kernel,
        shape((width, half + half // 2), f32),
        [VMEM] * 3,
        VMEM,
        [],
        "pack",
    )(position, rhs, counted)

    acc_shape = shape((6 * width, slots), f32)
    rows_shape = shape((32, slots), bf16)

    def pairs(parts, taken, rows=None, acc=None, ready=(), keep=False):
        first, last = rows is None, bool(ready)
        args, specs = list(parts), [VMEM] * len(parts)
        if first:
            args += [position, noise_var, rhs, block_count]
            specs += [HBM] * 4
        else:
            args += [rows, acc, *ready]
            specs += [VMEM] * (2 + len(ready))
        count = sum(stop - start for start, stop in taken)
        scratch = [
            pltpu.VMEM((32, count * half), bf16),
            pltpu.VMEM((6 * width, count * half), bf16),
        ]
        if last:
            outs = (shape((width, slots + LANES), f32),)
            scratch = [pltpu.VMEM(acc_shape.shape, f32)] + scratch
        else:
            outs = (shape(parts[0].shape, f32),) if keep else ()
            outs += (acc_shape,)
        if first:
            outs += (rows_shape, shape((width, LANES), f32))
            outs += (shape(position.shape, f32),) + (shape(rhs.shape, f32),) * 2
            scratch += [pltpu.SemaphoreType.DMA((4,))]
            scratch += [pos_buf, noise_buf, rhs_buf, count_buf]
        kernel = functools.partial(pair_kernel, first, last, keep, taken, tiles)
        flops = 2 * slots * count * half * 64
        name = f"pairs_{count}"
        return call(kernel, outs, specs, (VMEM,) * len(outs), scratch, name, flops)(*args)

    distances = [blocks >> k for k in range(1, blocks.bit_length())]
    known, size = packet, 1
    rows = None
    for distance in distances[:-2]:
        arrived = exchanged(known, distance)
        fresh = (size // 2, size)
        if rows is None:
            known, acc, rows, *ready = pairs([known], [fresh], keep=True)
        else:
            known, acc = pairs([known], [fresh], rows, acc, keep=True)
        known = jnp.concatenate([known, arrived], axis=1)
        size *= 2
    near = exchanged(known, distances[-2])
    far = exchanged(known, distances[-1])
    (acc,) = pairs([known], [(size // 2, size)], rows, acc)
    near, acc = lax.optimization_barrier((near, acc))
    rest = exchanged(near, distances[-1])
    (acc,) = pairs([near, far], [(0, size)] * 2, rows, acc)
    (mine,) = pairs([rest], [(0, size)], rows, acc, ready)
    direction = ready[2]
    other = exchanged(mine, 0)
    small = mine[:, slots:] + other[:, slots:]
    distance = blocks // 2
    while distance:
        small = small + exchanged(small, distance)
        distance //= 2

    return tuple(
        call(
            tail_kernel,
            (shape(rhs.shape, f32),) * 2,
            [VMEM] * 4,
            (VMEM, VMEM),
            [],
            "tail",
        )(small, mine, other, direction)
    )


def solution(mesh):
    return jax.shard_map(
        body,
        mesh=mesh,
        in_specs=(
            P(None, ("mocks", "blk")),
            P(("mocks", "blk")),
            P(None, ("mocks", "blk")),
            P(("mocks", "blk")),
        ),
        out_specs=(P(None, ("mocks", "blk")), P(None, ("mocks", "blk"))),
        check_vma=False,
    )
```

```python
import functools

import jax
import jax.numpy as jnp
from jax import lax
from jax.experimental import pallas as pl
from jax.experimental.pallas import tpu as pltpu
from jax.sharding import PartitionSpec as P

near_weight = 0.6
near_length = 40.0
far_weight = 0.4
far_length = 120.0
near_sq = near_length * near_length
far_sq = far_length * far_length
gap = far_sq - near_sq
scale = near_weight * near_sq + far_weight * far_sq
lift = near_weight * near_sq * gap / scale

LANES = 128
UNIT = 256
STEP = 1024
f32 = jnp.float32
bf16 = jnp.bfloat16
VMEM = pl.BlockSpec(memory_space=pltpu.VMEM)
HBM = pl.BlockSpec(memory_space=pltpu.HBM)
LIMIT = 24 * 2**20


def split3(x):
    top = x.astype(bf16).astype(f32)
    rest = x - top
    mid = rest.astype(bf16).astype(f32)
    return top, mid, rest - mid


def row_side(pos):
    width = pos.shape[1]
    one, none = jnp.ones((1, width), f32), jnp.zeros((1, width), f32)
    top, mid, low = split3(pos)
    square = split3(jnp.sum(pos * pos, axis=0, keepdims=True) + near_sq)
    a = jnp.concatenate([top, one, mid, none], axis=0)
    b = jnp.concatenate([top, one, low, none], axis=0)
    c = jnp.concatenate([*square, *[none] * 5], axis=0)
    return jnp.concatenate([a, b, a, c], axis=0).astype(bf16)


def column_sides(group):
    row = lax.broadcasted_iota(jnp.int32, group.shape, 0)
    fourth = row % 4 == 3
    upper = row < 4
    square = group * group
    square = sum(pltpu.roll(square, k, 0) for k in (1, 2, 3))
    scaled = jnp.where(fourth, square, -2.0 * group)
    ahead = split3(scaled)
    swapped = [pltpu.roll(x, 4, 0) for x in ahead]
    tail = jnp.where(upper, 1.0, 0.0)
    sides = []
    for (t, m, w), (tt, mm, _) in ((ahead, swapped), (swapped, ahead)):
        pairs = [(t, tt), (m, tt), (w, mm)]
        rows = [jnp.where(upper, x, y) for x, y in pairs] + [tail]
        sides.append(jnp.concatenate(rows, axis=0).astype(bf16))
    inverse = jnp.where(square > 0.0, lax.rsqrt(square), 0.0)
    return sides, inverse


def unit_of(pos):
    square = jnp.sum(pos * pos, axis=0, keepdims=True)
    return pos * jnp.where(square > 0.0, lax.rsqrt(square), 0.0)


def gram(left, right, first):
    width, slots = left.shape
    lane = lax.broadcasted_iota(jnp.int32, (width, LANES), 1)
    out = jnp.zeros((width, LANES), f32)
    for s in range(width):
        product = left * right[s : s + 1]
        folded = sum(product[:, t : t + LANES] for t in range(0, slots, LANES))
        out = jnp.where(lane == first + s, jnp.sum(folded, axis=1, keepdims=True), out)
    return out


def first_kernel(out):
    out[...] = jnp.zeros(out.shape, jnp.int32)


def count_kernel(count, first, out):
    out[...] = jnp.full(out.shape, count[0], jnp.int32) + first[...]


def pack_kernel(pos, rhs, count, out):
    width, slots = rhs.shape
    tiles = slots // LANES // 2
    side = (lax.axis_index("offs") + lax.axis_index("blk")) % 2
    odd = side == 1
    n = count[...]
    lane = lax.broadcasted_iota(jnp.int32, (1, LANES), 1)
    held = jnp.clip((n + LANES - 1 - side * LANES + LANES) // (2 * LANES), 0, tiles)
    held = held.astype(f32)
    for t in range(tiles):
        even_at = slice(2 * t * LANES, (2 * t + 1) * LANES)
        odd_at = slice((2 * t + 1) * LANES, (2 * t + 2) * LANES)
        first = (2 * t + side) * LANES
        value = jnp.where(odd, rhs[:, odd_at], rhs[:, even_at])
        out[:, t * LANES : (t + 1) * LANES] = jnp.where(first + lane < n, value, 0.0)
        place = jnp.where(odd, pos[:, odd_at], pos[:, even_at])
        at = (tiles + t // 2) * LANES
        row = (t % 2) * 4
        out[row : row + 4, at : at + LANES] = jnp.concatenate([place, held], axis=0)


def pair_kernel(first, last, keep, taken, tiles, *refs):
    refs = list(refs)
    packets = [refs.pop(0) for _ in taken]
    packet = packets[0]
    if first:
        hbm = [refs.pop(0) for _ in range(4)]
    else:
        rows_ref, acc_in = refs.pop(0), refs.pop(0)
    if last:
        norm, lead, direction_ref, own = (refs.pop(0) for _ in range(4))
        out, acc = refs.pop(0), refs.pop(0)
    else:
        known_out = refs.pop(0) if keep else None
        acc = refs.pop(0)
    if first:
        rows_ref, norm, lead, direction_ref, own = (refs.pop(0) for _ in range(5))
    cols, weights = refs.pop(0), refs.pop(0)
    copies = []
    if first:
        sems, *held_here = refs
        pos, noise, rhs, count = held_here
        copies = [
            pltpu.make_async_copy(source, target, sems.at[i])
            for i, (source, target) in enumerate(zip(hbm, held_here))
        ]
    for copy in copies:
        copy.start()
    if keep:
        known_out[...] = packet[...]

    width = packet.shape[0]
    half = tiles * LANES
    stride = half + half // 2
    filled = jnp.int32(0)
    listed = [(ref, b) for ref, (i, j) in zip(packets, taken) for b in range(i, j)]
    for packet, b in listed:
        base = b * stride
        for t in range(tiles):
            if t % 2 == 0:
                at = base + half + (t // 2) * LANES
                group = packet[:, at : at + LANES]
                sides, inverse = column_sides(group)
            v = packet[:, base + t * LANES : base + (t + 1) * LANES]
            row = (t % 2) * 4
            v = v * inverse[row + 3 : row + 4]
            rows = []
            for k in range(3):
                product = group[row + k : row + k + 1] * v
                top = product.astype(bf16).astype(f32)
                rows += [top, product - top]
            at = pl.ds(pl.multiple_of(filled + t * LANES, LANES), LANES)
            cols[:, at] = sides[t % 2]
            weights[:, at] = jnp.concatenate(rows, axis=0).astype(bf16)
        held = jnp.max(packet[3:4, base + half : base + half + LANES])
        filled = filled + held.astype(jnp.int32) * LANES

    slots = acc.shape[1]
    if first:
        copies[0].wait()
        rows_ref[...] = row_side(pos[...])
        norm[...] = gram(packets[0][:, :half], packets[0][:, :half], width)
        acc[...] = jnp.zeros(acc.shape, f32)
    else:
        acc[...] = acc_in[...]

    def step(begin, size):
        at = pl.ds(pl.multiple_of(begin, LANES), size)
        side, w = cols[:, at], weights[:, at]
        for r in range(0, slots, UNIT):
            near = slice(r, r + UNIT)
            u = lax.dot_general(
                side,
                rows_ref[:, near],
                (((0,), (0,)), ((), ())),
                preferred_element_type=f32,
            )
            u = jnp.maximum(u, near_sq)
            value = (u + lift) * pl.reciprocal(u * (u + gap), approx=True)
            top = value.astype(bf16)
            low = (value - top.astype(f32)).astype(bf16)
            part = acc[:, near] + jnp.dot(w, top, preferred_element_type=f32)
            acc[:, near] = part + jnp.dot(w, low, preferred_element_type=f32)

    most = len(listed) * half
    full = STEP - LANES if most == STEP else min(STEP, most)
    steps = filled // full
    rest = filled - steps * full

    @pl.loop(0, steps)
    def _(i):
        step(i * full, full)

    begin, longest = steps * full, full
    if most > STEP:
        longest = full // 2
        more = rest >= longest

        @pl.when(more)
        def _(begin=begin):
            step(begin, longest)

        begin = jnp.where(more, begin + longest, begin)
        rest = jnp.where(more, rest - longest, rest)

    for size in range(LANES, longest, LANES):

        @pl.when(rest == size)
        def _(size=size, begin=begin):
            step(begin, size)

    if first:
        for copy in copies[1:]:
            copy.wait()
        lane = lax.broadcasted_iota(jnp.int32, (1, slots), 1)
        live = (lane < count[0]).astype(f32)
        lead[...] = unit_of(pos[...]) * (live * scale)
        direction = rhs[...] * live
        direction_ref[...] = direction
        mine = (lax.axis_index("offs") == 0).astype(f32)
        own[...] = (mine * noise[...].reshape(1, slots) * live) * direction
    if last:
        image = own[...]
        for k in range(3):
            at = 2 * k * width
            pulled = acc[at : at + width] + acc[at + width : at + 2 * width]
            image += lead[k : k + 1] * pulled
        out[:, :slots] = image
        out[:, slots:] = norm[...] + gram(direction_ref[...], image, 0)


def solved(small):
    width = small.shape[0]
    shape = small.shape
    c = [jnp.broadcast_to(small[:, j : j + 1], shape) for j in range(width)]
    r = [
        jnp.broadcast_to(small[:, j : j + 1], shape) for j in range(width, 2 * width)
    ]
    for k in range(width):
        inverse = pl.reciprocal(c[k], approx=True)[k : k + 1]
        ck, rk = c[k], r[k]
        for j in range(width):
            if j != k:
                factor = c[j][k : k + 1] * inverse
                c[j] = c[j] - ck * factor
                r[j] = r[j] - rk * factor
        c[k], r[k] = ck * inverse, rk * inverse
    return r


def combined(columns, x):
    parts = []
    for t in range(0, x.shape[1], LANES):
        tile = x[:, t : t + LANES]
        parts.append(sum(col * tile[m : m + 1] for m, col in enumerate(columns)))
    return jnp.concatenate(parts, axis=1)


def tail_kernel(small, mine, other, direction_ref, sol, res):
    columns = solved(small[...])
    direction = direction_ref[...]
    slots = direction.shape[1]
    image = mine[:, :slots] + other[:, :slots]
    sol[...] = combined(columns, direction)
    res[...] = direction - combined(columns, image)


def call(kernel, out_shape, in_specs, out_specs, scratch, name, flops=0):
    return pl.pallas_call(
        kernel,
        out_shape=out_shape,
        in_specs=in_specs,
        out_specs=out_specs,
        scratch_shapes=scratch,
        compiler_params=pltpu.CompilerParams(vmem_limit_bytes=LIMIT),
        cost_estimate=pl.CostEstimate(
            flops=flops, bytes_accessed=1 << 17, transcendentals=0
        ),
        name=name,
    )


def exchanged(block, distance):
    blocks, sides = lax.axis_size("blk"), lax.axis_size("offs")
    route = [
        ((b ^ distance) * sides + sides - 1 - c, b * sides + c)
        for b in range(blocks)
        for c in range(sides)
    ]
    return lax.ppermute(block, ("blk", "offs"), route)


def body(position, noise_var, rhs, block_count):
    width, slots = rhs.shape
    blocks = lax.axis_size("blk")
    tiles = slots // LANES // 2
    half = tiles * LANES
    shape = jax.ShapeDtypeStruct
    pos_buf = pltpu.VMEM(position.shape, f32)
    rhs_buf = pltpu.VMEM(rhs.shape, f32)
    noise_buf = pltpu.VMEM(noise_var.shape, f32)
    count_buf = pltpu.SMEM((1,), jnp.int32)

    first = call(
        first_kernel, shape((1, LANES), jnp.int32), [], VMEM, [], "first", 1 << 30
    )()
    block_count, first = lax.optimization_barrier((block_count, first))
    counted = call(
        count_kernel,
        shape((1, LANES), jnp.int32),
        [pl.BlockSpec(memory_space=pltpu.SMEM), VMEM],
        VMEM,
        [],
        "count",
        0,
    )(block_count, first)
    packet = call(
        pack_kernel,
        shape((width, half + half // 2), f32),
        [VMEM] * 3,
        VMEM,
        [],
        "pack",
    )(position, rhs, counted)

    acc_shape = shape((6 * width, slots), f32)
    rows_shape = shape((32, slots), bf16)

    def pairs(parts, taken, rows=None, acc=None, ready=(), keep=False):
        first, last = rows is None, bool(ready)
        args, specs = list(parts), [VMEM] * len(parts)
        if first:
            args += [position, noise_var, rhs, block_count]
            specs += [HBM] * 4
        else:
            args += [rows, acc, *ready]
            specs += [VMEM] * (2 + len(ready))
        count = sum(stop - start for start, stop in taken)
        scratch = [
            pltpu.VMEM((32, count * half), bf16),
            pltpu.VMEM((6 * width, count * half), bf16),
        ]
        if last:
            outs = (shape((width, slots + LANES), f32),)
            scratch = [pltpu.VMEM(acc_shape.shape, f32)] + scratch
        else:
            outs = (shape(parts[0].shape, f32),) if keep else ()
            outs += (acc_shape,)
        if first:
            outs += (rows_shape, shape((width, LANES), f32))
            outs += (shape(position.shape, f32),) + (shape(rhs.shape, f32),) * 2
            scratch += [pltpu.SemaphoreType.DMA((4,))]
            scratch += [pos_buf, noise_buf, rhs_buf, count_buf]
        kernel = functools.partial(pair_kernel, first, last, keep, taken, tiles)
        flops = 2 * slots * count * half * 64
        name = f"pairs_{count}"
        return call(kernel, outs, specs, (VMEM,) * len(outs), scratch, name, flops)(*args)

    distances = [blocks >> k for k in range(1, blocks.bit_length())]
    known, size = packet, 1
    rows = None
    for distance in distances[:-2]:
        arrived = exchanged(known, distance)
        fresh = (size // 2, size)
        if rows is None:
            known, acc, rows, *ready = pairs([known], [fresh], keep=True)
        else:
            known, acc = pairs([known], [fresh], rows, acc, keep=True)
        known = jnp.concatenate([known, arrived], axis=1)
        size *= 2
    near = exchanged(known, distances[-2])
    far = exchanged(known, distances[-1])
    (acc,) = pairs([known], [(size // 2, size)], rows, acc)
    near, acc = lax.optimization_barrier((near, acc))
    rest = exchanged(near, distances[-1])
    (acc,) = pairs([near, far], [(0, size)] * 2, rows, acc)
    (mine,) = pairs([rest], [(0, size)], rows, acc, ready)
    direction = ready[2]
    other = exchanged(mine, 0)
    small = mine[:, slots:] + other[:, slots:]
    distance = blocks // 2
    while distance:
        small = small + exchanged(small, distance)
        distance //= 2

    return tuple(
        call(
            tail_kernel,
            (shape(rhs.shape, f32),) * 2,
            [VMEM] * 4,
            (VMEM, VMEM),
            [],
            "tail",
        )(small, mine, other, direction)
    )


def solution(mesh):
    return jax.shard_map(
        body,
        mesh=mesh,
        in_specs=(
            P(None, ("mocks", "blk")),
            P(("mocks", "blk")),
            P(None, ("mocks", "blk")),
            P(("mocks", "blk")),
        ),
        out_specs=(P(None, ("mocks", "blk")), P(None, ("mocks", "blk"))),
        check_vma=False,
    )
```

```python
import functools

import jax
import jax.numpy as jnp
from jax import lax
from jax.experimental import pallas as pl
from jax.experimental.pallas import tpu as pltpu
from jax.sharding import PartitionSpec as P

near_weight = 0.6
near_length = 40.0
far_weight = 0.4
far_length = 120.0
near_sq = near_length * near_length
far_sq = far_length * far_length
gap = far_sq - near_sq
scale = near_weight * near_sq + far_weight * far_sq
lift = near_weight * near_sq * gap / scale

LANES = 128
UNIT = 256
STEP = 1024
f32 = jnp.float32
bf16 = jnp.bfloat16
VMEM = pl.BlockSpec(memory_space=pltpu.VMEM)
HBM = pl.BlockSpec(memory_space=pltpu.HBM)
LIMIT = 24 * 2**20


def split3(x):
    top = x.astype(bf16).astype(f32)
    rest = x - top
    mid = rest.astype(bf16).astype(f32)
    return top, mid, rest - mid


def row_side(pos):
    width = pos.shape[1]
    one, none = jnp.ones((1, width), f32), jnp.zeros((1, width), f32)
    top, mid, low = split3(pos)
    square = split3(jnp.sum(pos * pos, axis=0, keepdims=True) + near_sq)
    a = jnp.concatenate([top, one, mid, none], axis=0)
    b = jnp.concatenate([top, one, low, none], axis=0)
    c = jnp.concatenate([*square, *[none] * 5], axis=0)
    return jnp.concatenate([a, b, a, c], axis=0).astype(bf16)


def column_sides(group):
    row = lax.broadcasted_iota(jnp.int32, group.shape, 0)
    fourth = row % 4 == 3
    upper = row < 4
    square = group * group
    square = sum(pltpu.roll(square, k, 0) for k in (1, 2, 3))
    scaled = jnp.where(fourth, square, -2.0 * group)
    ahead = split3(scaled)
    swapped = [pltpu.roll(x, 4, 0) for x in ahead]
    tail = jnp.where(upper, 1.0, 0.0)
    sides = []
    for (t, m, w), (tt, mm, _) in ((ahead, swapped), (swapped, ahead)):
        pairs = [(t, tt), (m, tt), (w, mm)]
        rows = [jnp.where(upper, x, y) for x, y in pairs] + [tail]
        sides.append(jnp.concatenate(rows, axis=0).astype(bf16))
    inverse = jnp.where(square > 0.0, lax.rsqrt(square), 0.0)
    return sides, inverse


def unit_of(pos):
    square = jnp.sum(pos * pos, axis=0, keepdims=True)
    return pos * jnp.where(square > 0.0, lax.rsqrt(square), 0.0)


def gram(left, right, first):
    width, slots = left.shape
    lane = lax.broadcasted_iota(jnp.int32, (width, LANES), 1)
    out = jnp.zeros((width, LANES), f32)
    for s in range(width):
        product = left * right[s : s + 1]
        folded = sum(product[:, t : t + LANES] for t in range(0, slots, LANES))
        out = jnp.where(lane == first + s, jnp.sum(folded, axis=1, keepdims=True), out)
    return out


def first_kernel(out):
    out[...] = jnp.zeros(out.shape, jnp.int32)


def count_kernel(count, first, out):
    out[...] = jnp.full(out.shape, count[0], jnp.int32) + first[...]


def pack_kernel(pos, rhs, count, out):
    width, slots = rhs.shape
    tiles = slots // LANES // 2
    side = (lax.axis_index("offs") + lax.axis_index("blk")) % 2
    odd = side == 1
    n = count[...]
    lane = lax.broadcasted_iota(jnp.int32, (1, LANES), 1)
    held = jnp.clip((n + LANES - 1 - side * LANES + LANES) // (2 * LANES), 0, tiles)
    held = held.astype(f32)
    for t in range(tiles):
        even_at = slice(2 * t * LANES, (2 * t + 1) * LANES)
        odd_at = slice((2 * t + 1) * LANES, (2 * t + 2) * LANES)
        first = (2 * t + side) * LANES
        value = jnp.where(odd, rhs[:, odd_at], rhs[:, even_at])
        out[:, t * LANES : (t + 1) * LANES] = jnp.where(first + lane < n, value, 0.0)
        place = jnp.where(odd, pos[:, odd_at], pos[:, even_at])
        at = (tiles + t // 2) * LANES
        row = (t % 2) * 4
        out[row : row + 4, at : at + LANES] = jnp.concatenate([place, held], axis=0)


def pair_kernel(first, last, keep, taken, tiles, *refs):
    refs = list(refs)
    packets = [refs.pop(0) for _ in taken]
    packet = packets[0]
    if first:
        hbm = [refs.pop(0) for _ in range(4)]
    else:
        rows_ref, acc_in = refs.pop(0), refs.pop(0)
    if last:
        norm, lead, direction_ref, own = (refs.pop(0) for _ in range(4))
        out, acc = refs.pop(0), refs.pop(0)
    else:
        known_out = refs.pop(0) if keep else None
        acc = refs.pop(0)
    if first:
        rows_ref, norm, lead, direction_ref, own = (refs.pop(0) for _ in range(5))
    cols, weights = refs.pop(0), refs.pop(0)
    copies = []
    if first:
        sems, *held_here = refs
        pos, noise, rhs, count = held_here
        copies = [
            pltpu.make_async_copy(source, target, sems.at[i])
            for i, (source, target) in enumerate(zip(hbm, held_here))
        ]
    for copy in copies:
        copy.start()
    if keep:
        known_out[...] = packet[...]

    width = packet.shape[0]
    half = tiles * LANES
    stride = half + half // 2
    filled = jnp.int32(0)
    listed = [(ref, b) for ref, (i, j) in zip(packets, taken) for b in range(i, j)]
    for packet, b in listed:
        base = b * stride
        for t in range(tiles):
            if t % 2 == 0:
                at = base + half + (t // 2) * LANES
                group = packet[:, at : at + LANES]
                sides, inverse = column_sides(group)
            v = packet[:, base + t * LANES : base + (t + 1) * LANES]
            row = (t % 2) * 4
            v = v * inverse[row + 3 : row + 4]
            rows = []
            for k in range(3):
                product = group[row + k : row + k + 1] * v
                top = product.astype(bf16).astype(f32)
                rows += [top, product - top]
            at = pl.ds(pl.multiple_of(filled + t * LANES, LANES), LANES)
            cols[:, at] = sides[t % 2]
            weights[:, at] = jnp.concatenate(rows, axis=0).astype(bf16)
        held = jnp.max(packet[3:4, base + half : base + half + LANES])
        filled = filled + held.astype(jnp.int32) * LANES

    slots = acc.shape[1]
    if first:
        copies[0].wait()
        rows_ref[...] = row_side(pos[...])
        norm[...] = gram(packets[0][:, :half], packets[0][:, :half], width)
        acc[...] = jnp.zeros(acc.shape, f32)
    else:
        acc[...] = acc_in[...]

    def step(begin, size):
        at = pl.ds(pl.multiple_of(begin, LANES), size)
        side, w = cols[:, at], weights[:, at]
        for r in range(0, slots, UNIT):
            near = slice(r, r + UNIT)
            u = lax.dot_general(
                side,
                rows_ref[:, near],
                (((0,), (0,)), ((), ())),
                preferred_element_type=f32,
            )
            u = jnp.maximum(u, near_sq)
            value = (u + lift) * pl.reciprocal(u * (u + gap), approx=True)
            top = value.astype(bf16)
            low = (value - top.astype(f32)).astype(bf16)
            part = acc[:, near] + jnp.dot(w, top, preferred_element_type=f32)
            acc[:, near] = part + jnp.dot(w, low, preferred_element_type=f32)

    full = min(STEP, len(listed) * half)
    steps = filled // full
    rest = filled - steps * full

    @pl.loop(0, steps)
    def _(i):
        step(i * full, full)

    begin, longest = steps * full, full
    if len(listed) * half > full:
        longest = full // 2
        more = rest >= longest

        @pl.when(more)
        def _(begin=begin):
            step(begin, longest)

        begin = jnp.where(more, begin + longest, begin)
        rest = jnp.where(more, rest - longest, rest)

    for size in range(LANES, longest, LANES):

        @pl.when(rest == size)
        def _(size=size, begin=begin):
            step(begin, size)

    if first:
        for copy in copies[1:]:
            copy.wait()
        lane = lax.broadcasted_iota(jnp.int32, (1, slots), 1)
        live = (lane < count[0]).astype(f32)
        lead[...] = unit_of(pos[...]) * (live * scale)
        direction = rhs[...] * live
        direction_ref[...] = direction
        mine = (lax.axis_index("offs") == 0).astype(f32)
        own[...] = (mine * noise[...].reshape(1, slots) * live) * direction
    if last:
        image = own[...]
        for k in range(3):
            at = 2 * k * width
            pulled = acc[at : at + width] + acc[at + width : at + 2 * width]
            image += lead[k : k + 1] * pulled
        out[:, :slots] = image
        out[:, slots:] = norm[...] + gram(direction_ref[...], image, 0)


def solved(small):
    width = small.shape[0]
    shape = small.shape
    c = [jnp.broadcast_to(small[:, j : j + 1], shape) for j in range(width)]
    r = [
        jnp.broadcast_to(small[:, j : j + 1], shape) for j in range(width, 2 * width)
    ]
    for k in range(width):
        inverse = pl.reciprocal(c[k], approx=True)[k : k + 1]
        ck, rk = c[k], r[k]
        for j in range(width):
            if j != k:
                factor = c[j][k : k + 1] * inverse
                c[j] = c[j] - ck * factor
                r[j] = r[j] - rk * factor
        c[k], r[k] = ck * inverse, rk * inverse
    return r


def combined(columns, x):
    parts = []
    for t in range(0, x.shape[1], LANES):
        tile = x[:, t : t + LANES]
        parts.append(sum(col * tile[m : m + 1] for m, col in enumerate(columns)))
    return jnp.concatenate(parts, axis=1)


def tail_kernel(small, mine, other, direction_ref, sol, res):
    columns = solved(small[...])
    direction = direction_ref[...]
    slots = direction.shape[1]
    image = mine[:, :slots] + other[:, :slots]
    sol[...] = combined(columns, direction)
    res[...] = direction - combined(columns, image)


def call(kernel, out_shape, in_specs, out_specs, scratch, name, flops=0):
    return pl.pallas_call(
        kernel,
        out_shape=out_shape,
        in_specs=in_specs,
        out_specs=out_specs,
        scratch_shapes=scratch,
        compiler_params=pltpu.CompilerParams(vmem_limit_bytes=LIMIT),
        cost_estimate=pl.CostEstimate(
            flops=flops, bytes_accessed=1 << 17, transcendentals=0
        ),
        name=name,
    )


def exchanged(block, distance):
    blocks, sides = lax.axis_size("blk"), lax.axis_size("offs")
    route = [
        ((b ^ distance) * sides + sides - 1 - c, b * sides + c)
        for b in range(blocks)
        for c in range(sides)
    ]
    return lax.ppermute(block, ("blk", "offs"), route)


def body(position, noise_var, rhs, block_count):
    width, slots = rhs.shape
    blocks = lax.axis_size("blk")
    tiles = slots // LANES // 2
    half = tiles * LANES
    shape = jax.ShapeDtypeStruct
    pos_buf = pltpu.VMEM(position.shape, f32)
    rhs_buf = pltpu.VMEM(rhs.shape, f32)
    noise_buf = pltpu.VMEM(noise_var.shape, f32)
    count_buf = pltpu.SMEM((1,), jnp.int32)

    first = call(
        first_kernel, shape((1, LANES), jnp.int32), [], VMEM, [], "first", 1 << 30
    )()
    block_count, first = lax.optimization_barrier((block_count, first))
    counted = call(
        count_kernel,
        shape((1, LANES), jnp.int32),
        [pl.BlockSpec(memory_space=pltpu.SMEM), VMEM],
        VMEM,
        [],
        "count",
        0,
    )(block_count, first)
    packet = call(
        pack_kernel,
        shape((width, half + half // 2), f32),
        [VMEM] * 3,
        VMEM,
        [],
        "pack",
    )(position, rhs, counted)

    acc_shape = shape((6 * width, slots), f32)
    rows_shape = shape((32, slots), bf16)

    def pairs(parts, taken, rows=None, acc=None, ready=(), keep=False):
        first, last = rows is None, bool(ready)
        args, specs = list(parts), [VMEM] * len(parts)
        if first:
            args += [position, noise_var, rhs, block_count]
            specs += [HBM] * 4
        else:
            args += [rows, acc, *ready]
            specs += [VMEM] * (2 + len(ready))
        count = sum(stop - start for start, stop in taken)
        scratch = [
            pltpu.VMEM((32, count * half), bf16),
            pltpu.VMEM((6 * width, count * half), bf16),
        ]
        if last:
            outs = (shape((width, slots + LANES), f32),)
            scratch = [pltpu.VMEM(acc_shape.shape, f32)] + scratch
        else:
            outs = (shape(parts[0].shape, f32),) if keep else ()
            outs += (acc_shape,)
        if first:
            outs += (rows_shape, shape((width, LANES), f32))
            outs += (shape(position.shape, f32),) + (shape(rhs.shape, f32),) * 2
            scratch += [pltpu.SemaphoreType.DMA((4,))]
            scratch += [pos_buf, noise_buf, rhs_buf, count_buf]
        kernel = functools.partial(pair_kernel, first, last, keep, taken, tiles)
        flops = 2 * slots * count * half * 64
        name = f"pairs_{count}"
        return call(kernel, outs, specs, (VMEM,) * len(outs), scratch, name, flops)(*args)

    distances = [blocks >> k for k in range(1, blocks.bit_length())]
    known, size = packet, 1
    rows = None
    for distance in distances[:-2]:
        arrived = exchanged(known, distance)
        fresh = (size // 2, size)
        if rows is None:
            known, acc, rows, *ready = pairs([known], [fresh], keep=True)
        else:
            known, acc = pairs([known], [fresh], rows, acc, keep=True)
        known = jnp.concatenate([known, arrived], axis=1)
        size *= 2
    near = exchanged(known, distances[-2])
    far = exchanged(known, distances[-1])
    (acc,) = pairs([known], [(size // 2, size)], rows, acc)
    near, acc = lax.optimization_barrier((near, acc))
    rest = exchanged(near, distances[-1])
    (acc,) = pairs([near, far], [(0, size)] * 2, rows, acc)
    (mine,) = pairs([rest], [(0, size)], rows, acc, ready)
    direction = ready[2]
    other = exchanged(mine, 0)
    small = mine[:, slots:] + other[:, slots:]
    for distance in reversed(distances):
        small = small + exchanged(small, distance)

    return tuple(
        call(
            tail_kernel,
            (shape(rhs.shape, f32),) * 2,
            [VMEM] * 4,
            (VMEM, VMEM),
            [],
            "tail",
        )(small, mine, other, direction)
    )


def solution(mesh):
    return jax.shard_map(
        body,
        mesh=mesh,
        in_specs=(
            P(None, ("mocks", "blk")),
            P(("mocks", "blk")),
            P(None, ("mocks", "blk")),
            P(("mocks", "blk")),
        ),
        out_specs=(P(None, ("mocks", "blk")), P(None, ("mocks", "blk"))),
        check_vma=False,
    )
```
